32 devices in a mesh: dp: 16 (over z, x, core), tensor: 2 (over y).
Axes of the slice: x: 2, y: 2, z: 4, core: 2. Of those that a mesh axis runs over, the one named last changes fastest.
Arguments:
- latent_tokens: float32 [16384, 1152], P(('dp', 'tensor')), may hold values from -6 to 6
- conditioning: float32 [16, 1152], P('dp'), may hold values from -6 to 6
- out_grad: float32 [16384, 1152], P(('dp', 'tensor')), may hold values from -6 to 6
- qkv_weight: float32 [1152, 3, 1152], P('dp', None, 'tensor'), may hold values from -0.1875 to 0.1875
- qkv_bias: float32 [2, 1152], P(None, 'tensor'), may hold values from -1.25 to 1.25
- proj_weight: float32 [1152, 1152], P('tensor', 'dp'), may hold values from -0.75 to 0.75
- proj_bias: float32 [1152], replicated, may hold values from -1.75 to 1.75
- first_layer_weight: float32 [1152, 4608], P('dp', 'tensor'), may hold values from -0.1875 to 0.1875
- fc1_bias: float32 [4608], P('tensor'), may hold values from -3 to 3
- fc2_weight: float32 [4608, 1152], P('tensor', 'dp'), may hold values from -0.09375 to 0.09375
- second_layer_bias: float32 [1152], replicated, may hold values from -1.75 to 1.75
- ada_weight: float32 [1152, 6, 1152], P('dp', None, 'tensor'), may hold values from -0.1875 to 0.1875
- ada_bias: float32 [6, 1152], P(None, 'tensor'), may hold values from -3 to 3
Outputs:
- layer_out: float32 [16384, 1152], P(('dp', 'tensor'))
- tokens_grad: float32 [16384, 1152], P(('dp', 'tensor'))
- conditioning_grad: float32 [16, 1152], P('dp')
- qkv_weight_grad: float32 [1152, 3, 1152], P('dp', None, 'tensor')
- qkv_bias_grad: float32 [2, 1152], P(None, 'tensor')
- proj_weight_grad: float32 [1152, 1152], P('tensor', 'dp')
- proj_bias_grad: float32 [1152], replicated
- fc1_weight_grad: float32 [1152, 4608], P('dp', 'tensor')
- first_layer_bias_gradient: float32 [4608], P('tensor')
- fc2_weight_grad: float32 [4608, 1152], P('tensor', 'dp')
- fc2_bias_grad: float32 [1152], replicated
- ada_weight_grad: float32 [1152, 6, 1152], P('dp', None, 'tensor')
- ada_bias_grad: float32 [6, 1152], P(None, 'tensor')
The draws below stay inside these ranges and needn't reach their ends.
All inputs are finite; a program needn't handle non-finite values.
Results may differ from the reference program's by a relative error of at most 0.012.
The reference program's roundings to bfloat16 on the way count: a program that leaves them out, or rounds other values in their place, can miss the bound.
Values may be sent and summed in bfloat16 or wider, within the bound.
A program may use at most 256 MiB of HBM per device.

```python
import jax
import jax.numpy as jnp
from jax import lax

D = 1152
HEADS = 16
HEAD_DIM = 72
FF = 4608
SEQ = 1024
LATENTS = 16
TOKENS = 16384


def strengthened(values, stream_key, source, target, blocks, factor):
    owner, partner = [(jnp.arange(values.shape[position]) // (values.shape[position] // blocks)).reshape([-1 if axis == position else 1 for axis in range(values.ndim)]) for position in (source, target)]
    chosen = jax.random.permutation(stream_key, blocks)[partner]
    strong = (owner == chosen) | (owner == (partner + blocks // 2) % blocks)
    return jnp.where(strong, factor * values, values)


def level_of(own_key, dims, pieces, least, top_value):
    loudness = 1.0
    for axis_at, shards_of in pieces:
        steps = jax.random.uniform(jax.random.fold_in(jax.random.fold_in(own_key, 6), axis_at), (shards_of,), jnp.float32, least / len(pieces), top_value / len(pieces))
        loudness = loudness * jnp.repeat(jnp.exp(steps), dims[axis_at] // shards_of).reshape((-1,) + (1,) * (len(dims) - 1 - axis_at))
    return loudness


def scatter_about(key, extent, spread, reach, cuts=(), dtype=jnp.bfloat16):
    array = jax.random.normal(key, extent, jnp.float32) * spread
    if len(cuts) > 0:
        array = level_of(key, extent, cuts, -0.22, 0.18) * array
    return jnp.clip(array, min=-reach, max=reach).astype(dtype)


def bell_draw_with(key, shape, deviation, limit, shards, heavy, dtype=jnp.bfloat16):
    values = deviation * jax.random.normal(key, shape, jnp.float32)
    if shards:
        values = values * level_of(key, shape, shards, -0.22, 0.18)
    return jnp.clip(strengthened(values, jax.random.fold_in(key, 3), *heavy), -limit, limit).astype(dtype)


def setup_inputs(seed: int = 0) -> dict:
    key_list = jax.random.split(jax.random.key(seed), 14)
    return {
        "latent_tokens": bell_draw_with(key_list[0], (TOKENS, D), 1.0, 6.0, ((0, 32),), (0, 1, 32, 2.75), jnp.float32),
        "conditioning": scatter_about(key_list[1], (LATENTS, D), 1.0, 6.0, ((0, 16),), jnp.float32),
        "out_grad": bell_draw_with(key_list[2], (TOKENS, D), 1.0, 6.0, ((0, 32),), (0, 1, 32, 2.75), jnp.float32),
        "qkv_weight": scatter_about(key_list[3], (D, 3, D), D ** -0.5, 0.1875, ((0, 16), (2, 2)), jnp.float32),
        "qkv_bias": scatter_about(key_list[4], (2, D), 0.2, 1.25, ((1, 2),), jnp.float32),
        "proj_weight": scatter_about(key_list[5], (D, D), (D // 16) ** -0.5, 0.75, ((0, 2), (1, 16)), jnp.float32),
        "proj_bias": scatter_about(key_list[6], (D,), 0.3, 1.75, (), jnp.float32),
        "first_layer_weight": scatter_about(key_list[7], (D, FF), D ** -0.5, 0.1875, ((0, 16), (1, 2)), jnp.float32),
        "fc1_bias": scatter_about(key_list[8], (FF,), 0.5, 3.0, ((0, 2),), jnp.float32),
        "fc2_weight": scatter_about(key_list[9], (FF, D), FF ** -0.5, 0.09375, ((0, 2), (1, 16)), jnp.float32),
        "second_layer_bias": scatter_about(key_list[10], (D,), 0.3, 1.75, (), jnp.float32),
        "ada_weight": scatter_about(key_list[11], (D, 6, D), D ** -0.5, 0.1875, ((0, 16), (2, 2)), jnp.float32),
        "ada_bias": scatter_about(key_list[12], (6, D), 0.5, 3.0, ((1, 2),), jnp.float32),
    }


@jax.custom_vjp
def low(v):
    return lax.optimization_barrier(v.astype(jnp.bfloat16)).astype(jnp.float32)

@jax.custom_vjp
def low_back(v):
    return v

def low_keep(v):
    return (low(v), None)

def low_pass(kept, grad):
    return (grad,)

def back_keep(v):
    return (v, None)

def back_low(kept, grad):
    return (low(grad),)
low.defvjp(low_keep, low_pass)
low_back.defvjp(back_keep, back_low)
highest_precision_mode = lax.Precision.HIGHEST
epsilon = 1e-06

def matmul(left, right):
    return jnp.dot(left, right, precision=highest_precision_mode, preferred_element_type=jnp.float32)

def gelu_tanh(values):
    return jax.nn.gelu(values, approximate=True)

def normalize(values):
    center = values - lax.optimization_barrier(jnp.mean(values, axis=-1, keepdims=True))
    return center * lax.rsqrt(lax.optimization_barrier(jnp.mean(center * center, axis=-1, keepdims=True)) + epsilon)

def latent_layer(tokens, modulation_values, w_query, w_key, w_value, b_query, b_value, w_proj, b_proj, w_first, b_first, w_second, b_second):
    attn_input = low(normalize(tokens) * (1.0 + modulation_values[1]) + modulation_values[0])
    query = low(low_back(matmul(attn_input, w_query) + b_query)).reshape(SEQ, HEADS, HEAD_DIM)
    keys = low(low_back(matmul(attn_input, w_key))).reshape(SEQ, HEADS, HEAD_DIM)
    values = low(low_back(matmul(attn_input, w_value) + b_value)).reshape(SEQ, HEADS, HEAD_DIM)
    scores = low_back(jnp.einsum('qhd,khd->hqk', query, keys, precision=highest_precision_mode) * HEAD_DIM ** (-0.5))
    probs = low(jax.nn.softmax(scores, axis=-1))
    attended = jnp.einsum('hqk,khd->qhd', probs, values, precision=highest_precision_mode).reshape(SEQ, D)
    attn = low(low_back(attended))
    branch_one = low_back(matmul(attn, w_proj) + b_proj)
    middle = tokens + modulation_values[2] * branch_one
    mlp_input = low(normalize(middle) * (1.0 + modulation_values[4]) + modulation_values[3])
    pre = low_back(matmul(mlp_input, w_first) + b_first)
    act = low(gelu_tanh(pre))
    branch_two = low_back(matmul(act, w_second) + b_second)
    return middle + modulation_values[5] * branch_two

def forward_apply(latent_tokens, conditioning, qkv_weight, qkv_bias, proj_weight, proj_bias, first_layer_weight, fc1_bias, fc2_weight, second_layer_bias, ada_weight, ada_bias):
    cond_low = low(jax.nn.silu(conditioning))
    modulation_values = jnp.einsum('ld,dkf->lkf', cond_low, low(ada_weight), precision=highest_precision_mode) + ada_bias
    qkv_low = low(qkv_weight)
    params = (qkv_low[:, 0], qkv_low[:, 1], qkv_low[:, 2], qkv_bias[0], qkv_bias[1], low(proj_weight), proj_bias, low(first_layer_weight), fc1_bias, low(fc2_weight), second_layer_bias)
    stepper = jax.checkpoint(latent_layer)

    def scan_step(carry, item):
        return (carry, stepper(item[0], item[1], *params))
    blocks = latent_tokens.reshape(LATENTS, SEQ, D)
    _, outputs = lax.scan(scan_step, jnp.zeros((), jnp.float32), (blocks, modulation_values))
    return outputs.reshape(TOKENS, D)

def reference(latent_tokens, conditioning, out_grad, qkv_weight, qkv_bias, proj_weight, proj_bias, first_layer_weight, fc1_bias, fc2_weight, second_layer_bias, ada_weight, ada_bias):
    layer_out, pullback = jax.vjp(forward_apply, latent_tokens, conditioning, qkv_weight, qkv_bias, proj_weight, proj_bias, first_layer_weight, fc1_bias, fc2_weight, second_layer_bias, ada_weight, ada_bias)
    grads = pullback(out_grad)
    return (layer_out, grads[0], grads[1], grads[2], grads[3], grads[4], grads[5], grads[6], grads[7], grads[8], grads[9], grads[10], grads[11])
```

```python
import functools

import jax
import jax.numpy as jnp
from jax import lax
from jax.experimental import pallas as pl
from jax.experimental.pallas import tpu as pltpu
from jax.sharding import PartitionSpec as P

HEAD_DIM = 72
SEQ = 1024


highest_precision_mode = lax.Precision.HIGHEST
epsilon = 1e-06


def gelu_tanh(values):
    return jax.nn.gelu(values, approximate=True)


def normalize(values):
    center = values - jnp.mean(values, axis=-1, keepdims=True)
    scaled = lax.rsqrt(jnp.mean(center * center, axis=-1, keepdims=True) + epsilon)
    return (center * scaled, scaled)


def norm_back(grad, normed, scaled):
    first = jnp.mean(grad, axis=-1, keepdims=True)
    second = jnp.mean(grad * normed, axis=-1, keepdims=True)
    return (grad - first - normed * second) * scaled


def general_body(
    latent_tokens,
    conditioning,
    out_grad,
    qkv_weight,
    qkv_bias,
    proj_weight,
    proj_bias,
    first_layer_weight,
    fc1_bias,
    fc2_weight,
    second_layer_bias,
    ada_weight,
    ada_bias,
):

    def fetch():
        return (
            lax.all_gather(qkv_weight.astype(jnp.bfloat16), "dp", axis=0, tiled=True),
            lax.all_gather(proj_weight.astype(jnp.bfloat16), "dp", axis=1, tiled=True),
            lax.all_gather(first_layer_weight.astype(jnp.bfloat16), "dp", axis=0, tiled=True),
            lax.all_gather(fc2_weight.astype(jnp.bfloat16), "dp", axis=1, tiled=True),
            lax.all_gather(ada_weight.astype(jnp.bfloat16), "dp", axis=0, tiled=True),
        )

    w_qkv, w_proj, w_fc1, w_fc2, w_ada = fetch()
    tok_rows, width_full = latent_tokens.shape
    latents = conditioning.shape[0]
    group_rows = tok_rows * lax.axis_size("tensor")
    width = w_qkv.shape[2]
    heads_local = width // HEAD_DIM
    factor = HEAD_DIM ** (-0.5)
    silu_cond, silu_pull = jax.vjp(jax.nn.silu, conditioning)
    cond_low = silu_cond.astype(jnp.bfloat16)
    mod_part = (
        jnp.einsum("ld,dkf->lkf", cond_low, w_ada, preferred_element_type=jnp.float32) + ada_bias
    )
    modulation_values = lax.all_gather(mod_part, "tensor", axis=2, tiled=True)
    span = min(tok_rows, SEQ)
    block_count = tok_rows // span
    first_row = lax.axis_index("tensor") * tok_rows
    block_latent = (first_row + jnp.arange(block_count, dtype=jnp.int32) * span) // SEQ
    select_helper = (block_latent[:, None] == jnp.arange(latents, dtype=jnp.int32)[None, :]).astype(
        jnp.float32
    )
    block_modulation_terms = jnp.einsum(
        "pe,egt->pgt", select_helper, modulation_values, precision=highest_precision_mode
    )

    def spread(values):
        return jnp.broadcast_to(values[:, None, :], (block_count, span, width_full)).reshape(
            tok_rows, width_full
        )

    def per_latent(values):
        sums = jnp.sum(values.reshape(block_count, span, width_full), axis=1)
        return jnp.einsum("bl,bd->ld", select_helper, sums, precision=highest_precision_mode)

    shift_one = spread(block_modulation_terms[:, 0])
    scale_one = spread(block_modulation_terms[:, 1])
    gate_one = spread(block_modulation_terms[:, 2])
    shift_two = spread(block_modulation_terms[:, 3])
    scale_two = spread(block_modulation_terms[:, 4])
    gate_two = spread(block_modulation_terms[:, 5])
    normed_one, rscale_one = normalize(latent_tokens)
    attn_input = (normed_one * (1.0 + scale_one) + shift_one).astype(jnp.bfloat16)
    qkv_shift = jnp.stack([qkv_bias[0], jnp.zeros_like(qkv_bias[0]), qkv_bias[1]])
    piece = lax.all_gather(attn_input, "tensor", axis=0, tiled=True)
    rows_buf = piece
    made = jnp.einsum("rd,dkf->rkf", piece, w_qkv, preferred_element_type=jnp.float32) + qkv_shift
    made_buf = made.astype(jnp.bfloat16)
    attn_rows = rows_buf
    qkv_all = made_buf
    qkv_latent = qkv_all.reshape(group_rows // SEQ, SEQ, 3, heads_local, HEAD_DIM)

    def attend(block):
        query, keys, values = (block[:, 0], block[:, 1], block[:, 2])
        scores = (
            jnp.einsum("qhd,khd->hqk", query, keys, preferred_element_type=jnp.float32) * factor
        )
        peak = jnp.max(scores, axis=-1, keepdims=True)
        expo = jnp.exp(scores - peak)
        total = jnp.sum(expo, axis=-1, keepdims=True)
        probs = (expo / total).astype(jnp.bfloat16)
        result = jnp.einsum("hqk,khd->qhd", probs, values, preferred_element_type=jnp.float32)
        return (result.astype(jnp.bfloat16), peak[..., 0] + jnp.log(total[..., 0]))

    attn_low, logsum = lax.map(attend, qkv_latent)
    attn_low = attn_low.reshape(group_rows, width)
    rows = attn_low
    branch_one = (
        lax.psum_scatter(
            jnp.dot(rows, w_proj, preferred_element_type=jnp.float32),
            "tensor",
            scatter_dimension=0,
            tiled=True,
        )
        + proj_bias
    )
    middle = latent_tokens + gate_one * branch_one
    normed_two, rscale_two = normalize(middle)
    mlp_input = (normed_two * (1.0 + scale_two) + shift_two).astype(jnp.bfloat16)
    piece = lax.all_gather(mlp_input, "tensor", axis=0, tiled=True)
    rows_buf = piece
    made = jnp.dot(piece, w_fc1, preferred_element_type=jnp.float32) + fc1_bias
    made_buf = made
    act, gelu_pull = jax.vjp(gelu_tanh, made_buf)
    act_low = act.astype(jnp.bfloat16)
    rows = act_low
    branch_two = (
        lax.psum_scatter(
            jnp.dot(rows, w_fc2, preferred_element_type=jnp.float32).astype(jnp.bfloat16),
            "tensor",
            scatter_dimension=0,
            tiled=True,
        ).astype(jnp.float32)
        + second_layer_bias
    )
    layer_out = middle + gate_two * branch_two
    w_qkv, w_proj, w_fc1, w_fc2, w_ada = fetch()
    d_gate_two = per_latent(out_grad * branch_two)
    grad_m = (gate_two * out_grad).astype(jnp.bfloat16)
    fc2_bias_part = jnp.sum(grad_m.astype(jnp.float32), axis=0)
    piece = lax.all_gather(grad_m, "tensor", axis=0, tiled=True)
    made = jnp.einsum("rd,fd->rf", piece, w_fc2, preferred_element_type=jnp.float32)
    act_buf = made
    weight_acc = jnp.einsum("rf,rd->fd", act_low, piece, preferred_element_type=jnp.float32)
    grad_fc2 = weight_acc
    grad_pre = gelu_pull(act_buf)[0].astype(jnp.bfloat16)
    fc1_bias_part = jnp.sum(grad_pre.astype(jnp.float32), axis=0)
    grad_fc1 = jnp.einsum("rd,rf->df", rows_buf, grad_pre, preferred_element_type=jnp.float32)
    rows = grad_pre
    grad_h_two = lax.psum_scatter(
        jnp.einsum("rf,df->rd", rows, w_fc1, preferred_element_type=jnp.float32),
        "tensor",
        scatter_dimension=0,
        tiled=True,
    )
    d_shift_two = per_latent(grad_h_two)
    d_scale_two = per_latent(grad_h_two * normed_two)
    grad_mid = out_grad + norm_back(grad_h_two * (1.0 + scale_two), normed_two, rscale_two)
    d_gate_one = per_latent(grad_mid * branch_one)
    grad_z = (gate_one * grad_mid).astype(jnp.bfloat16)
    proj_bias_part = jnp.sum(grad_z.astype(jnp.float32), axis=0)
    piece = lax.all_gather(grad_z, "tensor", axis=0, tiled=True)
    made = jnp.einsum("rd,fd->rf", piece, w_proj, preferred_element_type=jnp.float32)
    weight_acc = jnp.einsum("rf,rd->fd", attn_low, piece, preferred_element_type=jnp.float32)
    grad_attn_low = made.astype(jnp.bfloat16).reshape(group_rows // SEQ, SEQ, heads_local, HEAD_DIM)

    def attend_back(block):
        packed, grad_o, lse = block
        query, keys, values = (packed[:, 0], packed[:, 1], packed[:, 2])
        scores = (
            jnp.einsum("qhd,khd->hqk", query, keys, preferred_element_type=jnp.float32) * factor
        )
        probs = jnp.exp(scores - lse[..., None])
        probs_low = probs.astype(jnp.bfloat16)
        grad_p = jnp.einsum("qhd,khd->hqk", grad_o, values, preferred_element_type=jnp.float32)
        grad_v = jnp.einsum("hqk,qhd->khd", probs_low, grad_o, preferred_element_type=jnp.float32)
        delta = jnp.sum(grad_p * probs, axis=-1, keepdims=True)
        grad_s = (probs * (grad_p - delta)).astype(jnp.bfloat16)
        grad_q = (
            jnp.einsum("hqk,khd->qhd", grad_s, keys, preferred_element_type=jnp.float32) * factor
        )
        grad_k = (
            jnp.einsum("hqk,qhd->khd", grad_s, query, preferred_element_type=jnp.float32) * factor
        )
        return jnp.stack([grad_q, grad_k, grad_v], axis=1).astype(jnp.bfloat16)

    grad_qkv = lax.map(attend_back, (qkv_latent, grad_attn_low, logsum)).reshape(
        group_rows, 3, width
    )
    qkv_bias_part = jnp.sum(grad_qkv.astype(jnp.float32), axis=0)
    grad_qkv_weight = jnp.einsum(
        "rd,rkf->dkf", attn_rows, grad_qkv, preferred_element_type=jnp.float32
    )
    rows = grad_qkv
    grad_h_one = lax.psum_scatter(
        jnp.einsum("rkf,dkf->rd", rows, w_qkv, preferred_element_type=jnp.float32),
        "tensor",
        scatter_dimension=0,
        tiled=True,
    )
    d_shift_one = per_latent(grad_h_one)
    d_scale_one = per_latent(grad_h_one * normed_one)
    tokens_grad = grad_mid + norm_back(grad_h_one * (1.0 + scale_one), normed_one, rscale_one)
    grad_mods = jnp.stack(
        [d_shift_one, d_scale_one, d_gate_one, d_shift_two, d_scale_two, d_gate_two], axis=1
    )
    mods_share = lax.psum_scatter(grad_mods, "tensor", scatter_dimension=2, tiled=True)
    grad_ada = jnp.einsum(
        "ld,lkf->dkf", cond_low.astype(jnp.float32), mods_share, precision=highest_precision_mode
    )
    grad_ada_bias = jnp.sum(mods_share, axis=0)
    cond_part = jnp.einsum(
        "lkf,dkf->ld", mods_share, w_ada.astype(jnp.float32), precision=highest_precision_mode
    )
    tensor_totals = lax.psum((cond_part, proj_bias_part, fc2_bias_part), "tensor")
    conditioning_grad = silu_pull(tensor_totals[0])[0]
    weight_totals = (
        lax.psum_scatter(grad_qkv_weight, "dp", scatter_dimension=0, tiled=True),
        lax.psum_scatter(weight_acc, "dp", scatter_dimension=1, tiled=True),
        lax.psum_scatter(grad_fc1, "dp", scatter_dimension=0, tiled=True),
        lax.psum_scatter(grad_fc2, "dp", scatter_dimension=1, tiled=True),
        lax.psum_scatter(grad_ada, "dp", scatter_dimension=0, tiled=True),
    )
    qkv_bias_pair = jnp.stack([qkv_bias_part[0], qkv_bias_part[2]])
    bias_totals = lax.psum(
        (qkv_bias_pair, tensor_totals[1], fc1_bias_part, tensor_totals[2], grad_ada_bias), "dp"
    )
    return (
        layer_out,
        tokens_grad,
        conditioning_grad,
        weight_totals[0],
        bias_totals[0],
        weight_totals[1],
        bias_totals[1],
        weight_totals[2],
        bias_totals[2],
        weight_totals[3],
        bias_totals[3],
        weight_totals[4],
        bias_totals[4],
    )


LANES = 128
LOG2E = 1.4426950408889634
f32 = jnp.float32
bf16 = jnp.bfloat16


def fits(mesh):
    return mesh.shape["tensor"] == 2 and mesh.shape["dp"] == 16


def low(values):
    return lax.reduce_precision(values, 8, 7).astype(bf16)


def nn(a, b):
    return lax.dot_general(a, b, (((1,), (0,)), ((), ())), preferred_element_type=f32)


def nt(a, b):
    return lax.dot_general(a, b, (((1,), (1,)), ((), ())), preferred_element_type=f32)


def tn(a, b):
    return lax.dot_general(a, b, (((0,), (0,)), ((), ())), preferred_element_type=f32)


def window(head):
    start = pl.multiple_of(((head * HEAD_DIM) // LANES) * LANES, LANES)
    return start, head * HEAD_DIM - start


def lane_mask(shape, first):
    lane = lax.broadcasted_iota(jnp.int32, shape, 1)
    return (lane >= first) & (lane < first + HEAD_DIM)


def attend_kernel(q_ref, own_ref, oth_ref, o_ref, lse_ref, *, heads, block, pad, scale):
    rows = q_ref.shape[0]
    factor = scale * LOG2E
    o_ref[...] = jnp.zeros_like(o_ref)

    def one_head(h, carry):
        at, first = window(h)

        def one_block(i, inner):
            r = pl.ds(pl.multiple_of(i * block, block), block)
            mask = lane_mask((block, 2 * LANES), first)
            q = q_ref[r, pl.ds(at, 2 * LANES)]
            q = jnp.where(mask, q, jnp.zeros_like(q))
            scores = [nt(ref[:, pl.ds(pad + at, 2 * LANES)], q) for ref in (own_ref, oth_ref)]
            peak = functools.reduce(
                jnp.maximum, [jnp.max(s, axis=0, keepdims=True) for s in scores]
            )
            peak = peak * factor
            expo = [jnp.exp2(s * factor - peak) for s in scores]
            total = sum(jnp.sum(e, axis=0, keepdims=True) for e in expo)
            inverse = 1.0 / total
            out = sum(
                tn(ref[:, pl.ds(2 * pad + at, 2 * LANES)], (e * inverse).astype(bf16))
                for ref, e in zip((own_ref, oth_ref), expo)
            ).T
            o_ref[r, pl.ds(at, 2 * LANES)] = jnp.where(
                mask, out.astype(bf16), o_ref[r, pl.ds(at, 2 * LANES)]
            )
            lse_ref[pl.ds(h, 1), r] = peak + jnp.log2(total)
            return inner

        return lax.fori_loop(0, rows // block, one_block, carry)

    lax.fori_loop(0, heads, one_head, 0)


def attend(queries, own, oth, heads, pad):
    rows = queries.shape[0]
    flops = 4 * heads * rows * 2 * rows * 2 * LANES
    return pl.pallas_call(
        functools.partial(
            attend_kernel, heads=heads, block=min(rows, 512), pad=pad, scale=HEAD_DIM**-0.5
        ),
        out_shape=(
            jax.ShapeDtypeStruct((rows, pad), bf16),
            jax.ShapeDtypeStruct((heads, rows), f32),
        ),
        cost_estimate=pl.CostEstimate(
            flops=4 * flops, bytes_accessed=8 * rows * pad * 2, transcendentals=heads * rows * rows * 2
        ),
        compiler_params=pltpu.CompilerParams(vmem_limit_bytes=40 * 2**20),
    )(queries, own, oth)


def attend_back_kernel(
    own_ref, oth_ref, gown_ref, goth_ref, lown_ref, loth_ref, down_ref, doth_ref, dk_ref, dv_ref,
    *, heads, block, pad, scale,
):
    rows = own_ref.shape[0]
    factor = scale * LOG2E
    down_ref[...] = jnp.zeros_like(down_ref)
    doth_ref[...] = jnp.zeros_like(doth_ref)

    def one_head(h, carry):
        at, first = window(h)
        dk_ref[...] = jnp.zeros_like(dk_ref)
        dv_ref[...] = jnp.zeros_like(dv_ref)
        keys = [ref[:, pl.ds(pad + at, 2 * LANES)] for ref in (own_ref, oth_ref)]
        values = [ref[:, pl.ds(2 * pad + at, 2 * LANES)] for ref in (own_ref, oth_ref)]
        parts = ((own_ref, gown_ref, lown_ref, down_ref), (oth_ref, goth_ref, loth_ref, doth_ref))
        for q_ref, g_ref, l_ref, d_ref in parts:

            def one_block(i, inner):
                r = pl.ds(pl.multiple_of(i * block, block), block)
                mask = lane_mask((block, 2 * LANES), first)
                q = q_ref[r, pl.ds(at, 2 * LANES)]
                q = jnp.where(mask, q, jnp.zeros_like(q))
                g = g_ref[r, pl.ds(at, 2 * LANES)]
                g = jnp.where(mask, g, jnp.zeros_like(g))
                lse = l_ref[pl.ds(h, 1), r]
                probs = [jnp.exp2(nt(k, q) * factor - lse) for k in keys]
                grad_p = [nt(v, g) for v in values]
                delta = sum(jnp.sum(p * d, axis=0, keepdims=True) for p, d in zip(probs, grad_p))
                grad_s = [(p * (d - delta)).astype(bf16) for p, d in zip(probs, grad_p)]
                dq = sum(tn(k, s) for k, s in zip(keys, grad_s)).T * scale
                d_ref[r, pl.ds(at, 2 * LANES)] = jnp.where(
                    mask, dq.astype(bf16), d_ref[r, pl.ds(at, 2 * LANES)]
                )
                for j in range(2):
                    dk_ref[j] += nn(grad_s[j], q)
                    dv_ref[j] += nn(probs[j].astype(bf16), g)
                return inner

            lax.fori_loop(0, rows // block, one_block, 0)
        mask = lane_mask((rows, 2 * LANES), first)
        for j, d_ref in enumerate((down_ref, doth_ref)):
            for lane, new in ((pad, dk_ref[j] * scale), (2 * pad, dv_ref[j])):
                d_ref[:, pl.ds(lane + at, 2 * LANES)] = jnp.where(
                    mask, new.astype(bf16), d_ref[:, pl.ds(lane + at, 2 * LANES)]
                )
        return carry

    lax.fori_loop(0, heads, one_head, 0)


def attend_back(own, oth, gown, goth, lown, loth, heads, pad):
    rows = own.shape[0]
    flops = 10 * heads * 4 * rows * rows * 2 * LANES
    return pl.pallas_call(
        functools.partial(
            attend_back_kernel, heads=heads, block=min(rows, 512), pad=pad, scale=HEAD_DIM**-0.5
        ),
        out_shape=(jax.ShapeDtypeStruct((rows, 3 * pad), bf16),) * 2,
        scratch_shapes=[pltpu.VMEM((2, rows, 2 * LANES), f32)] * 2,
        cost_estimate=pl.CostEstimate(
            flops=flops, bytes_accessed=16 * rows * pad * 2, transcendentals=heads * rows * rows * 4
        ),
        compiler_params=pltpu.CompilerParams(vmem_limit_bytes=56 * 2**20),
    )(own, oth, gown, goth, lown, loth)


GELU = 0.7978845608028654


def feed_kernel(m_ref, g_ref, w1_ref, w2_ref, b_ref, act_ref, gp_ref, h_ref, acc_ref, *, steps):
    i = pl.program_id(0)

    @pl.when(i == 0)
    def _():
        acc_ref[...] = jnp.zeros_like(acc_ref)

    pre = nn(m_ref[...], w1_ref[...]) + b_ref[...]
    grad_act = nn(g_ref[...], w2_ref[...])
    square = pre * pre
    gate = 1.0 / (1.0 + jnp.exp((-2.0 * GELU) * pre * (1.0 + 0.044715 * square)))
    act_ref[...] = (pre * gate).astype(bf16)
    slope = gate + pre * gate * (1.0 - gate) * ((2.0 * GELU) * (1.0 + (3.0 * 0.044715) * square))
    grad_pre = (grad_act * slope).astype(bf16)
    gp_ref[...] = grad_pre
    acc_ref[...] += nt(grad_pre, w1_ref[...])

    @pl.when(i == steps - 1)
    def _():
        h_ref[...] = acc_ref[...].astype(h_ref.dtype)


def feed(m, g, weights, bias, out_dtype):
    rows, depth = m.shape
    hidden = weights.shape[1] // 2
    steps = 3 if hidden % (3 * LANES) == 0 else 1
    chunk = hidden // steps
    whole = pl.BlockSpec((rows, depth), lambda i: (0, 0))
    first = pl.BlockSpec((depth, chunk), lambda i: (0, i))
    second = pl.BlockSpec((depth, chunk), lambda i: (0, i + steps))
    tall = pl.BlockSpec((rows, chunk), lambda i: (0, i))
    return pl.pallas_call(
        functools.partial(feed_kernel, steps=steps),
        grid=(steps,),
        in_specs=[whole, whole, first, second, pl.BlockSpec((1, chunk), lambda i: (0, i))],
        out_specs=[tall, tall, whole],
        out_shape=(
            jax.ShapeDtypeStruct((rows, hidden), bf16),
            jax.ShapeDtypeStruct((rows, hidden), bf16),
            jax.ShapeDtypeStruct((rows, depth), out_dtype),
        ),
        scratch_shapes=[pltpu.VMEM((rows, depth), f32)],
        cost_estimate=pl.CostEstimate(
            flops=12 * rows * depth * hidden,
            bytes_accessed=4 * depth * hidden + 8 * rows * depth + 4 * rows * hidden,
            transcendentals=rows * hidden,
        ),
        compiler_params=pltpu.CompilerParams(vmem_limit_bytes=48 * 2**20),
    )(m, g, weights, weights, bias)


def outer_kernel(
    core_ref, lown_ref, loth_ref, rown_ref, roth_ref, keep_ref, send_ref, sum_ref, turned_ref,
    *, lines, block,
):
    core = core_ref[0]
    rows = lown_ref.shape[0]

    @pl.when(pl.program_id(0) == 0)
    def _():
        for j, ref in enumerate((lown_ref, loth_ref)):
            turned = ref[...].astype(f32).T
            for z in range(lines):
                for x in range(2):
                    for c in range(2):
                        b = (z * 2 + x) * 2 + c
                        turned_ref[c, pl.ds((x * lines + z) * block, block), pl.ds(j * rows, rows)] = (
                            turned[b * block : (b + 1) * block].astype(bf16)
                        )

    for out_ref, which in ((send_ref, 1 - core), (keep_ref, core)):
        made = nn(turned_ref[which, :, pl.ds(0, rows)], rown_ref[...])
        made += nn(turned_ref[which, :, pl.ds(rows, rows)], roth_ref[...])
        out_ref[...] = made.reshape(out_ref.shape)
    ones = jnp.ones((8, rows), bf16)
    sum_ref[...] = nn(ones, rown_ref[...]) + nn(ones, roth_ref[...])


def outer(core, left_own, left_oth, right_own, right_oth, block):
    rows, depth = left_own.shape
    wide = right_own.shape[1]
    lines = depth // block // 4
    steps = next(n for n in (3, 2, 1) if wide % (n * LANES) == 0)
    chunk = wide // steps
    whole = pl.BlockSpec((rows, depth), lambda i, c: (0, 0))
    tall = pl.BlockSpec((rows, chunk), lambda i, c: (0, i))
    out = pl.BlockSpec((2, lines, block, chunk), lambda i, c: (0, 0, 0, i))
    return pl.pallas_call(
        functools.partial(outer_kernel, lines=lines, block=block),
        grid_spec=pltpu.PrefetchScalarGridSpec(
            num_scalar_prefetch=1,
            grid=(steps,),
            in_specs=[whole, whole, tall, tall],
            out_specs=[out, out, pl.BlockSpec((8, chunk), lambda i, c: (0, i))],
            scratch_shapes=[pltpu.VMEM((2, depth // 2, 2 * rows), bf16)],
        ),
        out_shape=(jax.ShapeDtypeStruct((2, lines, block, wide), f32),) * 2
        + (jax.ShapeDtypeStruct((8, wide), f32),),
        cost_estimate=pl.CostEstimate(
            flops=8 * rows * depth * wide,
            bytes_accessed=4 * depth * wide + 4 * rows * (depth + wide),
            transcendentals=0,
        ),
        compiler_params=pltpu.CompilerParams(vmem_limit_bytes=48 * 2**20),
    )(core, left_own, left_oth, right_own, right_oth)


def turn_kernel(h_ref, got_ref, mid_ref, grad_ref, branch_ref, scale_ref, gate_ref, out_ref, z_ref, sum_ref):
    h = h_ref[...] + got_ref[...].astype(f32)
    normed, rscale = normalize(mid_ref[...])
    mid_grad = grad_ref[...] + norm_back(h * (1.0 + scale_ref[...]), normed, rscale)
    out_ref[...] = mid_grad
    z = (gate_ref[...] * mid_grad).astype(bf16)
    z_ref[...] = z

    @pl.when(pl.program_id(0) == 0)
    def _():
        sum_ref[...] = jnp.zeros_like(sum_ref)

    for j, values in enumerate((mid_grad * branch_ref[...], h, h * normed, z.astype(f32))):
        sum_ref[pl.ds(j, 1), :] += jnp.sum(values, axis=0, keepdims=True)


def turn(h_own, h_got, middle, out_grad, branch, scale, gate):
    rows, depth = middle.shape
    tile = min(rows, 128)
    part = pl.BlockSpec((tile, depth), lambda i: (i, 0))
    line = pl.BlockSpec((1, depth), lambda i: (0, 0))
    return pl.pallas_call(
        turn_kernel,
        grid=(rows // tile,),
        in_specs=[part] * 5 + [line] * 2,
        out_specs=[part, part, pl.BlockSpec((8, depth), lambda i: (0, 0))],
        out_shape=(
            jax.ShapeDtypeStruct((rows, depth), f32),
            jax.ShapeDtypeStruct((rows, depth), bf16),
            jax.ShapeDtypeStruct((8, depth), f32),
        ),
        cost_estimate=pl.CostEstimate(
            flops=40 * rows * depth, bytes_accessed=24 * rows * depth, transcendentals=rows
        ),
        compiler_params=pltpu.CompilerParams(vmem_limit_bytes=32 * 2**20),
    )(h_own, h_got, middle, out_grad, branch, scale.reshape(1, -1), gate.reshape(1, -1))


def peers(n_dp):
    me, side = lax.axis_index("dp"), lax.axis_index("tensor")
    n_z = n_dp // 4
    z, x, c = me // 4, (me // 2) % 2, me % 2
    across = (me, 1 - side)
    core = (z * 4 + x * 2 + 1 - c, side)
    beside = (z * 4 + (1 - x) * 2 + c, side)
    lines = [(lax.rem(z + s, n_z) * 4 + x * 2 + c, side) for s in range(1, n_z)]
    return (me, z, x, c), across, core, beside, lines


def greet(partners):
    barrier = pltpu.get_barrier_semaphore()
    for partner in partners:
        pl.semaphore_signal(barrier, inc=1, device_id=partner, device_id_type=pl.DeviceIdType.MESH)
    pl.semaphore_wait(barrier, len(partners))


def close_kernel(
    aown_ref, aoth_ref, down_ref, doth_ref, mine_ref, other_ref, cond_ref, scale_ref,
    w_any, x_any, mid_any, zown_any, zoth_any, oown_any, ooth_any, ada_any,
    tokens_ref, grads_ref, gada_ref, total_ref, row_ref,
    w_ref, x_ref, mid_ref, z_ref, o_ref, ada_ref,
    turned_ref, part_ref, got_ref, xgot_ref, zgot_ref, hsend_ref, hgot_ref, hown_ref,
    rows_ref, rgot_ref, all_ref, cpart_ref, cswap_ref, parts_ref,
    load_sem, send_sem, recv_sem,
    *, n_dp, n_mods, n_shared, pad,
):
    (me, z, x, c), across, core, beside, lines = peers(n_dp)
    n_z = n_dp // 4
    side = lax.axis_index("tensor")
    loads = [
        pltpu.make_async_copy(source, target, load_sem.at[k])
        for k, (source, target) in enumerate(
            (
                (w_any, w_ref),
                (zown_any, z_ref.at[0]),
                (zoth_any, z_ref.at[1]),
                (oown_any, o_ref.at[0]),
                (ooth_any, o_ref.at[1]),
                (x_any, x_ref),
                (mid_any, mid_ref),
                (ada_any, ada_ref),
            )
        )
    ]
    for load in loads:
        load.start()
    greet([across, core, beside] + lines)

    rows, depth = aown_ref.shape
    width = mine_ref.shape[1]
    block = got_ref.shape[3]
    n_parts = part_ref.shape[0]
    tile = min(rows, 128)

    def link(source, target, to, k):
        return pltpu.make_async_remote_copy(
            src_ref=source, dst_ref=target, send_sem=send_sem.at[k], recv_sem=recv_sem.at[k],
            device_id=to, device_id_type=pl.DeviceIdType.MESH,
        )

    def core_link(k):
        return link(part_ref.at[k], got_ref.at[k], core, k)

    def x_link(k):
        return link(got_ref.at[k, 1 - x], xgot_ref.at[k], beside, n_parts + k)

    def z_link(k, s):
        to = lax.rem(z + s + 1, n_z)
        at = 2 * n_parts + k * (n_z - 1) + s
        return link(got_ref.at[k, x, to], zgot_ref.at[k, s], lines[s], at)

    first_sum = (n_z + 1) * n_parts
    half = link(hsend_ref, hgot_ref, across, first_sum)

    def turn_over(refs):
        for j, read in enumerate(refs):
            turned = read().astype(f32).T
            for zz in range(n_z):
                for xx in range(2):
                    for cc in range(2):
                        b = (zz * 2 + xx) * 2 + cc
                        at = pl.ds((xx * n_z + zz) * block, block)
                        turned_ref[cc, at, pl.ds(j * rows, rows)] = turned[
                            b * block : (b + 1) * block
                        ].astype(bf16)

    def product(which, right_own, right_oth):
        made = nn(turned_ref[which, :, pl.ds(0, rows)], right_own)
        made += nn(turned_ref[which, :, pl.ds(rows, rows)], right_oth)
        return made.reshape(got_ref.shape[1:])

    def columns(k):
        at = pl.ds(pl.multiple_of(k * pad, LANES), pad)
        return down_ref[:, at], doth_ref[:, at]

    def to_core(k, carry):
        part_ref[k] = product(1 - c, *columns(k))
        core_link(k).start()
        return carry

    def to_beside(k, carry):
        core_link(k).wait_recv()
        got_ref[k] += product(c, *columns(k))
        x_link(k).start()
        return carry

    def to_lines(k, carry):
        x_link(k).wait_recv()
        got_ref[k, x] += xgot_ref[k]
        for s in range(n_z - 1):
            z_link(k, s).start()
        return carry

    turn_over((lambda: aown_ref[...], lambda: aoth_ref[...]))
    lax.fori_loop(0, 3, to_core, 0)
    lax.fori_loop(0, 3, to_beside, 0)

    loads[0].wait()

    def h_other(i, carry):
        r = pl.ds(pl.multiple_of(i * tile, tile), tile)
        hsend_ref[r, :] = nt(doth_ref[r, :], w_ref[...]).astype(bf16)
        return carry

    lax.fori_loop(0, rows // tile, h_other, 0)
    half.start()

    for load in loads[1:5]:
        load.wait()
    turn_over((lambda: z_ref[0], lambda: z_ref[1]))
    part_ref[3] = product(1 - c, o_ref[0], o_ref[1])
    core_link(3).start()

    def h_own(i, carry):
        r = pl.ds(pl.multiple_of(i * tile, tile), tile)
        hown_ref[r, :] = nt(down_ref[r, :], w_ref[...])
        return carry

    lax.fori_loop(0, rows // tile, h_own, 0)
    ones = jnp.ones((8, rows), bf16)
    d_sums = nn(ones, down_ref[...]) + nn(ones, doth_ref[...])
    core_link(3).wait_recv()
    got_ref[3] += product(c, o_ref[0], o_ref[1])
    x_link(3).start()
    to_lines(0, 0)

    for load in loads[5:]:
        load.wait()
    half.wait_recv()

    def last_norm(i, carry):
        r = pl.ds(pl.multiple_of(i * tile, tile), tile)
        h = hown_ref[r, :] + hgot_ref[r, :].astype(f32)
        normed, rscale = normalize(x_ref[r, :])
        tokens_ref[r, :] = mid_ref[r, :] + norm_back(h * (1.0 + scale_ref[...]), normed, rscale)
        shift_sum, scale_sum = carry
        shift_sum += jnp.sum(h, axis=0, keepdims=True)
        scale_sum += jnp.sum(h * normed, axis=0, keepdims=True)
        return shift_sum, scale_sum

    none = jnp.zeros((1, depth), f32)
    late = lax.fori_loop(0, rows // tile, last_norm, (none, none))

    rows_ref[0] = mine_ref[...]
    rows_ref[1] = other_ref[...]
    for j, values in enumerate(late):
        low_half, high_half = values[:, :width], values[:, width:]
        rows_ref[0, pl.ds(j, 1), :] = jnp.where(side == 0, low_half, high_half)
        rows_ref[1, pl.ds(j, 1), :] = jnp.where(side == 0, high_half, low_half)
    for j, at in ((0, 0), (1, 2 * pad)):
        rows_ref[0, pl.ds(n_mods + j, 1), :] = d_sums[:1, at : at + width]
    first_sum += 1
    swap_rows = link(rows_ref.at[1], rgot_ref, across, first_sum)
    swap_rows.start()
    to_lines(1, 0)
    swap_rows.wait()
    row = lax.broadcasted_iota(jnp.int32, mine_ref.shape, 0)
    shared = (row < n_mods) | (row >= mine_ref.shape[0] - n_shared)
    all_ref[z, x, c] = rows_ref[0] + jnp.where(shared, rgot_ref[...], 0.0)

    def spread(ref, first):
        copy = link(ref.at[z, x, c], ref.at[z, x, c], core, first)
        copy.start()
        copy.wait()
        copy = link(ref.at[z, x], ref.at[z, x], beside, first + 1)
        copy.start()
        copy.wait()
        copies = [link(ref.at[z], ref.at[z], to, first + 2 + s) for s, to in enumerate(lines)]
        for copy in copies:
            copy.start()
        for copy in copies:
            copy.wait()

    spread(all_ref, first_sum + 1)
    to_lines(2, 0)
    everything = all_ref[...].reshape((n_dp,) + mine_ref.shape)
    total_ref[...] = jnp.sum(everything, axis=0)
    cond = cond_ref[...]
    part = jnp.zeros(cond.shape, f32)
    for j in range(n_mods):
        grad = everything[:, j, :]
        gada_ref[j] = lax.dot_general(
            cond, grad, (((0,), (0,)), ((), ())),
            precision=highest_precision_mode, preferred_element_type=f32,
        )
        part += lax.dot_general(
            grad, ada_ref[j].astype(f32), (((1,), (1,)), ((), ())),
            precision=highest_precision_mode, preferred_element_type=f32,
        )
    cpart_ref[...] = part
    swap_part = link(cpart_ref, cswap_ref, across, first_sum + n_z + 2)
    swap_part.start()
    swap_part.wait()
    whole = cpart_ref[...] + cswap_ref[...]
    for l in range(n_dp):
        parts_ref[z, x, c, l] = whole[l : l + 1]
    spread(parts_ref, first_sum + n_z + 3)
    for p in range(n_dp):
        row_ref[pl.ds(p, 1), :] = parts_ref[p // 4, (p // 2) % 2, p % 2, me]

    to_lines(3, 0)

    def finish(k, carry):
        total = got_ref[k, x, z]
        for s in range(n_z - 1):
            z_link(k, s).wait_recv()
            total += zgot_ref[k, s]
        grads_ref[k] = total
        return carry

    lax.fori_loop(0, n_parts, finish, 0)
    half.wait_send()

    def sent(k, carry):
        core_link(k).wait_send()
        x_link(k).wait_send()
        for s in range(n_z - 1):
            z_link(k, s).wait_send()
        return carry

    lax.fori_loop(0, n_parts, sent, 0)


def close(
    a_own, a_oth, d_own, d_oth, mine, other, cond, scale, w_qkv, tokens, mid_grad,
    z_own, z_oth, o_own, o_oth, ada, n_shared,
):
    n_dp = lax.axis_size("dp")
    n_z = n_dp // 4
    n_mods, block, width = ada.shape
    rows, depth = tokens.shape
    pad = o_own.shape[1]
    n_rows = mine.shape[0]
    n_parts = 4
    n_links = (n_z + 1) * n_parts + 1 + 2 * (n_z + 2)
    vmem = pl.BlockSpec(memory_space=pltpu.VMEM)
    return pl.pallas_call(
        functools.partial(close_kernel, n_dp=n_dp, n_mods=n_mods, n_shared=n_shared, pad=pad),
        out_shape=(
            jax.ShapeDtypeStruct((rows, depth), f32),
            jax.ShapeDtypeStruct((n_parts, block, pad), f32),
            jax.ShapeDtypeStruct((n_mods, block, width), f32),
            jax.ShapeDtypeStruct((n_rows, width), f32),
            jax.ShapeDtypeStruct((n_dp, block), f32),
        ),
        in_specs=[vmem] * 8 + [pl.BlockSpec(memory_space=pl.ANY)] * 8,
        out_specs=[vmem] * 5,
        scratch_shapes=[
            pltpu.VMEM(w_qkv.shape, bf16),
            pltpu.VMEM((rows, depth), f32),
            pltpu.VMEM((rows, depth), f32),
            pltpu.VMEM((2, rows, depth), bf16),
            pltpu.VMEM((2, rows, pad), bf16),
            pltpu.VMEM(ada.shape, bf16),
            pltpu.VMEM((2, depth // 2, 2 * rows), bf16),
            pltpu.VMEM((n_parts, 2, n_z, block, pad), f32),
            pltpu.VMEM((n_parts, 2, n_z, block, pad), f32),
            pltpu.VMEM((n_parts, n_z, block, pad), f32),
            pltpu.VMEM((n_parts, n_z - 1, block, pad), f32),
            pltpu.VMEM((rows, depth), bf16),
            pltpu.VMEM((rows, depth), bf16),
            pltpu.VMEM((rows, depth), f32),
            pltpu.VMEM((2, n_rows, width), f32),
            pltpu.VMEM((n_rows, width), f32),
            pltpu.VMEM((n_z, 2, 2, n_rows, width), f32),
            pltpu.VMEM((n_dp, block), f32),
            pltpu.VMEM((n_dp, block), f32),
            pltpu.VMEM((n_z, 2, 2, n_dp, 1, block), f32),
            pltpu.SemaphoreType.DMA((8,)),
            pltpu.SemaphoreType.DMA((n_links,)),
            pltpu.SemaphoreType.DMA((n_links,)),
        ],
        cost_estimate=pl.CostEstimate(
            flops=60 * 10**9, bytes_accessed=100 * 10**6, transcendentals=0
        ),
        compiler_params=pltpu.CompilerParams(
            collective_id=0, has_side_effects=True, vmem_limit_bytes=60 * 2**20
        ),
    )(
        a_own, a_oth, d_own, d_oth, mine, other, cond, scale.reshape(1, -1),
        w_qkv, tokens, mid_grad, z_own, z_oth, o_own, o_oth, ada,
    )


def after(value, *others):
    return lax.optimization_barrier((value,) + others)[0]


TOP = 32768.0


def fast_body(
    latent_tokens,
    conditioning,
    out_grad,
    qkv_weight,
    qkv_bias,
    proj_weight,
    proj_bias,
    first_layer_weight,
    fc1_bias,
    fc2_weight,
    second_layer_bias,
    ada_weight,
    ada_bias,
):
    n_dp = lax.axis_size("dp")
    n_z = n_dp // 4
    me = lax.axis_index("dp")
    side = lax.axis_index("tensor")
    core, at_x, at_z = me % 2, (me // 2) % 2, me // 4
    rows, width_full = latent_tokens.shape
    block, _, width = qkv_weight.shape
    heads = width // HEAD_DIM
    pad = -(-width // LANES) * LANES

    def swap(values):
        return lax.ppermute(values, "tensor", [(0, 1), (1, 0)])

    def flip(values, bit):
        return lax.ppermute(values, "dp", [(i, i ^ bit) for i in range(n_dp)])

    def shift(values, step):
        return lax.ppermute(values, "dp", [(i, (i + 4 * step) % n_dp) for i in range(n_dp)])

    def place(pieces, spots):
        out = jnp.zeros((len(pieces),) + pieces[0].shape, pieces[0].dtype)
        for piece, spot in zip(pieces, spots):
            out = lax.dynamic_update_index_in_dim(out, piece, spot, 0)
        return out

    def pair(mine, other, bit):
        return jnp.where(bit == 0, jnp.stack([mine, other]), jnp.stack([other, mine]))

    def along_z(values):
        pieces = [values] + [shift(values, s) for s in range(1, n_z)]
        return place(pieces, [(at_z - s) % n_z for s in range(n_z)])

    def in_order(both, shape):
        both = both.reshape((2, 2, n_z) + shape)
        return jnp.transpose(both, (2, 1, 0) + tuple(range(3, both.ndim))).reshape((n_dp,) + shape)

    def gather(values):
        lines = along_z(values)
        planes = place([lines, flip(lines, 2)], [at_x, 1 - at_x])
        both = place([planes, flip(planes, 1)], [core, 1 - core])
        return in_order(both, values.shape)

    def pick(array, spot, axis):
        return lax.dynamic_index_in_dim(array, spot, axis, keepdims=False)

    def scatter_sum(values):
        parts = values.reshape((n_z, 2, 2) + values.shape[1:])
        parts = pick(parts, core, 2) + flip(pick(parts, 1 - core, 2), 1)
        parts = pick(parts, at_x, 1) + flip(pick(parts, 1 - at_x, 1), 2)
        total = pick(parts, at_z, 0)
        for s in range(1, n_z):
            total = total + shift(pick(parts, (at_z + s) % n_z, 0), s)
        return total

    def narrow(part, bound):
        return (part * (TOP / bound)).astype(jnp.float16)

    def wide(part, bound):
        return part.astype(f32) * (bound * (1.0 / TOP))

    def biggest_over_dp(values):
        values = jnp.maximum(values, flip(values, 1))
        values = jnp.maximum(values, flip(values, 2))
        others = [shift(values, s) for s in range(1, n_z)]
        return functools.reduce(jnp.maximum, others, values)

    def total_over_dp(values):
        values = values + flip(values, 1)
        values = values + flip(values, 2)
        return jnp.sum(along_z(values), axis=0)

    def halves(mine, other, axis):
        first = jnp.where(side == 0, mine, other)
        second = jnp.where(side == 0, other, mine)
        return jnp.concatenate([first, second], axis=axis)

    def pad_lanes(values):
        return jnp.pad(values, [(0, 0)] * (values.ndim - 1) + [(0, pad - width)])

    def biggest(*pieces):
        return functools.reduce(jnp.maximum, [jnp.max(jnp.abs(v.astype(f32))) for v in pieces])

    out_top = biggest(out_grad).reshape(1)
    out_top = jnp.maximum(out_top, swap(out_top))
    normed_one, rscale_one = normalize(latent_tokens)

    def full_weight(shard):
        return lax.all_gather(shard, "dp", axis=0, tiled=True)

    first = [
        pad_lanes(qkv_weight.astype(bf16)).reshape(block, 3 * pad),
        pad_lanes(proj_weight.astype(bf16).T),
    ]
    w_first = full_weight(jnp.concatenate(first, axis=1))
    w_qkv, w_proj = w_first[:, : 3 * pad], w_first[:, 3 * pad :]
    second = [first_layer_weight.astype(bf16), fc2_weight.astype(bf16).T]
    w_second = full_weight(jnp.concatenate(second, axis=1))
    hidden = first_layer_weight.shape[1]
    w_fc2 = w_second[:, hidden:]

    silu_cond, silu_pull = jax.vjp(jax.nn.silu, conditioning)
    cond_all = gather(low(silu_cond)).reshape(n_dp, width_full)
    cond_mine = lax.dynamic_slice_in_dim(cond_all, me * block, block, 1)
    w_ada = ada_weight.astype(bf16).reshape(block, 6 * width)
    mods_half = scatter_sum(nn(cond_mine, w_ada)).reshape(6, width) + ada_bias
    mods = halves(mods_half, swap(mods_half), 1)
    shift_one, scale_one, gate_one, shift_two, scale_two, gate_two = [mods[j] for j in range(6)]

    tokens = float(n_dp * SEQ)
    tiny = 1e-30
    norm = 1.01 * width_full**0.5
    bounds = jnp.concatenate(
        [
            out_top * biggest(gate_two),
            (biggest(scale_two) + biggest(shift_two) + 1.0).reshape(1) * norm,
        ]
    )
    bounds = biggest_over_dp(bounds)
    act_bound = bounds[1] * (0.1875 * norm) + 3.0
    gp_bound = bounds[0] * (1.2 * 0.09375 * width_full)
    fc2_bound = bounds[0] * act_bound * (1.01 * tokens) + tiny
    fc1_bound = bounds[1] * gp_bound * (1.01 * tokens) + tiny
    v_bound = (biggest(scale_one) + biggest(shift_one) + 1.0) * (norm * 0.1875 * norm) + 1.25
    p_bound = v_bound * (1.01 * 0.75 * width)

    a_own = low(normed_one * (1.0 + scale_one) + shift_one)
    a_oth = swap(a_own)
    g_own = low(gate_two * out_grad)
    g_oth = swap(after(g_own, a_own))
    bias = pad_lanes(jnp.stack([qkv_bias[0], jnp.zeros_like(qkv_bias[0]), qkv_bias[1]]))
    bias = bias.reshape(3 * pad)
    qkv_own = (nn(after(a_own, bounds), w_qkv) + bias).astype(bf16)
    qkv_oth = (nn(a_oth, w_qkv) + bias).astype(bf16)
    o_oth, lse_oth = attend(qkv_oth, qkv_own, qkv_oth, heads, pad)
    p_send = narrow(nt(o_oth, w_proj), p_bound)
    part_oth = wide(swap(p_send), p_bound)
    o_own, lse_own = attend(after(qkv_own, p_send), qkv_own, qkv_oth, heads, pad)
    branch_one = nt(o_own, w_proj) + part_oth + proj_bias
    middle = latent_tokens + gate_one * branch_one
    normed_two, rscale_two = normalize(middle)

    m_own = low(normed_two * (1.0 + scale_two) + shift_two)
    m_oth = swap(m_own)
    hidden_bias = fc1_bias.reshape(1, -1)
    act_own, gp_own, h_own = feed(m_own, g_own, w_second, hidden_bias, f32)
    act_oth, gp_oth, h_send = feed(m_oth, after(g_oth, m_own), w_second, hidden_bias, bf16)
    h_recv = swap(h_send)

    this_core = core.astype(jnp.int32).reshape(1)
    kept_fc2, sent_fc2, _ = outer(
        this_core, g_own, g_oth, after(act_own, h_send), act_oth, block
    )
    got_fc2 = flip(sent_fc2, 1)
    kept_fc1, sent_fc1, fc1_sums = outer(
        this_core, m_own, m_oth, after(gp_own, sent_fc2), gp_oth, block
    )
    got_fc1 = flip(sent_fc1, 1)

    def x_halves(kept, got, bound):
        mine = pick(kept, at_x, 0) + pick(got, at_x, 0)
        other = pick(kept, 1 - at_x, 0) + pick(got, 1 - at_x, 0)
        return mine, narrow(other, bound)

    def z_sent(parts, bound):
        return [narrow(pick(parts, (at_z + s) % n_z, 0), bound) for s in range(1, n_z)]

    fc2_mine, fc2_send = x_halves(kept_fc2, after(got_fc2, kept_fc1), fc2_bound)
    fc2_x = flip(fc2_send, 2)
    mid_grad, z_own, turned = turn(
        h_own, after(h_recv, fc2_send), middle, out_grad, branch_one, scale_two, gate_one
    )
    z_oth = swap(z_own)
    fc1_mine, fc1_send = x_halves(kept_fc1, after(got_fc1, z_own), fc1_bound)
    b_send = nt(after(act_oth, fc1_send), w_fc2).astype(bf16)
    b_own = nt(after(act_own, b_send), w_fc2)
    go_own = nn(after(z_own, b_own), w_proj).astype(bf16)
    fc2_parts = fc2_mine + wide(after(fc2_x, go_own), fc2_bound)
    fc2_z = z_sent(fc2_parts, fc2_bound)
    fc1_x = flip(after(fc1_send, fc2_z[0]), 2)
    go_oth = nn(after(z_oth, *fc2_z), w_proj).astype(bf16)
    b_oth = swap(after(b_send, go_oth)).astype(f32)
    d_own, d_oth = attend_back(
        qkv_own, qkv_oth, go_own, go_oth, lse_own, lse_oth, heads, pad
    )
    fc1_parts = fc1_mine + wide(after(fc1_x, d_own), fc1_bound)
    fc1_z = z_sent(fc1_parts, fc1_bound)

    def z_total(parts, sent, bound):
        return pick(parts, at_z, 0) + sum(
            wide(shift(part, s + 1), bound) for s, part in enumerate(sent)
        )

    grad_fc1 = z_total(fc1_parts, fc1_z, fc1_bound)
    grad_fc2 = z_total(fc2_parts, fc2_z, fc2_bound).T
    branch_two = b_own + b_oth + second_layer_bias
    layer_out = middle + gate_two * branch_two

    sums = functools.partial(jnp.sum, axis=0)
    empty = jnp.zeros((2, width_full), f32)
    mods_sums = jnp.stack([turned[0], turned[1], turned[2], sums(out_grad * branch_two)])
    mods_sums = jnp.concatenate([empty, mods_sums]).reshape(6, 2, width)
    apart = jnp.concatenate([jnp.zeros((2, width), f32), fc1_sums[0].reshape(-1, width)])
    shared = jnp.stack([turned[3], sums(g_own.astype(f32))]).reshape(-1, width)
    mine = jnp.concatenate([pick(mods_sums, side, 1), apart, shared])
    other = jnp.concatenate([pick(mods_sums, 1 - side, 1), apart, shared])
    ada = jnp.transpose(w_ada.reshape(block, 6, width), (1, 0, 2))
    tokens_grad, grads, grad_ada, totals, cond_row = close(
        a_own, a_oth, after(d_own, *fc1_z), d_oth, mine, other, cond_mine.astype(f32), scale_one,
        w_qkv, latent_tokens, mid_grad, z_own, z_oth, o_own, o_oth, ada, shared.shape[0],
    )
    grad_qkv = jnp.transpose(grads[:3, :, :width], (1, 0, 2))
    grad_proj = grads[3, :, :width].T
    conditioning_grad = silu_pull(cond_row.reshape(1, width_full))[0]
    fc1_rows = hidden // width
    qkv_bias_grad = totals[6:8]
    fc1_bias_grad = totals[8 : 8 + fc1_rows].reshape(hidden)
    proj_bias_grad, fc2_bias_grad = totals[8 + fc1_rows :].reshape(2, width_full)
    grad_ada_bias = totals[:6]
    grad_ada = jnp.transpose(grad_ada, (1, 0, 2))
    return (
        layer_out,
        tokens_grad,
        conditioning_grad,
        grad_qkv,
        qkv_bias_grad,
        grad_proj,
        proj_bias_grad,
        grad_fc1,
        fc1_bias_grad,
        grad_fc2,
        fc2_bias_grad,
        grad_ada,
        grad_ada_bias,
    )


def solution(mesh):
    in_specs = (
        P(("dp", "tensor"), None),
        P("dp", None),
        P(("dp", "tensor"), None),
        P("dp", None, "tensor"),
        P(None, "tensor"),
        P("tensor", "dp"),
        P(),
        P("dp", "tensor"),
        P("tensor"),
        P("tensor", "dp"),
        P(),
        P("dp", None, "tensor"),
        P(None, "tensor"),
    )
    out_specs = (
        P(("dp", "tensor"), None),
        P(("dp", "tensor"), None),
        P("dp", None),
        P("dp", None, "tensor"),
        P(None, "tensor"),
        P("tensor", "dp"),
        P(),
        P("dp", "tensor"),
        P("tensor"),
        P("tensor", "dp"),
        P(),
        P("dp", None, "tensor"),
        P(None, "tensor"),
    )
    body = fast_body if fits(mesh) else general_body
    return jax.shard_map(body, mesh=mesh, in_specs=in_specs, out_specs=out_specs, check_vma=False)
```

```python
import functools

import jax
import jax.numpy as jnp
from jax import lax
from jax.experimental import pallas as pl
from jax.experimental.pallas import tpu as pltpu
from jax.sharding import PartitionSpec as P

HEAD_DIM = 72
SEQ = 1024


highest_precision_mode = lax.Precision.HIGHEST
epsilon = 1e-06


def gelu_tanh(values):
    return jax.nn.gelu(values, approximate=True)


def normalize(values):
    center = values - jnp.mean(values, axis=-1, keepdims=True)
    scaled = lax.rsqrt(jnp.mean(center * center, axis=-1, keepdims=True) + epsilon)
    return (center * scaled, scaled)


def norm_back(grad, normed, scaled):
    first = jnp.mean(grad, axis=-1, keepdims=True)
    second = jnp.mean(grad * normed, axis=-1, keepdims=True)
    return (grad - first - normed * second) * scaled


def general_body(
    latent_tokens,
    conditioning,
    out_grad,
    qkv_weight,
    qkv_bias,
    proj_weight,
    proj_bias,
    first_layer_weight,
    fc1_bias,
    fc2_weight,
    second_layer_bias,
    ada_weight,
    ada_bias,
):

    def fetch():
        return (
            lax.all_gather(qkv_weight.astype(jnp.bfloat16), "dp", axis=0, tiled=True),
            lax.all_gather(proj_weight.astype(jnp.bfloat16), "dp", axis=1, tiled=True),
            lax.all_gather(first_layer_weight.astype(jnp.bfloat16), "dp", axis=0, tiled=True),
            lax.all_gather(fc2_weight.astype(jnp.bfloat16), "dp", axis=1, tiled=True),
            lax.all_gather(ada_weight.astype(jnp.bfloat16), "dp", axis=0, tiled=True),
        )

    w_qkv, w_proj, w_fc1, w_fc2, w_ada = fetch()
    tok_rows, width_full = latent_tokens.shape
    latents = conditioning.shape[0]
    group_rows = tok_rows * lax.axis_size("tensor")
    width = w_qkv.shape[2]
    heads_local = width // HEAD_DIM
    factor = HEAD_DIM ** (-0.5)
    silu_cond, silu_pull = jax.vjp(jax.nn.silu, conditioning)
    cond_low = silu_cond.astype(jnp.bfloat16)
    mod_part = (
        jnp.einsum("ld,dkf->lkf", cond_low, w_ada, preferred_element_type=jnp.float32) + ada_bias
    )
    modulation_values = lax.all_gather(mod_part, "tensor", axis=2, tiled=True)
    span = min(tok_rows, SEQ)
    block_count = tok_rows // span
    first_row = lax.axis_index("tensor") * tok_rows
    block_latent = (first_row + jnp.arange(block_count, dtype=jnp.int32) * span) // SEQ
    select_helper = (block_latent[:, None] == jnp.arange(latents, dtype=jnp.int32)[None, :]).astype(
        jnp.float32
    )
    block_modulation_terms = jnp.einsum(
        "pe,egt->pgt", select_helper, modulation_values, precision=highest_precision_mode
    )

    def spread(values):
        return jnp.broadcast_to(values[:, None, :], (block_count, span, width_full)).reshape(
            tok_rows, width_full
        )

    def per_latent(values):
        sums = jnp.sum(values.reshape(block_count, span, width_full), axis=1)
        return jnp.einsum("bl,bd->ld", select_helper, sums, precision=highest_precision_mode)

    shift_one = spread(block_modulation_terms[:, 0])
    scale_one = spread(block_modulation_terms[:, 1])
    gate_one = spread(block_modulation_terms[:, 2])
    shift_two = spread(block_modulation_terms[:, 3])
    scale_two = spread(block_modulation_terms[:, 4])
    gate_two = spread(block_modulation_terms[:, 5])
    normed_one, rscale_one = normalize(latent_tokens)
    attn_input = (normed_one * (1.0 + scale_one) + shift_one).astype(jnp.bfloat16)
    qkv_shift = jnp.stack([qkv_bias[0], jnp.zeros_like(qkv_bias[0]), qkv_bias[1]])
    piece = lax.all_gather(attn_input, "tensor", axis=0, tiled=True)
    rows_buf = piece
    made = jnp.einsum("rd,dkf->rkf", piece, w_qkv, preferred_element_type=jnp.float32) + qkv_shift
    made_buf = made.astype(jnp.bfloat16)
    attn_rows = rows_buf
    qkv_all = made_buf
    qkv_latent = qkv_all.reshape(group_rows // SEQ, SEQ, 3, heads_local, HEAD_DIM)

    def attend(block):
        query, keys, values = (block[:, 0], block[:, 1], block[:, 2])
        scores = (
            jnp.einsum("qhd,khd->hqk", query, keys, preferred_element_type=jnp.float32) * factor
        )
        peak = jnp.max(scores, axis=-1, keepdims=True)
        expo = jnp.exp(scores - peak)
        total = jnp.sum(expo, axis=-1, keepdims=True)
        probs = (expo / total).astype(jnp.bfloat16)
        result = jnp.einsum("hqk,khd->qhd", probs, values, preferred_element_type=jnp.float32)
        return (result.astype(jnp.bfloat16), peak[..., 0] + jnp.log(total[..., 0]))

    attn_low, logsum = lax.map(attend, qkv_latent)
    attn_low = attn_low.reshape(group_rows, width)
    rows = attn_low
    branch_one = (
        lax.psum_scatter(
            jnp.dot(rows, w_proj, preferred_element_type=jnp.float32),
            "tensor",
            scatter_dimension=0,
            tiled=True,
        )
        + proj_bias
    )
    middle = latent_tokens + gate_one * branch_one
    normed_two, rscale_two = normalize(middle)
    mlp_input = (normed_two * (1.0 + scale_two) + shift_two).astype(jnp.bfloat16)
    piece = lax.all_gather(mlp_input, "tensor", axis=0, tiled=True)
    rows_buf = piece
    made = jnp.dot(piece, w_fc1, preferred_element_type=jnp.float32) + fc1_bias
    made_buf = made
    act, gelu_pull = jax.vjp(gelu_tanh, made_buf)
    act_low = act.astype(jnp.bfloat16)
    rows = act_low
    branch_two = (
        lax.psum_scatter(
            jnp.dot(rows, w_fc2, preferred_element_type=jnp.float32).astype(jnp.bfloat16),
            "tensor",
            scatter_dimension=0,
            tiled=True,
        ).astype(jnp.float32)
        + second_layer_bias
    )
    layer_out = middle + gate_two * branch_two
    w_qkv, w_proj, w_fc1, w_fc2, w_ada = fetch()
    d_gate_two = per_latent(out_grad * branch_two)
    grad_m = (gate_two * out_grad).astype(jnp.bfloat16)
    fc2_bias_part = jnp.sum(grad_m.astype(jnp.float32), axis=0)
    piece = lax.all_gather(grad_m, "tensor", axis=0, tiled=True)
    made = jnp.einsum("rd,fd->rf", piece, w_fc2, preferred_element_type=jnp.float32)
    act_buf = made
    weight_acc = jnp.einsum("rf,rd->fd", act_low, piece, preferred_element_type=jnp.float32)
    grad_fc2 = weight_acc
    grad_pre = gelu_pull(act_buf)[0].astype(jnp.bfloat16)
    fc1_bias_part = jnp.sum(grad_pre.astype(jnp.float32), axis=0)
    grad_fc1 = jnp.einsum("rd,rf->df", rows_buf, grad_pre, preferred_element_type=jnp.float32)
    rows = grad_pre
    grad_h_two = lax.psum_scatter(
        jnp.einsum("rf,df->rd", rows, w_fc1, preferred_element_type=jnp.float32),
        "tensor",
        scatter_dimension=0,
        tiled=True,
    )
    d_shift_two = per_latent(grad_h_two)
    d_scale_two = per_latent(grad_h_two * normed_two)
    grad_mid = out_grad + norm_back(grad_h_two * (1.0 + scale_two), normed_two, rscale_two)
    d_gate_one = per_latent(grad_mid * branch_one)
    grad_z = (gate_one * grad_mid).astype(jnp.bfloat16)
    proj_bias_part = jnp.sum(grad_z.astype(jnp.float32), axis=0)
    piece = lax.all_gather(grad_z, "tensor", axis=0, tiled=True)
    made = jnp.einsum("rd,fd->rf", piece, w_proj, preferred_element_type=jnp.float32)
    weight_acc = jnp.einsum("rf,rd->fd", attn_low, piece, preferred_element_type=jnp.float32)
    grad_attn_low = made.astype(jnp.bfloat16).reshape(group_rows // SEQ, SEQ, heads_local, HEAD_DIM)

    def attend_back(block):
        packed, grad_o, lse = block
        query, keys, values = (packed[:, 0], packed[:, 1], packed[:, 2])
        scores = (
            jnp.einsum("qhd,khd->hqk", query, keys, preferred_element_type=jnp.float32) * factor
        )
        probs = jnp.exp(scores - lse[..., None])
        probs_low = probs.astype(jnp.bfloat16)
        grad_p = jnp.einsum("qhd,khd->hqk", grad_o, values, preferred_element_type=jnp.float32)
        grad_v = jnp.einsum("hqk,qhd->khd", probs_low, grad_o, preferred_element_type=jnp.float32)
        delta = jnp.sum(grad_p * probs, axis=-1, keepdims=True)
        grad_s = (probs * (grad_p - delta)).astype(jnp.bfloat16)
        grad_q = (
            jnp.einsum("hqk,khd->qhd", grad_s, keys, preferred_element_type=jnp.float32) * factor
        )
        grad_k = (
            jnp.einsum("hqk,qhd->khd", grad_s, query, preferred_element_type=jnp.float32) * factor
        )
        return jnp.stack([grad_q, grad_k, grad_v], axis=1).astype(jnp.bfloat16)

    grad_qkv = lax.map(attend_back, (qkv_latent, grad_attn_low, logsum)).reshape(
        group_rows, 3, width
    )
    qkv_bias_part = jnp.sum(grad_qkv.astype(jnp.float32), axis=0)
    grad_qkv_weight = jnp.einsum(
        "rd,rkf->dkf", attn_rows, grad_qkv, preferred_element_type=jnp.float32
    )
    rows = grad_qkv
    grad_h_one = lax.psum_scatter(
        jnp.einsum("rkf,dkf->rd", rows, w_qkv, preferred_element_type=jnp.float32),
        "tensor",
        scatter_dimension=0,
        tiled=True,
    )
    d_shift_one = per_latent(grad_h_one)
    d_scale_one = per_latent(grad_h_one * normed_one)
    tokens_grad = grad_mid + norm_back(grad_h_one * (1.0 + scale_one), normed_one, rscale_one)
    grad_mods = jnp.stack(
        [d_shift_one, d_scale_one, d_gate_one, d_shift_two, d_scale_two, d_gate_two], axis=1
    )
    mods_share = lax.psum_scatter(grad_mods, "tensor", scatter_dimension=2, tiled=True)
    grad_ada = jnp.einsum(
        "ld,lkf->dkf", cond_low.astype(jnp.float32), mods_share, precision=highest_precision_mode
    )
    grad_ada_bias = jnp.sum(mods_share, axis=0)
    cond_part = jnp.einsum(
        "lkf,dkf->ld", mods_share, w_ada.astype(jnp.float32), precision=highest_precision_mode
    )
    tensor_totals = lax.psum((cond_part, proj_bias_part, fc2_bias_part), "tensor")
    conditioning_grad = silu_pull(tensor_totals[0])[0]
    weight_totals = (
        lax.psum_scatter(grad_qkv_weight, "dp", scatter_dimension=0, tiled=True),
        lax.psum_scatter(weight_acc, "dp", scatter_dimension=1, tiled=True),
        lax.psum_scatter(grad_fc1, "dp", scatter_dimension=0, tiled=True),
        lax.psum_scatter(grad_fc2, "dp", scatter_dimension=1, tiled=True),
        lax.psum_scatter(grad_ada, "dp", scatter_dimension=0, tiled=True),
    )
    qkv_bias_pair = jnp.stack([qkv_bias_part[0], qkv_bias_part[2]])
    bias_totals = lax.psum(
        (qkv_bias_pair, tensor_totals[1], fc1_bias_part, tensor_totals[2], grad_ada_bias), "dp"
    )
    return (
        layer_out,
        tokens_grad,
        conditioning_grad,
        weight_totals[0],
        bias_totals[0],
        weight_totals[1],
        bias_totals[1],
        weight_totals[2],
        bias_totals[2],
        weight_totals[3],
        bias_totals[3],
        weight_totals[4],
        bias_totals[4],
    )


LANES = 128
LOG2E = 1.4426950408889634
f32 = jnp.float32
bf16 = jnp.bfloat16


def fits(mesh):
    return mesh.shape["tensor"] == 2 and mesh.shape["dp"] == 16


def low(values):
    return lax.reduce_precision(values, 8, 7).astype(bf16)


def nn(a, b):
    return lax.dot_general(a, b, (((1,), (0,)), ((), ())), preferred_element_type=f32)


def nt(a, b):
    return lax.dot_general(a, b, (((1,), (1,)), ((), ())), preferred_element_type=f32)


def tn(a, b):
    return lax.dot_general(a, b, (((0,), (0,)), ((), ())), preferred_element_type=f32)


def window(head):
    start = pl.multiple_of(((head * HEAD_DIM) // LANES) * LANES, LANES)
    return start, head * HEAD_DIM - start


def lane_mask(shape, first):
    lane = lax.broadcasted_iota(jnp.int32, shape, 1)
    return (lane >= first) & (lane < first + HEAD_DIM)


def attend_kernel(q_ref, own_ref, oth_ref, o_ref, lse_ref, *, heads, block, pad, scale):
    rows = q_ref.shape[0]
    factor = scale * LOG2E
    o_ref[...] = jnp.zeros_like(o_ref)

    def one_head(h, carry):
        at, first = window(h)

        def one_block(i, inner):
            r = pl.ds(pl.multiple_of(i * block, block), block)
            mask = lane_mask((block, 2 * LANES), first)
            q = q_ref[r, pl.ds(at, 2 * LANES)]
            q = jnp.where(mask, q, jnp.zeros_like(q))
            scores = [nt(ref[:, pl.ds(pad + at, 2 * LANES)], q) for ref in (own_ref, oth_ref)]
            peak = functools.reduce(
                jnp.maximum, [jnp.max(s, axis=0, keepdims=True) for s in scores]
            )
            peak = peak * factor
            expo = [jnp.exp2(s * factor - peak) for s in scores]
            total = sum(jnp.sum(e, axis=0, keepdims=True) for e in expo)
            inverse = 1.0 / total
            out = sum(
                tn(ref[:, pl.ds(2 * pad + at, 2 * LANES)], (e * inverse).astype(bf16))
                for ref, e in zip((own_ref, oth_ref), expo)
            ).T
            o_ref[r, pl.ds(at, 2 * LANES)] = jnp.where(
                mask, out.astype(bf16), o_ref[r, pl.ds(at, 2 * LANES)]
            )
            lse_ref[pl.ds(h, 1), r] = peak + jnp.log2(total)
            return inner

        return lax.fori_loop(0, rows // block, one_block, carry)

    lax.fori_loop(0, heads, one_head, 0)


def attend(queries, own, oth, heads, pad):
    rows = queries.shape[0]
    flops = 4 * heads * rows * 2 * rows * 2 * LANES
    return pl.pallas_call(
        functools.partial(
            attend_kernel, heads=heads, block=min(rows, 512), pad=pad, scale=HEAD_DIM**-0.5
        ),
        out_shape=(
            jax.ShapeDtypeStruct((rows, pad), bf16),
            jax.ShapeDtypeStruct((heads, rows), f32),
        ),
        cost_estimate=pl.CostEstimate(
            flops=4 * flops, bytes_accessed=8 * rows * pad * 2, transcendentals=heads * rows * rows * 2
        ),
        compiler_params=pltpu.CompilerParams(vmem_limit_bytes=40 * 2**20),
    )(queries, own, oth)


GELU = 0.7978845608028654


def feed_kernel(
    m_ref, g_ref, w1_ref, w2_ref, b_ref, act_ref, gp_ref, h_ref, out_ref, hacc_ref, oacc_ref, *, steps
):
    i = pl.program_id(0)

    @pl.when(i == 0)
    def _():
        hacc_ref[...] = jnp.zeros_like(hacc_ref)
        oacc_ref[...] = jnp.zeros_like(oacc_ref)

    pre = nn(m_ref[...], w1_ref[...]) + b_ref[...]
    grad_act = nn(g_ref[...], w2_ref[...])
    square = pre * pre
    gate = 1.0 / (1.0 + jnp.exp((-2.0 * GELU) * pre * (1.0 + 0.044715 * square)))
    act = (pre * gate).astype(bf16)
    act_ref[...] = act
    slope = gate + pre * gate * (1.0 - gate) * ((2.0 * GELU) * (1.0 + (3.0 * 0.044715) * square))
    grad_pre = (grad_act * slope).astype(bf16)
    gp_ref[...] = grad_pre
    hacc_ref[...] += nt(grad_pre, w1_ref[...])
    oacc_ref[...] += nt(act, w2_ref[...])

    @pl.when(i == steps - 1)
    def _():
        h_ref[...] = hacc_ref[...].astype(h_ref.dtype)
        out_ref[...] = oacc_ref[...].astype(out_ref.dtype)


def feed(m, g, weights, bias, out_dtype):
    rows, depth = m.shape
    hidden = weights.shape[1] // 2
    steps = 3 if hidden % (3 * LANES) == 0 else 1
    chunk = hidden // steps
    whole = pl.BlockSpec((rows, depth), lambda i: (0, 0))
    first = pl.BlockSpec((depth, chunk), lambda i: (0, i))
    second = pl.BlockSpec((depth, chunk), lambda i: (0, i + steps))
    tall = pl.BlockSpec((rows, chunk), lambda i: (0, i))
    return pl.pallas_call(
        functools.partial(feed_kernel, steps=steps),
        grid=(steps,),
        in_specs=[whole, whole, first, second, pl.BlockSpec((1, chunk), lambda i: (0, i))],
        out_specs=[tall, tall, whole, whole],
        out_shape=(
            jax.ShapeDtypeStruct((rows, hidden), bf16),
            jax.ShapeDtypeStruct((rows, hidden), bf16),
            jax.ShapeDtypeStruct((rows, depth), out_dtype),
            jax.ShapeDtypeStruct((rows, depth), out_dtype),
        ),
        scratch_shapes=[pltpu.VMEM((rows, depth), f32)] * 2,
        cost_estimate=pl.CostEstimate(
            flops=12 * rows * depth * hidden,
            bytes_accessed=4 * depth * hidden + 8 * rows * depth + 4 * rows * hidden,
            transcendentals=rows * hidden,
        ),
        compiler_params=pltpu.CompilerParams(vmem_limit_bytes=56 * 2**20),
    )(m, g, weights, weights, bias)


def peers(n_dp):
    me, side = lax.axis_index("dp"), lax.axis_index("tensor")
    n_z = n_dp // 4
    z, x, c = me // 4, (me // 2) % 2, me % 2
    across = (me, 1 - side)
    core = (z * 4 + x * 2 + 1 - c, side)
    beside = (z * 4 + (1 - x) * 2 + c, side)
    lines = [(lax.rem(z + s, n_z) * 4 + x * 2 + c, side) for s in range(1, n_z)]
    return (me, z, x, c), across, core, beside, lines


def greet(partners):
    barrier = pltpu.get_barrier_semaphore()
    for partner in partners:
        pl.semaphore_signal(barrier, inc=1, device_id=partner, device_id_type=pl.DeviceIdType.MESH)
    pl.semaphore_wait(barrier, len(partners))


SPAN = 2.0**63
QUARTERS = (SPAN, 1.0, 1.0 / SPAN, 1.0 / SPAN / SPAN)
STEP = 1.0 / 512.0


def encode(values, bound):
    scaled = (values * 2.0**40) * (0.98 * 2.0**23 / bound)
    size = jnp.abs(scaled)
    near = size.astype(bf16).astype(f32)
    rest, step = size - near, near * STEP
    below = jnp.where(rest < -step, QUARTERS[0], QUARTERS[1])
    above = jnp.where(rest < step, QUARTERS[2], QUARTERS[3])
    coded = near * jnp.where(rest < 0.0, below, above)
    coded = jnp.where(near <= 1.0, 0.0, coded)
    return jnp.where(scaled < 0.0, -coded, coded).astype(bf16)


def decode(coded, bound):
    coded = coded.astype(f32)
    size = jnp.abs(coded)
    factors = [(1.0 + (k - 1.5) * STEP) / q for k, q in enumerate(QUARTERS)]
    large = jnp.where(size > SPAN, factors[0], factors[1])
    small = jnp.where(size > 1.0 / SPAN, factors[2], factors[3])
    scaled = coded * jnp.where(size > 1.0, large, small)
    return (scaled * 2.0**-40) * (bound * (2.0**-23 / 0.98))


def linker(send_sem, recv_sem):
    def link(source, target, to, k):
        return pltpu.make_async_remote_copy(
            src_ref=source, dst_ref=target, send_sem=send_sem.at[k], recv_sem=recv_sem.at[k],
            device_id=to, device_id_type=pl.DeviceIdType.MESH,
        )

    return link


def turn_over(reads, turned_ref, n_z, block):
    for j, read in enumerate(reads):
        turned = read().astype(f32).T
        rows = turned.shape[1]
        for z in range(n_z):
            for x in range(2):
                for c in range(2):
                    b = (z * 2 + x) * 2 + c
                    at = pl.ds((x * n_z + z) * block, block)
                    turned_ref[c, at, pl.ds(j * rows, rows)] = turned[
                        b * block : (b + 1) * block
                    ].astype(bf16)


def open_kernel(
    cond_ref, ada_ref, bias_ref, x_ref, out_ref,
    aown_ref, aoth_ref, gown_ref, mods_ref, top_ref, mine_ref, gsum_ref,
    cond_all, part_ref, cgot_ref, xgot_ref, zgot_ref, half_ref, other_ref, normed_ref,
    tsend_ref, tgot_ref, send_sem, recv_sem,
    *, n_dp, n_mods, width,
):
    (me, z, x, c), across, core, beside, lines = peers(n_dp)
    n_z = n_dp // 4
    side = lax.axis_index("tensor")
    link = linker(send_sem, recv_sem)
    rows, depth = x_ref.shape
    block = ada_ref.shape[0]
    tile = min(rows, 128)
    per_mod = part_ref.shape[3] // n_mods
    greet([across, core, beside] + lines)

    def step(copies, beside_work=None):
        for copy in copies:
            copy.start()
        if beside_work is not None:
            beside_work()
        for copy in copies:
            copy.wait()

    def loop(body):
        def one(i, carry):
            body(pl.ds(pl.multiple_of(i * tile, tile), tile))
            return carry

        lax.fori_loop(0, rows // tile, one, 0)

    def norm_tile(r):
        normed_ref[r, :] = normalize(x_ref[r, :])[0]

    cond_all[z, x, c] = cond_ref[...]
    mine = cond_all.at[z, x, c]
    step([link(mine, mine, core, 0)], lambda: loop(norm_tile))
    mine = cond_all.at[z, x]
    step([link(mine, mine, beside, 1)])
    mine = cond_all.at[z]
    step([link(mine, mine, to, 2 + s) for s, to in enumerate(lines)])
    everyone = cond_all[...].reshape(n_dp, depth // LANES, LANES)
    flat = jnp.concatenate([everyone[:, i, :] for i in range(depth // LANES)], axis=1)
    feature = lax.broadcasted_iota(jnp.int32, (depth, block), 0)
    column = lax.broadcasted_iota(jnp.int32, (depth, block), 1)
    chosen = nn(flat.astype(bf16), (feature == column + me * block).astype(bf16))
    mine_ref[...] = chosen

    made = nn(chosen.astype(bf16), ada_ref[...])
    for g in range(part_ref.shape[3]):
        part_ref[:, :, :, g, :] = made[:, g * LANES : (g + 1) * LANES].reshape(n_z, 2, 2, LANES)
    at = 1 + n_z
    step([link(part_ref.at[:, :, 1 - c], cgot_ref, core, at)])
    cgot_ref[...] += part_ref[:, :, c]
    step([link(cgot_ref.at[:, 1 - x], xgot_ref, beside, at + 1)])
    xgot_ref[...] += cgot_ref[:, x]
    step(
        [
            link(xgot_ref.at[lax.rem(z + s + 1, n_z)], zgot_ref.at[s], to, at + 2 + s)
            for s, to in enumerate(lines)
        ]
    )
    total = xgot_ref[z] + bias_ref[...]
    for s in range(n_z - 1):
        total += zgot_ref[s]
    half_ref[...] = total
    at += n_z + 1
    step([link(half_ref, other_ref, across, at)])
    halves = []
    for ref in (half_ref, other_ref):
        values = ref[...]
        halves.append(
            [
                jnp.concatenate(
                    [values[j * per_mod + i : j * per_mod + i + 1, :] for i in range(per_mod)],
                    axis=1,
                )[:, :width]
                for j in range(n_mods)
            ]
        )
    mods_ref[...] = jnp.zeros_like(mods_ref)
    for j, (own, oth) in enumerate(zip(*halves)):
        first = jnp.where(side == 0, own, oth)
        second = jnp.where(side == 0, oth, own)
        mods_ref[pl.ds(j, 1), :] = jnp.concatenate([first, second], axis=1)

    def input_tile(r):
        made = normed_ref[r, :] * (1.0 + mods_ref[1:2, :]) + mods_ref[0:1, :]
        aown_ref[r, :] = made.astype(bf16)

    loop(input_tile)
    tokens = link(aown_ref, aoth_ref, across, at + 1)
    tokens.start()

    def grad_tile(i, carry):
        r = pl.ds(pl.multiple_of(i * tile, tile), tile)
        made = (mods_ref[5:6, :] * out_ref[r, :]).astype(bf16)
        gown_ref[r, :] = made
        made = made.astype(f32)
        most = jnp.max(jnp.abs(made), axis=0, keepdims=True)
        return carry[0] + jnp.sum(made, axis=0, keepdims=True), jnp.maximum(carry[1], most)

    none = (jnp.zeros((1, depth), f32),) * 2
    g_sum, g_top = lax.fori_loop(0, rows // tile, grad_tile, none)
    gsum_ref[...] = g_sum
    tops = (
        jnp.max(g_top, axis=1, keepdims=True),
        jnp.max(jnp.abs(mods_ref[4:5, :]), axis=1, keepdims=True)
        + jnp.max(jnp.abs(mods_ref[3:4, :]), axis=1, keepdims=True),
    )
    row = lax.broadcasted_iota(jnp.int32, top_ref.shape, 0)
    best = jnp.where(row == 0, tops[0], jnp.where(row == 1, tops[1], 0.0))
    at += 2
    for k, to in enumerate((across, core, beside)):
        tsend_ref[k] = best
        step([link(tsend_ref.at[k], tgot_ref.at[k], to, at + k)])
        best = jnp.maximum(best, tgot_ref[k])
    tsend_ref[3] = best
    step([link(tsend_ref.at[3], tgot_ref.at[3 + s], to, at + 3 + s) for s, to in enumerate(lines)])
    for s in range(n_z - 1):
        best = jnp.maximum(best, tgot_ref[3 + s])
    top_ref[...] = best
    tokens.wait()


def open_part(cond, ada, bias, tokens, out_grad, width):
    n_dp = lax.axis_size("dp")
    n_z = n_dp // 4
    rows, depth = tokens.shape
    block = ada.shape[0]
    groups = bias.shape[0]
    n_links = 2 * (n_z + 1) + 2 + 2 + n_z
    vmem = pl.BlockSpec(memory_space=pltpu.VMEM)
    return pl.pallas_call(
        functools.partial(open_kernel, n_dp=n_dp, n_mods=6, width=width),
        out_shape=(
            jax.ShapeDtypeStruct((rows, depth), bf16),
            jax.ShapeDtypeStruct((rows, depth), bf16),
            jax.ShapeDtypeStruct((rows, depth), bf16),
            jax.ShapeDtypeStruct((8, depth), f32),
            jax.ShapeDtypeStruct((8, LANES), f32),
            jax.ShapeDtypeStruct((n_dp, block), f32),
            jax.ShapeDtypeStruct((1, depth), f32),
        ),
        in_specs=[vmem] * 5,
        out_specs=[vmem] * 7,
        scratch_shapes=[
            pltpu.VMEM((n_z, 2, 2, depth // LANES, LANES), f32),
            pltpu.VMEM((n_z, 2, 2, groups, LANES), f32),
            pltpu.VMEM((n_z, 2, groups, LANES), f32),
            pltpu.VMEM((n_z, groups, LANES), f32),
            pltpu.VMEM((n_z - 1, groups, LANES), f32),
            pltpu.VMEM((groups, LANES), f32),
            pltpu.VMEM((groups, LANES), f32),
            pltpu.VMEM((rows, depth), f32),
            pltpu.VMEM((4, 8, LANES), f32),
            pltpu.VMEM((n_z + 2, 8, LANES), f32),
            pltpu.SemaphoreType.DMA((n_links,)),
            pltpu.SemaphoreType.DMA((n_links,)),
        ],
        cost_estimate=pl.CostEstimate(
            flops=40 * 10**9, bytes_accessed=20 * 10**6, transcendentals=0
        ),
        compiler_params=pltpu.CompilerParams(
            collective_id=3, has_side_effects=True, vmem_limit_bytes=32 * 2**20
        ),
    )(cond, ada, bias, tokens, out_grad)


def middle_kernel(
    hsend_ref, scale_ref, gate_ref, bound_ref,
    gown_any, goth_any, mown_any, moth_any, aown_any, aoth_any, pown_any, poth_any,
    hown_any, mid_any, out_any, branch_any, proj_any,
    grad_ref, zown_ref, zoth_ref, goown_ref, gooth_ref, sum_ref, colsum_ref,
    own2_ref, code2_ref, mine1_ref, code1_ref,
    left_ref, right_ref, hown_ref, mid_ref, branch_ref, proj_ref, turned_ref,
    csend_ref, cgot_ref, mine2_ref, xsend_ref, xgot_ref, hgot_ref,
    load_sem, left_sem, right_sem, send_sem, recv_sem,
    *, n_dp, steps,
):
    (me, z, x, c), across, core, beside, lines = peers(n_dp)
    n_z = n_dp // 4
    rows, depth = hsend_ref.shape
    block, hidden = own2_ref.shape
    chunk = hidden // steps
    tile = min(rows, 128)
    link = linker(send_sem, recv_sem)

    def left_loads(pieces):
        return [
            pltpu.make_async_copy(piece, left_ref.at[j], left_sem.at[j])
            for j, piece in enumerate(pieces)
        ]

    def right_loads(pieces, k):
        at = pl.ds(k * chunk, chunk)
        return [
            pltpu.make_async_copy(piece.at[:, at], right_ref.at[k % 2, j], right_sem.at[k % 2, j])
            for j, piece in enumerate(pieces)
        ]

    loads = [
        pltpu.make_async_copy(source, target, load_sem.at[k])
        for k, (source, target) in enumerate(
            (
                (hown_any, hown_ref),
                (mid_any, mid_ref),
                (out_any, grad_ref),
                (branch_any, branch_ref),
                (proj_any, proj_ref),
            )
        )
    ]

    def start(copies):
        for copy in copies:
            copy.start()

    def wait(copies):
        for copy in copies:
            copy.wait()

    start(left_loads((gown_any, goth_any)))
    for k in range(min(2, steps)):
        start(right_loads((aown_any, aoth_any), k))
    start(loads)
    greet([across, core, beside])
    half = link(hsend_ref, hgot_ref, across, 0)
    half.start()

    def product(which, slot):
        made = nn(turned_ref[which, :, pl.ds(0, rows)], right_ref[slot, 0])
        made += nn(turned_ref[which, :, pl.ds(rows, rows)], right_ref[slot, 1])
        return made.reshape(csend_ref.shape[1:])

    def core_link(w, k):
        return link(csend_ref.at[k % 2], cgot_ref.at[w, k], core, 2 + w * steps + k)

    def x_link(k):
        return link(xsend_ref.at[k], xgot_ref.at[k], beside, 2 + 2 * steps + k)

    def rounds(w, pieces, use):
        for k in range(steps + 1):
            if k < steps:
                wait(right_loads(pieces, k))
                if k >= 2:
                    core_link(w, k - 2).wait_send()
                csend_ref[k % 2] = product(1 - c, k % 2)
                core_link(w, k).start()
            if k > 0:
                j = k - 1
                core_link(w, j).wait_recv()
                cgot_ref[w, j] += product(c, j % 2)
                use(j)
                if j + 2 < steps:
                    start(right_loads(pieces, j + 2))
        for k in range(max(steps - 2, 0), steps):
            core_link(w, k).wait_send()

    def use_two(j):
        at = pl.ds(j * chunk, chunk)
        mine2_ref[:, :, at] = cgot_ref[0, j, x]
        away = cgot_ref[0, j, 1 - x].reshape(n_z * block, chunk)
        xsend_ref[j] = encode(away, bound_ref[0:1, 0:1])
        x_link(j).start()

    def use_one(j):
        at = pl.ds(j * chunk, chunk)
        mine1_ref[:, :, at] = cgot_ref[1, j, x]
        away = cgot_ref[1, j, 1 - x].reshape(n_z * block, chunk)
        code1_ref[:, at] = encode(away, bound_ref[1:2, 0:1])
        ones = jnp.ones((8, rows), bf16)
        colsum_ref[:, at] = nn(ones, right_ref[j % 2, 0]) + nn(ones, right_ref[j % 2, 1])

    wait(left_loads((gown_any, goth_any)))
    turn_over([lambda j=j: left_ref[j] for j in range(2)], turned_ref, n_z, block)
    start(left_loads((mown_any, moth_any)))
    rounds(0, (aown_any, aoth_any), use_two)
    for k in range(min(2, steps)):
        start(right_loads((pown_any, poth_any), k))

    wait(loads)
    half.wait()

    def norm_tile(i, carry):
        r = pl.ds(pl.multiple_of(i * tile, tile), tile)
        h = hown_ref[r, :] + hgot_ref[r, :].astype(f32)
        normed, rscale = normalize(mid_ref[r, :])
        grad = grad_ref[r, :] + norm_back(h * (1.0 + scale_ref[...]), normed, rscale)
        grad_ref[r, :] = grad
        turned = (gate_ref[...] * grad).astype(bf16)
        zown_ref[r, :] = turned
        parts = (grad * branch_ref[r, :], h, h * normed, turned.astype(f32))
        return tuple(
            total + jnp.sum(part, axis=0, keepdims=True) for total, part in zip(carry, parts)
        )

    totals = lax.fori_loop(0, rows // tile, norm_tile, (jnp.zeros((1, depth), f32),) * 4)
    turn_link = link(zown_ref, zoth_ref, across, 1)
    turn_link.start()
    sum_ref[...] = jnp.zeros_like(sum_ref)
    for j, total in enumerate(totals):
        sum_ref[pl.ds(j, 1), :] = total

    wait(left_loads((mown_any, moth_any)))
    turn_over([lambda j=j: left_ref[j] for j in range(2)], turned_ref, n_z, block)
    rounds(1, (pown_any, poth_any), use_one)
    goown_ref[...] = nn(zown_ref[...], proj_ref[...]).astype(bf16)

    code2_ref[...] = jnp.zeros_like(code2_ref)
    for k in range(steps):
        x_link(k).wait()
        at = pl.ds(k * chunk, chunk)
        came = decode(xgot_ref[k], bound_ref[0:1, 0:1]).reshape(n_z, block, chunk)
        mine2_ref[:, :, at] += came
        own2_ref[:, at] = mine2_ref[z, :, at]
        for s in range(n_z - 1):
            away = mine2_ref[lax.rem(z + s + 1, n_z), :, at]
            code2_ref[s, pl.ds(0, block), at] = encode(away, bound_ref[0:1, 0:1])
    turn_link.wait()
    gooth_ref[...] = nn(zoth_ref[...], proj_ref[...]).astype(bf16)


def middle_part(
    h_send, scale, gate, bounds, g_own, g_oth, m_own, m_oth, act_own, act_oth, gp_own, gp_oth,
    h_own, middle, out_grad, branch, w_proj, block,
):
    n_dp = lax.axis_size("dp")
    n_z = n_dp // 4
    rows, depth = h_send.shape
    hidden = act_own.shape[1]
    pad = w_proj.shape[1]
    steps = 3 if hidden % (3 * LANES) == 0 else 1
    chunk = hidden // steps
    tall = -(-block // 16) * 16
    vmem = pl.BlockSpec(memory_space=pltpu.VMEM)
    n_links = 2 + 3 * steps
    return pl.pallas_call(
        functools.partial(middle_kernel, n_dp=n_dp, steps=steps),
        out_shape=(
            jax.ShapeDtypeStruct((rows, depth), f32),
            jax.ShapeDtypeStruct((rows, depth), bf16),
            jax.ShapeDtypeStruct((rows, depth), bf16),
            jax.ShapeDtypeStruct((rows, pad), bf16),
            jax.ShapeDtypeStruct((rows, pad), bf16),
            jax.ShapeDtypeStruct((8, depth), f32),
            jax.ShapeDtypeStruct((8, hidden), f32),
            jax.ShapeDtypeStruct((block, hidden), f32),
            jax.ShapeDtypeStruct((n_z - 1, tall, hidden), bf16),
            jax.ShapeDtypeStruct((n_z, block, hidden), f32),
            jax.ShapeDtypeStruct((n_z * block, hidden), bf16),
        ),
        in_specs=[vmem] * 4 + [pl.BlockSpec(memory_space=pl.ANY)] * 13,
        out_specs=[vmem] * 11,
        scratch_shapes=[
            pltpu.VMEM((2, rows, depth), bf16),
            pltpu.VMEM((2, 2, rows, chunk), bf16),
            pltpu.VMEM((rows, depth), f32),
            pltpu.VMEM((rows, depth), f32),
            pltpu.VMEM((rows, depth), f32),
            pltpu.VMEM(w_proj.shape, bf16),
            pltpu.VMEM((2, depth // 2, 2 * rows), bf16),
            pltpu.VMEM((2, 2, n_z, block, chunk), f32),
            pltpu.VMEM((2, steps, 2, n_z, block, chunk), f32),
            pltpu.VMEM((n_z, block, hidden), f32),
            pltpu.VMEM((steps, n_z * block, chunk), bf16),
            pltpu.VMEM((steps, n_z * block, chunk), bf16),
            pltpu.VMEM((rows, depth), bf16),
            pltpu.SemaphoreType.DMA((5,)),
            pltpu.SemaphoreType.DMA((2,)),
            pltpu.SemaphoreType.DMA((2, 2)),
            pltpu.SemaphoreType.DMA((n_links,)),
            pltpu.SemaphoreType.DMA((n_links,)),
        ],
        cost_estimate=pl.CostEstimate(
            flops=60 * 10**9, bytes_accessed=100 * 10**6, transcendentals=0
        ),
        compiler_params=pltpu.CompilerParams(
            collective_id=1, has_side_effects=True, vmem_limit_bytes=62 * 2**20
        ),
    )(
        h_send, scale.reshape(1, -1), gate.reshape(1, -1), bounds, g_own, g_oth, m_own, m_oth,
        act_own, act_oth, gp_own, gp_oth, h_own, middle, out_grad, branch, w_proj,
    )


def attend_back_kernel(
    own_ref, oth_ref, gown_ref, goth_ref, lown_ref, loth_ref, bound_ref, own2_ref,
    out_any, code2_any, code1_any, mine1_any,
    down_ref, doth_ref, branch_ref, total2_ref, own1_ref, next1_ref,
    dk_ref, dv_ref, out_ref, code2_ref, got2_ref, code1_ref, got1_ref, mine1_ref,
    load_sem, send_sem, recv_sem,
    *, n_dp, heads, block, pad, scale,
):
    (me, z, x, c), across, core, beside, lines = peers(n_dp)
    n_z = n_dp // 4
    link = linker(send_sem, recv_sem)
    loads = [
        pltpu.make_async_copy(source, target, load_sem.at[k])
        for k, (source, target) in enumerate(
            (
                (out_any, out_ref),
                (code2_any, code2_ref),
                (code1_any, code1_ref),
                (mine1_any, mine1_ref),
            )
        )
    ]
    for load in loads:
        load.start()
    greet([across, beside] + lines)
    for load in loads:
        load.wait()
    links = [
        link(out_ref, branch_ref, across, 0),
        link(code1_ref, got1_ref, beside, 1),
    ] + [link(code2_ref.at[s], got2_ref.at[s], to, 2 + s) for s, to in enumerate(lines)]
    for one in links:
        one.start()
    rows = own_ref.shape[0]
    factor = scale * LOG2E
    down_ref[...] = jnp.zeros_like(down_ref)
    doth_ref[...] = jnp.zeros_like(doth_ref)

    def one_head(h, carry):
        at, first = window(h)
        dk_ref[...] = jnp.zeros_like(dk_ref)
        dv_ref[...] = jnp.zeros_like(dv_ref)
        keys = [ref[:, pl.ds(pad + at, 2 * LANES)] for ref in (own_ref, oth_ref)]
        values = [ref[:, pl.ds(2 * pad + at, 2 * LANES)] for ref in (own_ref, oth_ref)]
        parts = ((own_ref, gown_ref, lown_ref, down_ref), (oth_ref, goth_ref, loth_ref, doth_ref))
        for q_ref, g_ref, l_ref, d_ref in parts:

            def one_block(i, inner):
                r = pl.ds(pl.multiple_of(i * block, block), block)
                mask = lane_mask((block, 2 * LANES), first)
                q = q_ref[r, pl.ds(at, 2 * LANES)]
                q = jnp.where(mask, q, jnp.zeros_like(q))
                g = g_ref[r, pl.ds(at, 2 * LANES)]
                g = jnp.where(mask, g, jnp.zeros_like(g))
                lse = l_ref[pl.ds(h, 1), r]
                probs = [jnp.exp2(nt(k, q) * factor - lse) for k in keys]
                grad_p = [nt(v, g) for v in values]
                delta = sum(jnp.sum(p * d, axis=0, keepdims=True) for p, d in zip(probs, grad_p))
                grad_s = [(p * (d - delta)).astype(bf16) for p, d in zip(probs, grad_p)]
                dq = sum(tn(k, s) for k, s in zip(keys, grad_s)).T * scale
                d_ref[r, pl.ds(at, 2 * LANES)] = jnp.where(
                    mask, dq.astype(bf16), d_ref[r, pl.ds(at, 2 * LANES)]
                )
                for j in range(2):
                    dk_ref[j] += nn(grad_s[j], q)
                    dv_ref[j] += nn(probs[j].astype(bf16), g)
                return inner

            lax.fori_loop(0, rows // block, one_block, 0)
        mask = lane_mask((rows, 2 * LANES), first)
        for j, d_ref in enumerate((down_ref, doth_ref)):
            for lane, new in ((pad, dk_ref[j] * scale), (2 * pad, dv_ref[j])):
                d_ref[:, pl.ds(lane + at, 2 * LANES)] = jnp.where(
                    mask, new.astype(bf16), d_ref[:, pl.ds(lane + at, 2 * LANES)]
                )
        return carry

    lax.fori_loop(0, heads, one_head, 0)

    for one in links:
        one.wait()
    depth = own1_ref.shape[0]
    hidden = own1_ref.shape[1]
    total = own2_ref[...]
    for s in range(n_z - 1):
        total += decode(got2_ref[s, pl.ds(0, depth), :], bound_ref[0:1, 0:1])
    total2_ref[...] = total
    mine1_ref[...] += decode(got1_ref[...], bound_ref[1:2, 0:1]).reshape(n_z, depth, hidden)
    own1_ref[...] = mine1_ref[z]
    next1_ref[...] = jnp.zeros_like(next1_ref)
    for s in range(n_z - 1):
        away = mine1_ref[lax.rem(z + s + 1, n_z)]
        next1_ref[s, pl.ds(0, depth), :] = encode(away, bound_ref[1:2, 0:1])


def attend_back(
    own, oth, gown, goth, lown, loth, bounds, own2, b_send, code2, code1, mine1, heads, pad
):
    n_dp = lax.axis_size("dp")
    n_z, depth, hidden = mine1.shape
    n_links = n_z + 1
    rows = own.shape[0]
    vmem = pl.BlockSpec(memory_space=pltpu.VMEM)
    flops = 10 * heads * 4 * rows * rows * 2 * LANES
    return pl.pallas_call(
        functools.partial(
            attend_back_kernel, n_dp=n_dp, heads=heads, block=min(rows, 512), pad=pad, scale=HEAD_DIM**-0.5
        ),
        out_shape=(jax.ShapeDtypeStruct((rows, 3 * pad), bf16),) * 2
        + (
            jax.ShapeDtypeStruct(b_send.shape, b_send.dtype),
            jax.ShapeDtypeStruct((depth, hidden), f32),
            jax.ShapeDtypeStruct((depth, hidden), f32),
            jax.ShapeDtypeStruct(code2.shape, code2.dtype),
        ),
        in_specs=[vmem] * 8 + [pl.BlockSpec(memory_space=pl.ANY)] * 4,
        out_specs=[vmem] * 6,
        scratch_shapes=[pltpu.VMEM((2, rows, 2 * LANES), f32)] * 2
        + [
            pltpu.VMEM(b_send.shape, b_send.dtype),
            pltpu.VMEM(code2.shape, bf16),
            pltpu.VMEM(code2.shape, bf16),
            pltpu.VMEM(code1.shape, bf16),
            pltpu.VMEM(code1.shape, bf16),
            pltpu.VMEM(mine1.shape, f32),
            pltpu.SemaphoreType.DMA((4,)),
            pltpu.SemaphoreType.DMA((n_links,)),
            pltpu.SemaphoreType.DMA((n_links,)),
        ],
        cost_estimate=pl.CostEstimate(
            flops=flops, bytes_accessed=16 * rows * pad * 2, transcendentals=heads * rows * rows * 4
        ),
        compiler_params=pltpu.CompilerParams(
            collective_id=2, has_side_effects=True, vmem_limit_bytes=60 * 2**20
        ),
    )(own, oth, gown, goth, lown, loth, bounds, own2, b_send, code2, code1, mine1)


def close_kernel(
    aown_ref, aoth_ref, down_ref, doth_ref, mine_ref, other_ref, cond_ref, scale_ref, tops_ref,
    fcbound_ref, fcown_ref, fccode_ref,
    w_any, x_any, mid_any, zown_any, zoth_any, oown_any, ooth_any, ada_any,
    tokens_ref, grads_ref, gada_ref, total_ref, row_ref, fctotal_ref,
    w_ref, x_ref, mid_ref, z_ref, o_ref, ada_ref,
    turned_ref, part_ref, got_ref, xsend_ref, xgot_ref, zsend_ref, zgot_ref,
    hsend_ref, hgot_ref, hown_ref, fcgot_ref,
    rows_ref, rgot_ref, all_ref, cpart_ref, cswap_ref, parts_ref, bound_ref, bgot_ref,
    load_sem, send_sem, recv_sem,
    *, n_dp, n_mods, n_shared, pad,
):
    (me, z, x, c), across, core, beside, lines = peers(n_dp)
    n_z = n_dp // 4
    side = lax.axis_index("tensor")
    loads = [
        pltpu.make_async_copy(source, target, load_sem.at[k])
        for k, (source, target) in enumerate(
            (
                (w_any, w_ref),
                (x_any, x_ref),
                (zown_any, z_ref.at[0]),
                (zoth_any, z_ref.at[1]),
                (oown_any, o_ref.at[0]),
                (ooth_any, o_ref.at[1]),
                (mid_any, mid_ref),
                (ada_any, ada_ref),
            )
        )
    ]
    for load in loads:
        load.start()
    greet([across, core, beside] + lines)

    rows, depth = aown_ref.shape
    width = mine_ref.shape[1]
    block = got_ref.shape[3]
    n_parts = part_ref.shape[0]
    tile = min(rows, 128)

    link = linker(send_sem, recv_sem)

    def core_link(k):
        return link(part_ref.at[k], got_ref.at[k], core, k)

    def x_link(k):
        return link(xsend_ref.at[k], xgot_ref.at[k], beside, n_parts + k)

    def z_link(k, s):
        at = 2 * n_parts + k * (n_z - 1) + s
        return link(zsend_ref.at[k, s], zgot_ref.at[k, s], lines[s], at)

    n_sums = (n_z + 1) * n_parts
    half = link(hsend_ref, hgot_ref, across, n_sums)
    swap_rows = link(rows_ref.at[1], rgot_ref, across, n_sums + 1)
    swap_part = link(cpart_ref, cswap_ref, across, n_sums + 2)
    core_bound = link(bound_ref.at[0], bgot_ref.at[0], core, n_sums + 3)
    x_bound = link(bound_ref.at[1], bgot_ref.at[1], beside, n_sums + 4)
    z_bounds = [
        link(bound_ref.at[2], bgot_ref.at[2 + s], lines[s], n_sums + 5 + s) for s in range(n_z - 1)
    ]

    fc_links = [
        link(fccode_ref.at[s], fcgot_ref.at[s], to, n_sums + 7 + 3 * n_z + s)
        for s, to in enumerate(lines)
    ]
    for one in fc_links:
        one.start()

    def spread(ref, first):
        return (
            [link(ref.at[z, x, c], ref.at[z, x, c], core, first)],
            [link(ref.at[z, x], ref.at[z, x], beside, first + 1)],
            [link(ref.at[z], ref.at[z], to, first + 2 + s) for s, to in enumerate(lines)],
        )

    def start(links):
        for one in links:
            one.start()

    def wait(links):
        for one in links:
            one.wait()

    def largest(ref):
        return jnp.max(jnp.abs(ref[...].astype(f32)))

    def product(which, right_own, right_oth):
        made = nn(turned_ref[which, :, pl.ds(0, rows)], right_own)
        made += nn(turned_ref[which, :, pl.ds(rows, rows)], right_oth)
        return made.reshape(got_ref.shape[1:])

    def columns(k):
        at = pl.ds(pl.multiple_of(k * pad, LANES), pad)
        return down_ref[:, at], doth_ref[:, at]

    def to_core(k, right):
        part_ref[k] = product(1 - c, *right)
        core_link(k).start()

    def to_beside(k, right):
        core_link(k).wait_recv()
        got_ref[k] += product(c, *right)
        away = got_ref[k, 1 - x].reshape(n_z * block, pad)
        xsend_ref[k] = encode(away, bound_ref[1, 0:1, 0:1])
        x_link(k).start()

    def to_lines(k):
        x_link(k).wait_recv()
        came = decode(xgot_ref[k], bgot_ref[1, 0:1, 0:1])
        got_ref[k, x] += came.reshape(n_z, block, pad)
        for s in range(n_z - 1):
            away = got_ref[k, x, lax.rem(z + s + 1, n_z)]
            zsend_ref[k, s, pl.ds(0, block), :] = encode(away, bound_ref[2, 0:1, 0:1])
            z_link(k, s).start()

    def loop(count, step):
        def body(k, carry):
            step(k)
            return carry

        lax.fori_loop(0, count, body, 0)

    most = tops_ref[0:1, 0:1] * jnp.maximum(largest(down_ref), largest(doth_ref))
    most = (most + tops_ref[1:2, 0:1]) * (1.02 * 2 * rows) + 1e-30
    bound_ref[0] = jnp.broadcast_to(most, bound_ref.shape[1:])
    core_bound.start()
    zsend_ref[...] = jnp.zeros_like(zsend_ref)
    turn_over((lambda: aown_ref[...], lambda: aoth_ref[...]), turned_ref, n_z, block)
    loop(3, lambda k: to_core(k, columns(k)))
    core_bound.wait()
    bound_ref[1] = bound_ref[0] + bgot_ref[0]
    x_bound.start()

    x_bound.wait()
    bound_ref[2] = bound_ref[1] + bgot_ref[1]
    start(z_bounds)
    loop(3, lambda k: to_beside(k, columns(k)))

    wait(loads[:1])

    def h_other(i):
        r = pl.ds(pl.multiple_of(i * tile, tile), tile)
        hsend_ref[r, :] = nt(doth_ref[r, :], w_ref[...]).astype(bf16)

    loop(rows // tile, h_other)
    half.start()
    wait(loads[2:6])
    turn_over((lambda: z_ref[0], lambda: z_ref[1]), turned_ref, n_z, block)
    last = n_parts - 1
    to_core(last, (o_ref[0], o_ref[1]))
    to_lines(0)

    def h_own(i):
        r = pl.ds(pl.multiple_of(i * tile, tile), tile)
        hown_ref[r, :] = nt(down_ref[r, :], w_ref[...])

    loop(rows // tile, h_own)
    ones = jnp.ones((8, rows), bf16)
    d_sums = nn(ones, down_ref[...]) + nn(ones, doth_ref[...])
    to_beside(last, (o_ref[0], o_ref[1]))
    to_lines(1)

    wait(loads[1:2] + loads[6:])
    half.wait_recv()

    def last_norm(i, carry):
        r = pl.ds(pl.multiple_of(i * tile, tile), tile)
        h = hown_ref[r, :] + hgot_ref[r, :].astype(f32)
        normed, rscale = normalize(x_ref[r, :])
        tokens_ref[r, :] = mid_ref[r, :] + norm_back(h * (1.0 + scale_ref[...]), normed, rscale)
        return (
            carry[0] + jnp.sum(h, axis=0, keepdims=True),
            carry[1] + jnp.sum(h * normed, axis=0, keepdims=True),
        )

    late = lax.fori_loop(0, rows // tile, last_norm, (jnp.zeros((1, depth), f32),) * 2)
    rows_ref[0] = mine_ref[...]
    rows_ref[1] = other_ref[...]
    for j, values in enumerate(late):
        low_half, high_half = values[:, :width], values[:, width:]
        rows_ref[0, pl.ds(j, 1), :] = jnp.where(side == 0, low_half, high_half)
        rows_ref[1, pl.ds(j, 1), :] = jnp.where(side == 0, high_half, low_half)
    swap_rows.start()
    for j, at in ((0, 0), (1, 2 * pad)):
        rows_ref[0, pl.ds(n_mods + j, 1), :] = d_sums[:1, at : at + width]
    to_lines(2)

    swap_rows.wait()
    row = lax.broadcasted_iota(jnp.int32, mine_ref.shape, 0)
    shared = (row < n_mods) | (row >= mine_ref.shape[0] - n_shared)
    all_ref[z, x, c] = rows_ref[0] + jnp.where(shared, rgot_ref[...], 0.0)
    along = spread(all_ref, n_sums + 4 + n_z)
    start(along[0])
    wait(along[0])
    start(along[1])
    to_lines(last)
    wait(along[1])
    start(along[2])
    wait(along[2])
    everything = all_ref[...].reshape((n_dp,) + mine_ref.shape)
    total_ref[...] = jnp.sum(everything, axis=0)
    cond = cond_ref[...]
    part = jnp.zeros(cond.shape, f32)
    for j in range(n_mods):
        part += lax.dot_general(
            everything[:, j, :], ada_ref[j].astype(f32), (((1,), (1,)), ((), ())),
            precision=highest_precision_mode, preferred_element_type=f32,
        )
    cpart_ref[...] = part
    swap_part.start()
    for j in range(n_mods):
        gada_ref[j] = lax.dot_general(
            cond, everything[:, j, :], (((0,), (0,)), ((), ())),
            precision=highest_precision_mode, preferred_element_type=f32,
        )
    swap_part.wait()
    whole = cpart_ref[...] + cswap_ref[...]
    parts_ref[z, x, c] = whole
    along = spread(parts_ref, n_sums + 6 + 2 * n_z)
    for links in along:
        start(links)
        wait(links)
    for p in range(n_dp):
        row_ref[pl.ds(p, 1), :] = parts_ref[p // 4, (p // 2) % 2, p % 2, pl.ds(me, 1), :]

    wait(z_bounds)

    def finish(k):
        total = got_ref[k, x, z]
        for s in range(n_z - 1):
            z_link(k, s).wait_recv()
            total += decode(zgot_ref[k, s, pl.ds(0, block), :], bgot_ref[2 + s, 0:1, 0:1])
        grads_ref[k] = total

    loop(n_parts, finish)
    half.wait_send()
    wait(fc_links)
    total = fcown_ref[...]
    for s in range(n_z - 1):
        total += decode(fcgot_ref[s, pl.ds(0, block), :], fcbound_ref[1:2, 0:1])
    fctotal_ref[...] = total

    def sent(k):
        core_link(k).wait_send()
        x_link(k).wait_send()
        for s in range(n_z - 1):
            z_link(k, s).wait_send()

    loop(n_parts, sent)


def close(
    a_own, a_oth, d_own, d_oth, mine, other, cond, scale, tops, fc_bounds, fc_own, fc_code, w_qkv, tokens, mid_grad,
    z_own, z_oth, o_own, o_oth, ada, n_shared,
):
    n_dp = lax.axis_size("dp")
    n_z = n_dp // 4
    n_mods, block, width = ada.shape
    rows, depth = tokens.shape
    pad = o_own.shape[1]
    n_rows = mine.shape[0]
    n_parts = 4
    n_links = (n_z + 1) * n_parts + 6 + 4 * n_z
    tall = -(-block // 16) * 16
    vmem = pl.BlockSpec(memory_space=pltpu.VMEM)
    return pl.pallas_call(
        functools.partial(close_kernel, n_dp=n_dp, n_mods=n_mods, n_shared=n_shared, pad=pad),
        out_shape=(
            jax.ShapeDtypeStruct((rows, depth), f32),
            jax.ShapeDtypeStruct((n_parts, block, pad), f32),
            jax.ShapeDtypeStruct((n_mods, block, width), f32),
            jax.ShapeDtypeStruct((n_rows, width), f32),
            jax.ShapeDtypeStruct((n_dp, block), f32),
            jax.ShapeDtypeStruct(fc_own.shape, f32),
        ),
        in_specs=[vmem] * 12 + [pl.BlockSpec(memory_space=pl.ANY)] * 8,
        out_specs=[vmem] * 6,
        scratch_shapes=[
            pltpu.VMEM(w_qkv.shape, bf16),
            pltpu.VMEM((rows, depth), f32),
            pltpu.VMEM((rows, depth), f32),
            pltpu.VMEM((2, rows, depth), bf16),
            pltpu.VMEM((2, rows, pad), bf16),
            pltpu.VMEM(ada.shape, bf16),
            pltpu.VMEM((2, depth // 2, 2 * rows), bf16),
            pltpu.VMEM((n_parts, 2, n_z, block, pad), f32),
            pltpu.VMEM((n_parts, 2, n_z, block, pad), f32),
            pltpu.VMEM((n_parts, n_z * block, pad), bf16),
            pltpu.VMEM((n_parts, n_z * block, pad), bf16),
            pltpu.VMEM((n_parts, n_z - 1, tall, pad), bf16),
            pltpu.VMEM((n_parts, n_z - 1, tall, pad), bf16),
            pltpu.VMEM((rows, depth), bf16),
            pltpu.VMEM((rows, depth), bf16),
            pltpu.VMEM((rows, depth), f32),
            pltpu.VMEM(fc_code.shape, bf16),
            pltpu.VMEM((2, n_rows, width), f32),
            pltpu.VMEM((n_rows, width), f32),
            pltpu.VMEM((n_z, 2, 2, n_rows, width), f32),
            pltpu.VMEM((n_dp, block), f32),
            pltpu.VMEM((n_dp, block), f32),
            pltpu.VMEM((n_z, 2, 2, n_dp, block), f32),
            pltpu.VMEM((3, 8, LANES), f32),
            pltpu.VMEM((n_z + 1, 8, LANES), f32),
            pltpu.SemaphoreType.DMA((8,)),
            pltpu.SemaphoreType.DMA((n_links,)),
            pltpu.SemaphoreType.DMA((n_links,)),
        ],
        cost_estimate=pl.CostEstimate(
            flops=60 * 10**9, bytes_accessed=100 * 10**6, transcendentals=0
        ),
        compiler_params=pltpu.CompilerParams(
            collective_id=0, has_side_effects=True, vmem_limit_bytes=60 * 2**20
        ),
    )(
        a_own, a_oth, d_own, d_oth, mine, other, cond, scale.reshape(1, -1), tops,
        fc_bounds, fc_own, fc_code, w_qkv, tokens, mid_grad, z_own, z_oth, o_own, o_oth, ada,
    )


def after(value, *others):
    return lax.optimization_barrier((value,) + others)[0]


TOP = 32768.0


def fast_body(
    latent_tokens,
    conditioning,
    out_grad,
    qkv_weight,
    qkv_bias,
    proj_weight,
    proj_bias,
    first_layer_weight,
    fc1_bias,
    fc2_weight,
    second_layer_bias,
    ada_weight,
    ada_bias,
):
    n_dp = lax.axis_size("dp")
    n_z = n_dp // 4
    me = lax.axis_index("dp")
    side = lax.axis_index("tensor")
    core, at_x, at_z = me % 2, (me // 2) % 2, me // 4
    rows, width_full = latent_tokens.shape
    block, _, width = qkv_weight.shape
    heads = width // HEAD_DIM
    pad = -(-width // LANES) * LANES

    def swap(values):
        return lax.ppermute(values, "tensor", [(0, 1), (1, 0)])

    def flip(values, bit):
        return lax.ppermute(values, "dp", [(i, i ^ bit) for i in range(n_dp)])

    def shift(values, step):
        return lax.ppermute(values, "dp", [(i, (i + 4 * step) % n_dp) for i in range(n_dp)])

    def place(pieces, spots):
        out = jnp.zeros((len(pieces),) + pieces[0].shape, pieces[0].dtype)
        for piece, spot in zip(pieces, spots):
            out = lax.dynamic_update_index_in_dim(out, piece, spot, 0)
        return out

    def pair(mine, other, bit):
        return jnp.where(bit == 0, jnp.stack([mine, other]), jnp.stack([other, mine]))

    def along_z(values):
        pieces = [values] + [shift(values, s) for s in range(1, n_z)]
        return place(pieces, [(at_z - s) % n_z for s in range(n_z)])

    def in_order(both, shape):
        both = both.reshape((2, 2, n_z) + shape)
        return jnp.transpose(both, (2, 1, 0) + tuple(range(3, both.ndim))).reshape((n_dp,) + shape)

    def gather(values):
        lines = along_z(values)
        planes = place([lines, flip(lines, 2)], [at_x, 1 - at_x])
        both = place([planes, flip(planes, 1)], [core, 1 - core])
        return in_order(both, values.shape)

    def pick(array, spot, axis):
        return lax.dynamic_index_in_dim(array, spot, axis, keepdims=False)

    def scatter_sum(values):
        parts = values.reshape((n_z, 2, 2) + values.shape[1:])
        parts = pick(parts, core, 2) + flip(pick(parts, 1 - core, 2), 1)
        parts = pick(parts, at_x, 1) + flip(pick(parts, 1 - at_x, 1), 2)
        total = pick(parts, at_z, 0)
        for s in range(1, n_z):
            total = total + shift(pick(parts, (at_z + s) % n_z, 0), s)
        return total

    def narrow(part, bound):
        return (part * (TOP / bound)).astype(jnp.float16)

    def wide(part, bound):
        return part.astype(f32) * (bound * (1.0 / TOP))

    def biggest_over_dp(values):
        values = jnp.maximum(values, flip(values, 1))
        values = jnp.maximum(values, flip(values, 2))
        others = [shift(values, s) for s in range(1, n_z)]
        return functools.reduce(jnp.maximum, others, values)

    def total_over_dp(values):
        values = values + flip(values, 1)
        values = values + flip(values, 2)
        return jnp.sum(along_z(values), axis=0)

    def halves(mine, other, axis):
        first = jnp.where(side == 0, mine, other)
        second = jnp.where(side == 0, other, mine)
        return jnp.concatenate([first, second], axis=axis)

    def pad_lanes(values):
        return jnp.pad(values, [(0, 0)] * (values.ndim - 1) + [(0, pad - width)])

    def biggest(*pieces):
        return functools.reduce(jnp.maximum, [jnp.max(jnp.abs(v.astype(f32))) for v in pieces])

    def full_weight(shard):
        return lax.all_gather(shard, "dp", axis=0, tiled=True)

    first = [
        pad_lanes(qkv_weight.astype(bf16)).reshape(block, 3 * pad),
        pad_lanes(proj_weight.astype(bf16).T),
    ]
    w_first = full_weight(jnp.concatenate(first, axis=1))
    w_qkv, w_proj = w_first[:, : 3 * pad], w_first[:, 3 * pad :]
    second = [first_layer_weight.astype(bf16), fc2_weight.astype(bf16).T]
    w_second = full_weight(jnp.concatenate(second, axis=1))
    hidden = first_layer_weight.shape[1]

    tokens = float(n_dp * SEQ)
    tiny = 1e-30
    silu_cond, silu_pull = jax.vjp(jax.nn.silu, conditioning)
    cond_tiles = lax.reduce_precision(silu_cond, 8, 7).reshape(-1, LANES)
    ada = ada_weight.astype(bf16)
    a_own, a_oth, g_own, mods, tops, cond_mine, g_sums = open_part(
        cond_tiles, pad_lanes(ada).reshape(block, 6 * pad),
        pad_lanes(ada_bias).reshape(-1, LANES), latent_tokens, out_grad, width,
    )
    shift_one, scale_one, gate_one, shift_two, scale_two, gate_two = [mods[j] for j in range(6)]
    g_oth = swap(g_own)

    norm = 1.01 * width_full**0.5
    g_bound, m_norm = tops[0, 0] * 1.01, (tops[1, 0] + 1.0) * norm
    act_bound = m_norm * (0.1875 * norm) + 3.0
    gp_bound = g_bound * (1.2 * 0.09375 * width_full)
    fc2_bound = g_bound * act_bound * (1.01 * tokens) + tiny
    fc1_bound = m_norm * gp_bound * (1.01 * tokens) + tiny
    v_bound = (biggest(scale_one) + biggest(shift_one) + 1.0) * (norm * 0.1875 * norm) + 1.25
    p_bound = v_bound * (1.01 * 0.75 * width)

    bias = pad_lanes(jnp.stack([qkv_bias[0], jnp.zeros_like(qkv_bias[0]), qkv_bias[1]]))
    bias = bias.reshape(3 * pad)
    qkv_own = (nn(a_own, w_qkv) + bias).astype(bf16)
    qkv_oth = (nn(a_oth, w_qkv) + bias).astype(bf16)
    o_oth, lse_oth = attend(qkv_oth, qkv_own, qkv_oth, heads, pad)
    p_send = narrow(nt(o_oth, w_proj), p_bound)
    part_oth = wide(swap(p_send), p_bound)
    o_own, lse_own = attend(after(qkv_own, p_send), qkv_own, qkv_oth, heads, pad)
    branch_one = nt(o_own, w_proj) + part_oth + proj_bias
    middle = latent_tokens + gate_one * branch_one
    normed_two, rscale_two = normalize(middle)

    m_own = low(normed_two * (1.0 + scale_two) + shift_two)
    m_oth = swap(m_own)
    hidden_bias = fc1_bias.reshape(1, -1)
    act_own, gp_own, h_own, b_own = feed(m_own, g_own, w_second, hidden_bias, f32)
    act_oth, gp_oth, h_send, b_send = feed(
        m_oth, after(g_oth, m_own), w_second, hidden_bias, bf16
    )
    fc_bounds = jnp.broadcast_to(jnp.pad(jnp.stack([fc2_bound, fc1_bound]), (0, 6))[:, None], (8, LANES))
    (
        mid_grad, z_own, z_oth, go_own, go_oth, turned, fc1_sums,
        fc2_own, fc2_code, fc1_mine, fc1_code,
    ) = middle_part(
        h_send, scale_two, gate_one, fc_bounds, g_own, g_oth, m_own, m_oth, act_own, act_oth,
        gp_own, gp_oth, h_own, middle, out_grad, branch_one, w_proj, block,
    )
    ends = jnp.stack([biggest(a_own, a_oth), biggest(z_own, z_oth) * biggest(o_own, o_oth)])
    ends = jnp.broadcast_to(jnp.pad(ends, (0, 6))[:, None], (8, LANES))
    d_own, d_oth, b_oth, grad_fc2, fc1_own, fc1_code = attend_back(
        qkv_own, qkv_oth, go_own, go_oth, lse_own, lse_oth, fc_bounds, fc2_own, b_send,
        fc2_code, fc1_code, fc1_mine, heads, pad,
    )
    branch_two = b_own + b_oth.astype(f32) + second_layer_bias
    layer_out = middle + gate_two * branch_two

    sums = functools.partial(jnp.sum, axis=0)
    empty = jnp.zeros((2, width_full), f32)
    mods_sums = jnp.stack([turned[0], turned[1], turned[2], sums(out_grad * branch_two)])
    mods_sums = jnp.concatenate([empty, mods_sums]).reshape(6, 2, width)
    apart = jnp.concatenate([jnp.zeros((2, width), f32), fc1_sums[0].reshape(-1, width)])
    shared = jnp.stack([turned[3], g_sums[0]]).reshape(-1, width)
    mine = jnp.concatenate([pick(mods_sums, side, 1), apart, shared])
    other = jnp.concatenate([pick(mods_sums, 1 - side, 1), apart, shared])
    ada = jnp.transpose(ada, (1, 0, 2))
    tokens_grad, grads, grad_ada, totals, cond_row, grad_fc1 = close(
        a_own, a_oth, d_own, d_oth, mine, other, cond_mine,
        scale_one, ends, fc_bounds, fc1_own, fc1_code, w_qkv, latent_tokens, mid_grad, z_own, z_oth, o_own, o_oth, ada, shared.shape[0],
    )
    grad_qkv = jnp.transpose(grads[:3, :, :width], (1, 0, 2))
    grad_proj = grads[3, :, :width].T
    conditioning_grad = silu_pull(cond_row.reshape(1, width_full))[0]
    fc1_rows = hidden // width
    qkv_bias_grad = totals[6:8]
    fc1_bias_grad = totals[8 : 8 + fc1_rows].reshape(hidden)
    proj_bias_grad, fc2_bias_grad = totals[8 + fc1_rows :].reshape(2, width_full)
    grad_ada_bias = totals[:6]
    grad_ada = jnp.transpose(grad_ada, (1, 0, 2))
    grad_fc2 = grad_fc2.T
    return (
        layer_out,
        tokens_grad,
        conditioning_grad,
        grad_qkv,
        qkv_bias_grad,
        grad_proj,
        proj_bias_grad,
        grad_fc1,
        fc1_bias_grad,
        grad_fc2,
        fc2_bias_grad,
        grad_ada,
        grad_ada_bias,
    )


def solution(mesh):
    in_specs = (
        P(("dp", "tensor"), None),
        P("dp", None),
        P(("dp", "tensor"), None),
        P("dp", None, "tensor"),
        P(None, "tensor"),
        P("tensor", "dp"),
        P(),
        P("dp", "tensor"),
        P("tensor"),
        P("tensor", "dp"),
        P(),
        P("dp", None, "tensor"),
        P(None, "tensor"),
    )
    out_specs = (
        P(("dp", "tensor"), None),
        P(("dp", "tensor"), None),
        P("dp", None),
        P("dp", None, "tensor"),
        P(None, "tensor"),
        P("tensor", "dp"),
        P(),
        P("dp", "tensor"),
        P("tensor"),
        P("tensor", "dp"),
        P(),
        P("dp", None, "tensor"),
        P(None, "tensor"),
    )
    body = fast_body if fits(mesh) else general_body
    return jax.shard_map(body, mesh=mesh, in_specs=in_specs, out_specs=out_specs, check_vma=False)
```

```python
import functools

import jax
import jax.numpy as jnp
from jax import lax
from jax.experimental import pallas as pl
from jax.experimental.pallas import tpu as pltpu
from jax.sharding import PartitionSpec as P

HEAD_DIM = 72
SEQ = 1024


highest_precision_mode = lax.Precision.HIGHEST
epsilon = 1e-06


def gelu_tanh(values):
    return jax.nn.gelu(values, approximate=True)


def normalize(values):
    center = values - jnp.mean(values, axis=-1, keepdims=True)
    scaled = lax.rsqrt(jnp.mean(center * center, axis=-1, keepdims=True) + epsilon)
    return (center * scaled, scaled)


def norm_back(grad, normed, scaled):
    first = jnp.mean(grad, axis=-1, keepdims=True)
    second = jnp.mean(grad * normed, axis=-1, keepdims=True)
    return (grad - first - normed * second) * scaled


def general_body(
    latent_tokens,
    conditioning,
    out_grad,
    qkv_weight,
    qkv_bias,
    proj_weight,
    proj_bias,
    first_layer_weight,
    fc1_bias,
    fc2_weight,
    second_layer_bias,
    ada_weight,
    ada_bias,
):

    def fetch():
        return (
            lax.all_gather(qkv_weight.astype(jnp.bfloat16), "dp", axis=0, tiled=True),
            lax.all_gather(proj_weight.astype(jnp.bfloat16), "dp", axis=1, tiled=True),
            lax.all_gather(first_layer_weight.astype(jnp.bfloat16), "dp", axis=0, tiled=True),
            lax.all_gather(fc2_weight.astype(jnp.bfloat16), "dp", axis=1, tiled=True),
            lax.all_gather(ada_weight.astype(jnp.bfloat16), "dp", axis=0, tiled=True),
        )

    w_qkv, w_proj, w_fc1, w_fc2, w_ada = fetch()
    tok_rows, width_full = latent_tokens.shape
    latents = conditioning.shape[0]
    group_rows = tok_rows * lax.axis_size("tensor")
    width = w_qkv.shape[2]
    heads_local = width // HEAD_DIM
    factor = HEAD_DIM ** (-0.5)
    silu_cond, silu_pull = jax.vjp(jax.nn.silu, conditioning)
    cond_low = silu_cond.astype(jnp.bfloat16)
    mod_part = (
        jnp.einsum("ld,dkf->lkf", cond_low, w_ada, preferred_element_type=jnp.float32) + ada_bias
    )
    modulation_values = lax.all_gather(mod_part, "tensor", axis=2, tiled=True)
    span = min(tok_rows, SEQ)
    block_count = tok_rows // span
    first_row = lax.axis_index("tensor") * tok_rows
    block_latent = (first_row + jnp.arange(block_count, dtype=jnp.int32) * span) // SEQ
    select_helper = (block_latent[:, None] == jnp.arange(latents, dtype=jnp.int32)[None, :]).astype(
        jnp.float32
    )
    block_modulation_terms = jnp.einsum(
        "pe,egt->pgt", select_helper, modulation_values, precision=highest_precision_mode
    )

    def spread(values):
        return jnp.broadcast_to(values[:, None, :], (block_count, span, width_full)).reshape(
            tok_rows, width_full
        )

    def per_latent(values):
        sums = jnp.sum(values.reshape(block_count, span, width_full), axis=1)
        return jnp.einsum("bl,bd->ld", select_helper, sums, precision=highest_precision_mode)

    shift_one = spread(block_modulation_terms[:, 0])
    scale_one = spread(block_modulation_terms[:, 1])
    gate_one = spread(block_modulation_terms[:, 2])
    shift_two = spread(block_modulation_terms[:, 3])
    scale_two = spread(block_modulation_terms[:, 4])
    gate_two = spread(block_modulation_terms[:, 5])
    normed_one, rscale_one = normalize(latent_tokens)
    attn_input = (normed_one * (1.0 + scale_one) + shift_one).astype(jnp.bfloat16)
    qkv_shift = jnp.stack([qkv_bias[0], jnp.zeros_like(qkv_bias[0]), qkv_bias[1]])
    piece = lax.all_gather(attn_input, "tensor", axis=0, tiled=True)
    rows_buf = piece
    made = jnp.einsum("rd,dkf->rkf", piece, w_qkv, preferred_element_type=jnp.float32) + qkv_shift
    made_buf = made.astype(jnp.bfloat16)
    attn_rows = rows_buf
    qkv_all = made_buf
    qkv_latent = qkv_all.reshape(group_rows // SEQ, SEQ, 3, heads_local, HEAD_DIM)

    def attend(block):
        query, keys, values = (block[:, 0], block[:, 1], block[:, 2])
        scores = (
            jnp.einsum("qhd,khd->hqk", query, keys, preferred_element_type=jnp.float32) * factor
        )
        peak = jnp.max(scores, axis=-1, keepdims=True)
        expo = jnp.exp(scores - peak)
        total = jnp.sum(expo, axis=-1, keepdims=True)
        probs = (expo / total).astype(jnp.bfloat16)
        result = jnp.einsum("hqk,khd->qhd", probs, values, preferred_element_type=jnp.float32)
        return (result.astype(jnp.bfloat16), peak[..., 0] + jnp.log(total[..., 0]))

    attn_low, logsum = lax.map(attend, qkv_latent)
    attn_low = attn_low.reshape(group_rows, width)
    rows = attn_low
    branch_one = (
        lax.psum_scatter(
            jnp.dot(rows, w_proj, preferred_element_type=jnp.float32),
            "tensor",
            scatter_dimension=0,
            tiled=True,
        )
        + proj_bias
    )
    middle = latent_tokens + gate_one * branch_one
    normed_two, rscale_two = normalize(middle)
    mlp_input = (normed_two * (1.0 + scale_two) + shift_two).astype(jnp.bfloat16)
    piece = lax.all_gather(mlp_input, "tensor", axis=0, tiled=True)
    rows_buf = piece
    made = jnp.dot(piece, w_fc1, preferred_element_type=jnp.float32) + fc1_bias
    made_buf = made
    act, gelu_pull = jax.vjp(gelu_tanh, made_buf)
    act_low = act.astype(jnp.bfloat16)
    rows = act_low
    branch_two = (
        lax.psum_scatter(
            jnp.dot(rows, w_fc2, preferred_element_type=jnp.float32).astype(jnp.bfloat16),
            "tensor",
            scatter_dimension=0,
            tiled=True,
        ).astype(jnp.float32)
        + second_layer_bias
    )
    layer_out = middle + gate_two * branch_two
    w_qkv, w_proj, w_fc1, w_fc2, w_ada = fetch()
    d_gate_two = per_latent(out_grad * branch_two)
    grad_m = (gate_two * out_grad).astype(jnp.bfloat16)
    fc2_bias_part = jnp.sum(grad_m.astype(jnp.float32), axis=0)
    piece = lax.all_gather(grad_m, "tensor", axis=0, tiled=True)
    made = jnp.einsum("rd,fd->rf", piece, w_fc2, preferred_element_type=jnp.float32)
    act_buf = made
    weight_acc = jnp.einsum("rf,rd->fd", act_low, piece, preferred_element_type=jnp.float32)
    grad_fc2 = weight_acc
    grad_pre = gelu_pull(act_buf)[0].astype(jnp.bfloat16)
    fc1_bias_part = jnp.sum(grad_pre.astype(jnp.float32), axis=0)
    grad_fc1 = jnp.einsum("rd,rf->df", rows_buf, grad_pre, preferred_element_type=jnp.float32)
    rows = grad_pre
    grad_h_two = lax.psum_scatter(
        jnp.einsum("rf,df->rd", rows, w_fc1, preferred_element_type=jnp.float32),
        "tensor",
        scatter_dimension=0,
        tiled=True,
    )
    d_shift_two = per_latent(grad_h_two)
    d_scale_two = per_latent(grad_h_two * normed_two)
    grad_mid = out_grad + norm_back(grad_h_two * (1.0 + scale_two), normed_two, rscale_two)
    d_gate_one = per_latent(grad_mid * branch_one)
    grad_z = (gate_one * grad_mid).astype(jnp.bfloat16)
    proj_bias_part = jnp.sum(grad_z.astype(jnp.float32), axis=0)
    piece = lax.all_gather(grad_z, "tensor", axis=0, tiled=True)
    made = jnp.einsum("rd,fd->rf", piece, w_proj, preferred_element_type=jnp.float32)
    weight_acc = jnp.einsum("rf,rd->fd", attn_low, piece, preferred_element_type=jnp.float32)
    grad_attn_low = made.astype(jnp.bfloat16).reshape(group_rows // SEQ, SEQ, heads_local, HEAD_DIM)

    def attend_back(block):
        packed, grad_o, lse = block
        query, keys, values = (packed[:, 0], packed[:, 1], packed[:, 2])
        scores = (
            jnp.einsum("qhd,khd->hqk", query, keys, preferred_element_type=jnp.float32) * factor
        )
        probs = jnp.exp(scores - lse[..., None])
        probs_low = probs.astype(jnp.bfloat16)
        grad_p = jnp.einsum("qhd,khd->hqk", grad_o, values, preferred_element_type=jnp.float32)
        grad_v = jnp.einsum("hqk,qhd->khd", probs_low, grad_o, preferred_element_type=jnp.float32)
        delta = jnp.sum(grad_p * probs, axis=-1, keepdims=True)
        grad_s = (probs * (grad_p - delta)).astype(jnp.bfloat16)
        grad_q = (
            jnp.einsum("hqk,khd->qhd", grad_s, keys, preferred_element_type=jnp.float32) * factor
        )
        grad_k = (
            jnp.einsum("hqk,qhd->khd", grad_s, query, preferred_element_type=jnp.float32) * factor
        )
        return jnp.stack([grad_q, grad_k, grad_v], axis=1).astype(jnp.bfloat16)

    grad_qkv = lax.map(attend_back, (qkv_latent, grad_attn_low, logsum)).reshape(
        group_rows, 3, width
    )
    qkv_bias_part = jnp.sum(grad_qkv.astype(jnp.float32), axis=0)
    grad_qkv_weight = jnp.einsum(
        "rd,rkf->dkf", attn_rows, grad_qkv, preferred_element_type=jnp.float32
    )
    rows = grad_qkv
    grad_h_one = lax.psum_scatter(
        jnp.einsum("rkf,dkf->rd", rows, w_qkv, preferred_element_type=jnp.float32),
        "tensor",
        scatter_dimension=0,
        tiled=True,
    )
    d_shift_one = per_latent(grad_h_one)
    d_scale_one = per_latent(grad_h_one * normed_one)
    tokens_grad = grad_mid + norm_back(grad_h_one * (1.0 + scale_one), normed_one, rscale_one)
    grad_mods = jnp.stack(
        [d_shift_one, d_scale_one, d_gate_one, d_shift_two, d_scale_two, d_gate_two], axis=1
    )
    mods_share = lax.psum_scatter(grad_mods, "tensor", scatter_dimension=2, tiled=True)
    grad_ada = jnp.einsum(
        "ld,lkf->dkf", cond_low.astype(jnp.float32), mods_share, precision=highest_precision_mode
    )
    grad_ada_bias = jnp.sum(mods_share, axis=0)
    cond_part = jnp.einsum(
        "lkf,dkf->ld", mods_share, w_ada.astype(jnp.float32), precision=highest_precision_mode
    )
    tensor_totals = lax.psum((cond_part, proj_bias_part, fc2_bias_part), "tensor")
    conditioning_grad = silu_pull(tensor_totals[0])[0]
    weight_totals = (
        lax.psum_scatter(grad_qkv_weight, "dp", scatter_dimension=0, tiled=True),
        lax.psum_scatter(weight_acc, "dp", scatter_dimension=1, tiled=True),
        lax.psum_scatter(grad_fc1, "dp", scatter_dimension=0, tiled=True),
        lax.psum_scatter(grad_fc2, "dp", scatter_dimension=1, tiled=True),
        lax.psum_scatter(grad_ada, "dp", scatter_dimension=0, tiled=True),
    )
    qkv_bias_pair = jnp.stack([qkv_bias_part[0], qkv_bias_part[2]])
    bias_totals = lax.psum(
        (qkv_bias_pair, tensor_totals[1], fc1_bias_part, tensor_totals[2], grad_ada_bias), "dp"
    )
    return (
        layer_out,
        tokens_grad,
        conditioning_grad,
        weight_totals[0],
        bias_totals[0],
        weight_totals[1],
        bias_totals[1],
        weight_totals[2],
        bias_totals[2],
        weight_totals[3],
        bias_totals[3],
        weight_totals[4],
        bias_totals[4],
    )


LANES = 128
LOG2E = 1.4426950408889634
f32 = jnp.float32
bf16 = jnp.bfloat16


def fits(mesh):
    return mesh.shape["tensor"] == 2 and mesh.shape["dp"] == 16


def low(values):
    return lax.reduce_precision(values, 8, 7).astype(bf16)


def nn(a, b):
    return lax.dot_general(a, b, (((1,), (0,)), ((), ())), preferred_element_type=f32)


def nt(a, b):
    return lax.dot_general(a, b, (((1,), (1,)), ((), ())), preferred_element_type=f32)


def tn(a, b):
    return lax.dot_general(a, b, (((0,), (0,)), ((), ())), preferred_element_type=f32)


def window(head):
    start = pl.multiple_of(((head * HEAD_DIM) // LANES) * LANES, LANES)
    return start, head * HEAD_DIM - start


def lane_mask(shape, first):
    lane = lax.broadcasted_iota(jnp.int32, shape, 1)
    return (lane >= first) & (lane < first + HEAD_DIM)


def attend_kernel(q_ref, own_ref, oth_ref, o_ref, lse_ref, *, heads, block, pad, scale):
    rows = q_ref.shape[0]
    factor = scale * LOG2E
    o_ref[...] = jnp.zeros_like(o_ref)

    def one_head(h, carry):
        at, first = window(h)

        def one_block(i, inner):
            r = pl.ds(pl.multiple_of(i * block, block), block)
            mask = lane_mask((block, 2 * LANES), first)
            q = q_ref[r, pl.ds(at, 2 * LANES)]
            q = jnp.where(mask, q, jnp.zeros_like(q))
            scores = [nt(ref[:, pl.ds(pad + at, 2 * LANES)], q) for ref in (own_ref, oth_ref)]
            peak = functools.reduce(
                jnp.maximum, [jnp.max(s, axis=0, keepdims=True) for s in scores]
            )
            peak = peak * factor
            expo = [jnp.exp2(s * factor - peak) for s in scores]
            total = sum(jnp.sum(e, axis=0, keepdims=True) for e in expo)
            inverse = 1.0 / total
            out = sum(
                tn(ref[:, pl.ds(2 * pad + at, 2 * LANES)], (e * inverse).astype(bf16))
                for ref, e in zip((own_ref, oth_ref), expo)
            ).T
            o_ref[r, pl.ds(at, 2 * LANES)] = jnp.where(
                mask, out.astype(bf16), o_ref[r, pl.ds(at, 2 * LANES)]
            )
            lse_ref[pl.ds(h, 1), r] = peak + jnp.log2(total)
            return inner

        return lax.fori_loop(0, rows // block, one_block, carry)

    lax.fori_loop(0, heads, one_head, 0)


def attend(queries, own, oth, heads, pad):
    rows = queries.shape[0]
    flops = 4 * heads * rows * 2 * rows * 2 * LANES
    return pl.pallas_call(
        functools.partial(
            attend_kernel, heads=heads, block=min(rows, 512), pad=pad, scale=HEAD_DIM**-0.5
        ),
        out_shape=(
            jax.ShapeDtypeStruct((rows, pad), bf16),
            jax.ShapeDtypeStruct((heads, rows), f32),
        ),
        cost_estimate=pl.CostEstimate(
            flops=4 * flops, bytes_accessed=8 * rows * pad * 2, transcendentals=heads * rows * rows * 2
        ),
        compiler_params=pltpu.CompilerParams(vmem_limit_bytes=40 * 2**20),
    )(queries, own, oth)


GELU = 0.7978845608028654


def feed_kernel(
    m_ref, g_ref, w1_ref, w2_ref, b_ref, act_ref, gp_ref, h_ref, out_ref, hacc_ref, oacc_ref, *, steps
):
    i = pl.program_id(0)

    @pl.when(i == 0)
    def _():
        hacc_ref[...] = jnp.zeros_like(hacc_ref)
        oacc_ref[...] = jnp.zeros_like(oacc_ref)

    pre = nn(m_ref[...], w1_ref[...]) + b_ref[...]
    grad_act = nn(g_ref[...], w2_ref[...])
    square = pre * pre
    gate = 1.0 / (1.0 + jnp.exp((-2.0 * GELU) * pre * (1.0 + 0.044715 * square)))
    act = (pre * gate).astype(bf16)
    act_ref[...] = act
    slope = gate + pre * gate * (1.0 - gate) * ((2.0 * GELU) * (1.0 + (3.0 * 0.044715) * square))
    grad_pre = (grad_act * slope).astype(bf16)
    gp_ref[...] = grad_pre
    hacc_ref[...] += nt(grad_pre, w1_ref[...])
    oacc_ref[...] += nt(act, w2_ref[...])

    @pl.when(i == steps - 1)
    def _():
        h_ref[...] = hacc_ref[...].astype(h_ref.dtype)
        out_ref[...] = oacc_ref[...].astype(out_ref.dtype)


def feed(m, g, weights, bias, out_dtype):
    rows, depth = m.shape
    hidden = weights.shape[1] // 2
    steps = 3 if hidden % (3 * LANES) == 0 else 1
    chunk = hidden // steps
    whole = pl.BlockSpec((rows, depth), lambda i: (0, 0))
    first = pl.BlockSpec((depth, chunk), lambda i: (0, i))
    second = pl.BlockSpec((depth, chunk), lambda i: (0, i + steps))
    tall = pl.BlockSpec((rows, chunk), lambda i: (0, i))
    return pl.pallas_call(
        functools.partial(feed_kernel, steps=steps),
        grid=(steps,),
        in_specs=[whole, whole, first, second, pl.BlockSpec((1, chunk), lambda i: (0, i))],
        out_specs=[tall, tall, whole, whole],
        out_shape=(
            jax.ShapeDtypeStruct((rows, hidden), bf16),
            jax.ShapeDtypeStruct((rows, hidden), bf16),
            jax.ShapeDtypeStruct((rows, depth), out_dtype),
            jax.ShapeDtypeStruct((rows, depth), out_dtype),
        ),
        scratch_shapes=[pltpu.VMEM((rows, depth), f32)] * 2,
        cost_estimate=pl.CostEstimate(
            flops=12 * rows * depth * hidden,
            bytes_accessed=4 * depth * hidden + 8 * rows * depth + 4 * rows * hidden,
            transcendentals=rows * hidden,
        ),
        compiler_params=pltpu.CompilerParams(vmem_limit_bytes=56 * 2**20),
    )(m, g, weights, weights, bias)


def peers(n_dp):
    me, side = lax.axis_index("dp"), lax.axis_index("tensor")
    n_z = n_dp // 4
    z, x, c = me // 4, (me // 2) % 2, me % 2
    across = (me, 1 - side)
    core = (z * 4 + x * 2 + 1 - c, side)
    beside = (z * 4 + (1 - x) * 2 + c, side)
    lines = [(lax.rem(z + s, n_z) * 4 + x * 2 + c, side) for s in range(1, n_z)]
    return (me, z, x, c), across, core, beside, lines


def greet(partners):
    barrier = pltpu.get_barrier_semaphore()
    for partner in partners:
        pl.semaphore_signal(barrier, inc=1, device_id=partner, device_id_type=pl.DeviceIdType.MESH)
    pl.semaphore_wait(barrier, len(partners))


SPAN = 2.0**63
QUARTERS = (SPAN, 1.0, 1.0 / SPAN, 1.0 / SPAN / SPAN)
STEP = 1.0 / 512.0


def encode(values, bound):
    scaled = (values * 2.0**40) * (0.98 * 2.0**23 / bound)
    size = jnp.abs(scaled)
    near = size.astype(bf16).astype(f32)
    rest, step = size - near, near * STEP
    below = jnp.where(rest < -step, QUARTERS[0], QUARTERS[1])
    above = jnp.where(rest < step, QUARTERS[2], QUARTERS[3])
    coded = near * jnp.where(rest < 0.0, below, above)
    coded = jnp.where(near <= 1.0, 0.0, coded)
    return jnp.where(scaled < 0.0, -coded, coded).astype(bf16)


def decode(coded, bound):
    coded = coded.astype(f32)
    size = jnp.abs(coded)
    factors = [(1.0 + (k - 1.5) * STEP) / q for k, q in enumerate(QUARTERS)]
    large = jnp.where(size > SPAN, factors[0], factors[1])
    small = jnp.where(size > 1.0 / SPAN, factors[2], factors[3])
    scaled = coded * jnp.where(size > 1.0, large, small)
    return (scaled * 2.0**-40) * (bound * (2.0**-23 / 0.98))


def linker(send_sem, recv_sem):
    def link(source, target, to, k):
        return pltpu.make_async_remote_copy(
            src_ref=source, dst_ref=target, send_sem=send_sem.at[k], recv_sem=recv_sem.at[k],
            device_id=to, device_id_type=pl.DeviceIdType.MESH,
        )

    return link


def turn_over(reads, turned_ref, n_z, block):
    for j, read in enumerate(reads):
        turned = read().astype(f32).T
        rows = turned.shape[1]
        for z in range(n_z):
            for x in range(2):
                for c in range(2):
                    b = (z * 2 + x) * 2 + c
                    at = pl.ds((x * n_z + z) * block, block)
                    turned_ref[c, at, pl.ds(j * rows, rows)] = turned[
                        b * block : (b + 1) * block
                    ].astype(bf16)


def open_kernel(
    cond_ref, ada_ref, bias_ref, x_ref, out_ref,
    aown_ref, gown_ref, noth_ref, mods_ref, top_ref, mine_ref, gsum_ref,
    cond_all, part_ref, cgot_ref, xgot_ref, zgot_ref, half_ref, other_ref, normed_ref, nown_ref,
    send_sem, recv_sem,
    *, n_dp, n_mods, width,
):
    (me, z, x, c), across, core, beside, lines = peers(n_dp)
    n_z = n_dp // 4
    side = lax.axis_index("tensor")
    link = linker(send_sem, recv_sem)
    rows, depth = x_ref.shape
    block = ada_ref.shape[0]
    tile = min(rows, 128)
    per_mod = part_ref.shape[3] // n_mods
    greet([across, core, beside] + lines)

    def step(copies, beside_work=None):
        for copy in copies:
            copy.start()
        if beside_work is not None:
            beside_work()
        for copy in copies:
            copy.wait()

    def loop(body):
        def one(i, carry):
            body(pl.ds(pl.multiple_of(i * tile, tile), tile))
            return carry

        lax.fori_loop(0, rows // tile, one, 0)

    def norm_tile(r):
        normed = normalize(x_ref[r, :])[0]
        normed_ref[r, :] = normed
        nown_ref[r, :] = normed.astype(bf16)

    cond_all[z, x, c] = cond_ref[...]
    mine = cond_all.at[z, x, c]
    step([link(mine, mine, core, 0)], lambda: loop(norm_tile))
    normed_link = link(nown_ref, noth_ref, across, 3 + 2 * n_z)
    normed_link.start()
    mine = cond_all.at[z, x]
    step([link(mine, mine, beside, 1)])
    mine = cond_all.at[z]
    step([link(mine, mine, to, 2 + s) for s, to in enumerate(lines)])
    everyone = cond_all[...].reshape(n_dp, depth // LANES, LANES)
    flat = jnp.concatenate([everyone[:, i, :] for i in range(depth // LANES)], axis=1)
    feature = lax.broadcasted_iota(jnp.int32, (depth, block), 0)
    column = lax.broadcasted_iota(jnp.int32, (depth, block), 1)
    chosen = nn(flat.astype(bf16), (feature == column + me * block).astype(bf16))
    mine_ref[...] = chosen

    made = nn(chosen.astype(bf16), ada_ref[...])
    for g in range(part_ref.shape[3]):
        part_ref[:, :, :, g, :] = made[:, g * LANES : (g + 1) * LANES].reshape(n_z, 2, 2, LANES)
    at = 1 + n_z
    step([link(part_ref.at[:, :, 1 - c], cgot_ref, core, at)])
    cgot_ref[...] += part_ref[:, :, c]
    step([link(cgot_ref.at[:, 1 - x], xgot_ref, beside, at + 1)])
    xgot_ref[...] += cgot_ref[:, x]
    step(
        [
            link(xgot_ref.at[lax.rem(z + s + 1, n_z)], zgot_ref.at[s], to, at + 2 + s)
            for s, to in enumerate(lines)
        ]
    )
    total = xgot_ref[z] + bias_ref[...]
    for s in range(n_z - 1):
        total += zgot_ref[s]
    half_ref[...] = total
    at += n_z + 1
    step([link(half_ref, other_ref, across, at)])
    halves = []
    for ref in (half_ref, other_ref):
        values = ref[...]
        halves.append(
            [
                jnp.concatenate(
                    [values[j * per_mod + i : j * per_mod + i + 1, :] for i in range(per_mod)],
                    axis=1,
                )[:, :width]
                for j in range(n_mods)
            ]
        )
    mods_ref[...] = jnp.zeros_like(mods_ref)
    for j, (own, oth) in enumerate(zip(*halves)):
        first = jnp.where(side == 0, own, oth)
        second = jnp.where(side == 0, oth, own)
        mods_ref[pl.ds(j, 1), :] = jnp.concatenate([first, second], axis=1)

    def input_tile(r):
        made = normed_ref[r, :] * (1.0 + mods_ref[1:2, :]) + mods_ref[0:1, :]
        aown_ref[r, :] = made.astype(bf16)

    loop(input_tile)

    def grad_tile(i, carry):
        r = pl.ds(pl.multiple_of(i * tile, tile), tile)
        made = (mods_ref[5:6, :] * out_ref[r, :]).astype(bf16)
        gown_ref[r, :] = made
        made = made.astype(f32)
        most = jnp.max(jnp.abs(made), axis=0, keepdims=True)
        return carry[0] + jnp.sum(made, axis=0, keepdims=True), jnp.maximum(carry[1], most)

    none = (jnp.zeros((1, depth), f32),) * 2
    g_sum, g_top = lax.fori_loop(0, rows // tile, grad_tile, none)
    gsum_ref[...] = g_sum

    def largest(j):
        return jnp.max(jnp.abs(mods_ref[j : j + 1, :]), axis=1, keepdims=True)

    tops = (
        jnp.max(g_top, axis=1, keepdims=True),
        largest(4) + largest(3),
        largest(1) + largest(0),
    )
    row = lax.broadcasted_iota(jnp.int32, top_ref.shape, 0)
    best = jnp.zeros(top_ref.shape, f32)
    for j, top in enumerate(tops):
        best = jnp.where(row == j, top, best)
    top_ref[...] = best
    normed_link.wait()


def open_part(cond, ada, bias, tokens, out_grad, width):
    n_dp = lax.axis_size("dp")
    n_z = n_dp // 4
    rows, depth = tokens.shape
    block = ada.shape[0]
    groups = bias.shape[0]
    n_links = 4 + 2 * n_z
    vmem = pl.BlockSpec(memory_space=pltpu.VMEM)
    return pl.pallas_call(
        functools.partial(open_kernel, n_dp=n_dp, n_mods=6, width=width),
        out_shape=(
            jax.ShapeDtypeStruct((rows, depth), bf16),
            jax.ShapeDtypeStruct((rows, depth), bf16),
            jax.ShapeDtypeStruct((rows, depth), bf16),
            jax.ShapeDtypeStruct((8, depth), f32),
            jax.ShapeDtypeStruct((8, LANES), f32),
            jax.ShapeDtypeStruct((n_dp, block), f32),
            jax.ShapeDtypeStruct((1, depth), f32),
        ),
        in_specs=[vmem] * 5,
        out_specs=[vmem] * 7,
        scratch_shapes=[
            pltpu.VMEM((n_z, 2, 2, depth // LANES, LANES), f32),
            pltpu.VMEM((n_z, 2, 2, groups, LANES), f32),
            pltpu.VMEM((n_z, 2, groups, LANES), f32),
            pltpu.VMEM((n_z, groups, LANES), f32),
            pltpu.VMEM((n_z - 1, groups, LANES), f32),
            pltpu.VMEM((groups, LANES), f32),
            pltpu.VMEM((groups, LANES), f32),
            pltpu.VMEM((rows, depth), f32),
            pltpu.VMEM((rows, depth), bf16),
            pltpu.SemaphoreType.DMA((n_links,)),
            pltpu.SemaphoreType.DMA((n_links,)),
        ],
        cost_estimate=pl.CostEstimate(
            flops=40 * 10**9, bytes_accessed=20 * 10**6, transcendentals=0
        ),
        compiler_params=pltpu.CompilerParams(
            collective_id=3, has_side_effects=True, vmem_limit_bytes=32 * 2**20
        ),
    )(cond, ada, bias, tokens, out_grad)


def middle_kernel(
    hsend_ref, scale_ref, gate_ref, top_ref,
    gown_any, goth_any, mown_any, moth_any, aown_any, aoth_any, pown_any, poth_any,
    hown_any, mid_any, out_any, branch_any, proj_any,
    grad_ref, zown_ref, zoth_ref, goown_ref, gooth_ref, sum_ref, colsum_ref,
    own2_ref, code2_ref, mine1_ref, code1_ref, bound_ref,
    left_ref, right_ref, hown_ref, mid_ref, branch_ref, proj_ref, turned_ref,
    csend_ref, cgot_ref, mine2_ref, xsend_ref, xgot_ref, hgot_ref, zgot_ref, zsend_ref,
    tsend_ref, tgot_ref,
    load_sem, left_sem, right_sem, send_sem, recv_sem,
    *, n_dp, steps, tokens,
):
    (me, z, x, c), across, core, beside, lines = peers(n_dp)
    n_z = n_dp // 4
    rows, depth = hsend_ref.shape
    block, hidden = own2_ref.shape
    chunk = hidden // steps
    tile = min(rows, 128)
    link = linker(send_sem, recv_sem)

    def left_loads(pieces):
        return [
            pltpu.make_async_copy(piece, left_ref.at[j], left_sem.at[j])
            for j, piece in enumerate(pieces)
        ]

    def right_loads(pieces, k):
        at = pl.ds(k * chunk, chunk)
        return [
            pltpu.make_async_copy(piece.at[:, at], right_ref.at[k % 2, j], right_sem.at[k % 2, j])
            for j, piece in enumerate(pieces)
        ]

    loads = [
        pltpu.make_async_copy(source, target, load_sem.at[k])
        for k, (source, target) in enumerate(
            (
                (hown_any, hown_ref),
                (mid_any, mid_ref),
                (out_any, grad_ref),
                (branch_any, branch_ref),
                (proj_any, proj_ref),
            )
        )
    ]

    def start(copies):
        for copy in copies:
            copy.start()

    def wait(copies):
        for copy in copies:
            copy.wait()

    start(left_loads((gown_any, goth_any)))
    for k in range(min(2, steps)):
        start(right_loads((aown_any, aoth_any), k))
    start(loads)
    greet([across, core, beside] + lines)

    first_top = 2 + 3 * steps

    def top_links(k):
        if k < 3:
            return [link(tsend_ref.at[k], tgot_ref.at[k], (across, core, beside)[k], first_top + k)]
        return [
            link(tsend_ref.at[3], tgot_ref.at[3 + s], to, first_top + 3 + s)
            for s, to in enumerate(lines)
        ]

    def raise_top(k):
        if k == 0:
            best = top_ref[...]
        else:
            wait(top_links(k - 1))
            best = jnp.maximum(tsend_ref[k - 1], tgot_ref[k - 1])
        tsend_ref[k] = best
        start(top_links(k))

    def settle_bounds():
        wait(top_links(3))
        best = tsend_ref[3]
        for s in range(n_z - 1):
            best = jnp.maximum(best, tgot_ref[3 + s])
        norm = 1.01 * depth**0.5
        g_bound, m_norm = best[0:1, :] * 1.01, (best[1:2, :] + 1.0) * norm
        act_bound = m_norm * (0.1875 * norm) + 3.0
        gp_bound = g_bound * (1.2 * 0.09375 * depth)
        bound_ref[...] = jnp.zeros_like(bound_ref)
        bound_ref[0:1, :] = g_bound * act_bound * (1.01 * tokens) + 1e-30
        bound_ref[1:2, :] = m_norm * gp_bound * (1.01 * tokens) + 1e-30

    code2_ref[...] = jnp.zeros_like(code2_ref)
    zsend_ref[...] = jnp.zeros_like(zsend_ref)
    raise_top(0)
    half = link(hsend_ref, hgot_ref, across, 0)
    half.start()

    def product(which, slot):
        made = nn(turned_ref[which, :, pl.ds(0, rows)], right_ref[slot, 0])
        made += nn(turned_ref[which, :, pl.ds(rows, rows)], right_ref[slot, 1])
        return made.reshape(csend_ref.shape[1:])

    def core_link(w, k):
        return link(csend_ref.at[k % 2], cgot_ref.at[w, k], core, 2 + w * steps + k)

    def x_link(k):
        return link(xsend_ref.at[k], xgot_ref.at[k], beside, 2 + 2 * steps + k)

    def rounds(w, pieces, use):
        for k in range(steps + 1):
            if k < steps:
                wait(right_loads(pieces, k))
                if k >= 2:
                    core_link(w, k - 2).wait_send()
                csend_ref[k % 2] = product(1 - c, k % 2)
                core_link(w, k).start()
            if w == 0 and k < 2:
                raise_top(k + 2)
            if w == 0 and k == 1:
                settle_bounds()
            if k > 0:
                j = k - 1
                core_link(w, j).wait_recv()
                cgot_ref[w, j] += product(c, j % 2)
                use(j)
                if j + 2 < steps:
                    start(right_loads(pieces, j + 2))
        for k in range(max(steps - 2, 0), steps):
            core_link(w, k).wait_send()

    def use_two(j):
        at = pl.ds(j * chunk, chunk)
        mine2_ref[:, :, at] = cgot_ref[0, j, x]
        away = cgot_ref[0, j, 1 - x].reshape(n_z * block, chunk)
        xsend_ref[j] = encode(away, bound_ref[0:1, 0:1])
        x_link(j).start()

    z_links = [
        link(zsend_ref.at[s], zgot_ref.at[s], to, first_top + n_z + 2 + s)
        for s, to in enumerate(lines)
    ]

    def pass_two(k):
        x_link(k).wait()
        at = pl.ds(k * chunk, chunk)
        came = decode(xgot_ref[k], bound_ref[0:1, 0:1]).reshape(n_z, block, chunk)
        mine2_ref[:, :, at] += came
        own2_ref[:, at] = mine2_ref[z, :, at]
        for s in range(n_z - 1):
            away = encode(mine2_ref[lax.rem(z + s + 1, n_z), :, at], bound_ref[0:1, 0:1])
            if k == 0:
                zsend_ref[s, pl.ds(0, block), :] = away
            else:
                code2_ref[s, pl.ds(0, block), pl.ds((k - 1) * chunk, chunk)] = away
        if k == 0:
            start(z_links)

    def use_one(j):
        if j == min(1, steps - 1):
            pass_two(0)
        at = pl.ds(j * chunk, chunk)
        mine1_ref[:, :, at] = cgot_ref[1, j, x]
        away = cgot_ref[1, j, 1 - x].reshape(n_z * block, chunk)
        code1_ref[:, at] = encode(away, bound_ref[1:2, 0:1])
        ones = jnp.ones((8, rows), bf16)
        colsum_ref[:, at] = nn(ones, right_ref[j % 2, 0]) + nn(ones, right_ref[j % 2, 1])

    wait(left_loads((gown_any, goth_any)))
    turn_over([lambda j=j: left_ref[j] for j in range(2)], turned_ref, n_z, block)
    start(left_loads((mown_any, moth_any)))
    raise_top(1)
    rounds(0, (aown_any, aoth_any), use_two)
    for k in range(min(2, steps)):
        start(right_loads((pown_any, poth_any), k))

    wait(loads)
    half.wait()

    def norm_tile(i, carry):
        r = pl.ds(pl.multiple_of(i * tile, tile), tile)
        h = hown_ref[r, :] + hgot_ref[r, :].astype(f32)
        normed, rscale = normalize(mid_ref[r, :])
        grad = grad_ref[r, :] + norm_back(h * (1.0 + scale_ref[...]), normed, rscale)
        grad_ref[r, :] = grad
        turned = (gate_ref[...] * grad).astype(bf16)
        zown_ref[r, :] = turned
        parts = (grad * branch_ref[r, :], h, h * normed, turned.astype(f32))
        added = tuple(
            total + jnp.sum(part, axis=0, keepdims=True) for total, part in zip(carry, parts)
        )
        most = jnp.max(jnp.abs(turned.astype(f32)), axis=0, keepdims=True)
        return added + (jnp.maximum(carry[4], most),)

    totals = lax.fori_loop(0, rows // tile, norm_tile, (jnp.zeros((1, depth), f32),) * 5)
    turn_link = link(zown_ref, zoth_ref, across, 1)
    turn_link.start()
    sum_ref[...] = jnp.zeros_like(sum_ref)
    for j, total in enumerate(totals):
        sum_ref[pl.ds(j, 1), :] = total

    wait(left_loads((mown_any, moth_any)))
    turn_over([lambda j=j: left_ref[j] for j in range(2)], turned_ref, n_z, block)
    rounds(1, (pown_any, poth_any), use_one)
    goown_ref[...] = nn(zown_ref[...], proj_ref[...]).astype(bf16)

    for k in range(1, steps):
        pass_two(k)
    for s in range(n_z - 1):
        z_links[s].wait()
        came = decode(zgot_ref[s, pl.ds(0, block), :], bound_ref[0:1, 0:1])
        own2_ref[:, pl.ds(0, chunk)] += came
    turn_link.wait()
    gooth_ref[...] = nn(zoth_ref[...], proj_ref[...]).astype(bf16)
    most = jnp.max(jnp.abs(zoth_ref[...].astype(f32)), axis=0, keepdims=True)
    sum_ref[4:5, :] = jnp.maximum(sum_ref[4:5, :], most)


def middle_part(
    h_send, scale, gate, tops, g_own, g_oth, m_own, m_oth, act_own, act_oth, gp_own, gp_oth,
    h_own, middle, out_grad, branch, w_proj, block,
):
    n_dp = lax.axis_size("dp")
    n_z = n_dp // 4
    rows, depth = h_send.shape
    hidden = act_own.shape[1]
    pad = w_proj.shape[1]
    steps = 3 if hidden % (3 * LANES) == 0 else 1
    chunk = hidden // steps
    tall = -(-block // 16) * 16
    vmem = pl.BlockSpec(memory_space=pltpu.VMEM)
    n_links = 2 + 3 * steps + 2 * n_z + 1
    later = max(steps - 1, 1) * chunk
    return pl.pallas_call(
        functools.partial(middle_kernel, n_dp=n_dp, steps=steps, tokens=float(n_dp * SEQ)),
        out_shape=(
            jax.ShapeDtypeStruct((rows, depth), f32),
            jax.ShapeDtypeStruct((rows, depth), bf16),
            jax.ShapeDtypeStruct((rows, depth), bf16),
            jax.ShapeDtypeStruct((rows, pad), bf16),
            jax.ShapeDtypeStruct((rows, pad), bf16),
            jax.ShapeDtypeStruct((8, depth), f32),
            jax.ShapeDtypeStruct((8, hidden), f32),
            jax.ShapeDtypeStruct((block, hidden), f32),
            jax.ShapeDtypeStruct((n_z - 1, tall, later), bf16),
            jax.ShapeDtypeStruct((n_z, block, hidden), f32),
            jax.ShapeDtypeStruct((n_z * block, hidden), bf16),
            jax.ShapeDtypeStruct((8, LANES), f32),
        ),
        in_specs=[vmem] * 4 + [pl.BlockSpec(memory_space=pl.ANY)] * 13,
        out_specs=[vmem] * 12,
        scratch_shapes=[
            pltpu.VMEM((2, rows, depth), bf16),
            pltpu.VMEM((2, 2, rows, chunk), bf16),
            pltpu.VMEM((rows, depth), f32),
            pltpu.VMEM((rows, depth), f32),
            pltpu.VMEM((rows, depth), f32),
            pltpu.VMEM(w_proj.shape, bf16),
            pltpu.VMEM((2, depth // 2, 2 * rows), bf16),
            pltpu.VMEM((2, 2, n_z, block, chunk), f32),
            pltpu.VMEM((2, steps, 2, n_z, block, chunk), f32),
            pltpu.VMEM((n_z, block, hidden), f32),
            pltpu.VMEM((steps, n_z * block, chunk), bf16),
            pltpu.VMEM((steps, n_z * block, chunk), bf16),
            pltpu.VMEM((rows, depth), bf16),
            pltpu.VMEM((n_z - 1, tall, chunk), bf16),
            pltpu.VMEM((n_z - 1, tall, chunk), bf16),
            pltpu.VMEM((4, 8, LANES), f32),
            pltpu.VMEM((n_z + 2, 8, LANES), f32),
            pltpu.SemaphoreType.DMA((5,)),
            pltpu.SemaphoreType.DMA((2,)),
            pltpu.SemaphoreType.DMA((2, 2)),
            pltpu.SemaphoreType.DMA((n_links,)),
            pltpu.SemaphoreType.DMA((n_links,)),
        ],
        cost_estimate=pl.CostEstimate(
            flops=60 * 10**9, bytes_accessed=100 * 10**6, transcendentals=0
        ),
        compiler_params=pltpu.CompilerParams(
            collective_id=1, has_side_effects=True, vmem_limit_bytes=62 * 2**20
        ),
    )(
        h_send, scale.reshape(1, -1), gate.reshape(1, -1), tops, g_own, g_oth, m_own, m_oth,
        act_own, act_oth, gp_own, gp_oth, h_own, middle, out_grad, branch, w_proj,
    )


def attend_back_kernel(
    own_ref, oth_ref, gown_ref, goth_ref, lown_ref, loth_ref, bound_ref, own2_ref,
    out_any, code2_any, code1_any, mine1_any,
    down_ref, doth_ref, branch_ref, total2_ref, own1_ref, next1_ref,
    dk_ref, dv_ref, out_ref, code2_ref, got2_ref, code1_ref, got1_ref, mine1_ref, zsend_ref, zgot_ref,
    load_sem, send_sem, recv_sem,
    *, n_dp, chunk, heads, block, pad, scale,
):
    (me, z, x, c), across, core, beside, lines = peers(n_dp)
    n_z = n_dp // 4
    link = linker(send_sem, recv_sem)
    loads = [
        pltpu.make_async_copy(source, target, load_sem.at[k])
        for k, (source, target) in enumerate(
            (
                (out_any, out_ref),
                (code2_any, code2_ref),
                (code1_any, code1_ref),
                (mine1_any, mine1_ref),
            )
        )
    ]
    for load in loads:
        load.start()
    greet([across, beside] + lines)
    for load in loads:
        load.wait()
    depth, hidden = own1_ref.shape
    first, later = pl.ds(0, chunk), pl.ds(chunk, hidden - chunk)
    branch = link(out_ref, branch_ref, across, 0)
    z_links = [link(code2_ref.at[s], got2_ref.at[s], to, 1 + s) for s, to in enumerate(lines)]
    x_links = [
        link(code1_ref.at[:, at], got1_ref.at[:, at], beside, n_z + k)
        for k, at in enumerate((first, later))
    ]
    next_links = [
        link(zsend_ref.at[s], zgot_ref.at[s], to, n_z + 2 + s) for s, to in enumerate(lines)
    ]
    for one in [branch] + x_links + z_links:
        one.start()
    zsend_ref[...] = jnp.zeros_like(zsend_ref)
    next1_ref[...] = jnp.zeros_like(next1_ref)

    def pass_one(k, at, target):
        x_links[k].wait()
        came = decode(got1_ref[:, at], bound_ref[1:2, 0:1])
        mine1_ref[:, :, at] += came.reshape(n_z, depth, came.shape[1])
        own1_ref[:, at] = mine1_ref[z, :, at]
        for s in range(n_z - 1):
            away = mine1_ref[lax.rem(z + s + 1, n_z), :, at]
            target[s, pl.ds(0, depth), :] = encode(away, bound_ref[1:2, 0:1])

    rows = own_ref.shape[0]
    factor = scale * LOG2E
    down_ref[...] = jnp.zeros_like(down_ref)
    doth_ref[...] = jnp.zeros_like(doth_ref)

    def one_head(h, carry):
        at, first = window(h)
        dk_ref[...] = jnp.zeros_like(dk_ref)
        dv_ref[...] = jnp.zeros_like(dv_ref)
        keys = [ref[:, pl.ds(pad + at, 2 * LANES)] for ref in (own_ref, oth_ref)]
        values = [ref[:, pl.ds(2 * pad + at, 2 * LANES)] for ref in (own_ref, oth_ref)]
        parts = ((own_ref, gown_ref, lown_ref, down_ref), (oth_ref, goth_ref, loth_ref, doth_ref))
        for q_ref, g_ref, l_ref, d_ref in parts:

            def one_block(i, inner):
                r = pl.ds(pl.multiple_of(i * block, block), block)
                mask = lane_mask((block, 2 * LANES), first)
                q = q_ref[r, pl.ds(at, 2 * LANES)]
                q = jnp.where(mask, q, jnp.zeros_like(q))
                g = g_ref[r, pl.ds(at, 2 * LANES)]
                g = jnp.where(mask, g, jnp.zeros_like(g))
                lse = l_ref[pl.ds(h, 1), r]
                probs = [jnp.exp2(nt(k, q) * factor - lse) for k in keys]
                grad_p = [nt(v, g) for v in values]
                delta = sum(jnp.sum(p * d, axis=0, keepdims=True) for p, d in zip(probs, grad_p))
                grad_s = [(p * (d - delta)).astype(bf16) for p, d in zip(probs, grad_p)]
                dq = sum(tn(k, s) for k, s in zip(keys, grad_s)).T * scale
                d_ref[r, pl.ds(at, 2 * LANES)] = jnp.where(
                    mask, dq.astype(bf16), d_ref[r, pl.ds(at, 2 * LANES)]
                )
                for j in range(2):
                    dk_ref[j] += nn(grad_s[j], q)
                    dv_ref[j] += nn(probs[j].astype(bf16), g)
                return inner

            lax.fori_loop(0, rows // block, one_block, 0)
        mask = lane_mask((rows, 2 * LANES), first)
        for j, d_ref in enumerate((down_ref, doth_ref)):
            for lane, new in ((pad, dk_ref[j] * scale), (2 * pad, dv_ref[j])):
                d_ref[:, pl.ds(lane + at, 2 * LANES)] = jnp.where(
                    mask, new.astype(bf16), d_ref[:, pl.ds(lane + at, 2 * LANES)]
                )
        return carry

    lax.fori_loop(0, heads // 2, one_head, 0)
    pass_one(0, first, zsend_ref)
    for one in next_links:
        one.start()
    lax.fori_loop(heads // 2, heads, one_head, 0)
    pass_one(1, later, next1_ref)
    branch.wait()
    total2_ref[...] = own2_ref[...]
    for s in range(n_z - 1):
        z_links[s].wait()
        total2_ref[:, later] += decode(got2_ref[s, pl.ds(0, depth), :], bound_ref[0:1, 0:1])
        next_links[s].wait()
        own1_ref[:, first] += decode(zgot_ref[s, pl.ds(0, depth), :], bound_ref[1:2, 0:1])


def attend_back(
    own, oth, gown, goth, lown, loth, bounds, own2, b_send, code2, code1, mine1, heads, pad
):
    n_dp = lax.axis_size("dp")
    n_z, depth, hidden = mine1.shape
    chunk = hidden - code2.shape[2]
    n_links = 2 * n_z + 1
    rows = own.shape[0]
    vmem = pl.BlockSpec(memory_space=pltpu.VMEM)
    flops = 10 * heads * 4 * rows * rows * 2 * LANES
    return pl.pallas_call(
        functools.partial(
            attend_back_kernel, n_dp=n_dp, chunk=chunk, heads=heads, block=min(rows, 512), pad=pad, scale=HEAD_DIM**-0.5
        ),
        out_shape=(jax.ShapeDtypeStruct((rows, 3 * pad), bf16),) * 2
        + (
            jax.ShapeDtypeStruct(b_send.shape, b_send.dtype),
            jax.ShapeDtypeStruct((depth, hidden), f32),
            jax.ShapeDtypeStruct((depth, hidden), f32),
            jax.ShapeDtypeStruct(code2.shape, code2.dtype),
        ),
        in_specs=[vmem] * 8 + [pl.BlockSpec(memory_space=pl.ANY)] * 4,
        out_specs=[vmem] * 6,
        scratch_shapes=[pltpu.VMEM((2, rows, 2 * LANES), f32)] * 2
        + [
            pltpu.VMEM(b_send.shape, b_send.dtype),
            pltpu.VMEM(code2.shape, bf16),
            pltpu.VMEM(code2.shape, bf16),
            pltpu.VMEM(code1.shape, bf16),
            pltpu.VMEM(code1.shape, bf16),
            pltpu.VMEM(mine1.shape, f32),
            pltpu.VMEM(code2.shape[:2] + (chunk,), bf16),
            pltpu.VMEM(code2.shape[:2] + (chunk,), bf16),
            pltpu.SemaphoreType.DMA((4,)),
            pltpu.SemaphoreType.DMA((n_links,)),
            pltpu.SemaphoreType.DMA((n_links,)),
        ],
        cost_estimate=pl.CostEstimate(
            flops=flops, bytes_accessed=16 * rows * pad * 2, transcendentals=heads * rows * rows * 4
        ),
        compiler_params=pltpu.CompilerParams(
            collective_id=2, has_side_effects=True, vmem_limit_bytes=60 * 2**20
        ),
    )(own, oth, gown, goth, lown, loth, bounds, own2, b_send, code2, code1, mine1)


def close_kernel(
    aown_ref, aoth_ref, down_ref, doth_ref, mine_ref, other_ref, extra_ref, cond_ref, scale_ref,
    tops_ref, zsum_ref, fcbound_ref, fcown_ref, fccode_ref,
    w_any, noth_any, x_any, mid_any, zown_any, zoth_any, oown_any, ooth_any, ada_any,
    tokens_ref, gqkv_ref, gproj_ref, gada_ref, total_ref, etotal_ref, row_ref, fctotal_ref,
    w_ref, noth_ref, x_ref, mid_ref, z_ref, o_ref, ada_ref,
    turned_ref, part_ref, got_ref, xsend_ref, xgot_ref, zsend_ref, zgot_ref,
    hsend_ref, hgot_ref, hown_ref, fcgot_ref,
    rows_ref, rgot_ref, all_ref, cpart_ref, cswap_ref, parts_ref, bound_ref, bgot_ref, esend_ref, egot_ref,
    load_sem, send_sem, recv_sem,
    *, n_dp, n_mods, n_shared, pad,
):
    (me, z, x, c), across, core, beside, lines = peers(n_dp)
    n_z = n_dp // 4
    side = lax.axis_index("tensor")
    loads = [
        pltpu.make_async_copy(source, target, load_sem.at[k])
        for k, (source, target) in enumerate(
            (
                (zown_any, z_ref.at[0]),
                (zoth_any, z_ref.at[1]),
                (oown_any, o_ref.at[0]),
                (ooth_any, o_ref.at[1]),
                (w_any, w_ref),
                (noth_any, noth_ref),
                (x_any, x_ref),
                (mid_any, mid_ref),
                (ada_any, ada_ref),
            )
        )
    ]
    for load in loads:
        load.start()
    greet([across, core, beside] + lines)

    rows, depth = aown_ref.shape
    width = mine_ref.shape[1]
    block = got_ref.shape[3]
    n_parts = part_ref.shape[0]
    tile = min(rows, 128)

    link = linker(send_sem, recv_sem)

    def core_link(k):
        return link(part_ref.at[k], got_ref.at[k], core, k)

    def x_link(k):
        return link(xsend_ref.at[k], xgot_ref.at[k], beside, n_parts + k)

    def z_link(k, s):
        at = 2 * n_parts + k * (n_z - 1) + s
        return link(zsend_ref.at[k, s], zgot_ref.at[k, s], lines[s], at)

    n_sums = (n_z + 1) * n_parts
    middle = rows // 2
    half = [
        link(hsend_ref.at[pl.ds(at, middle)], hgot_ref.at[pl.ds(at, middle)], across, k)
        for at, k in ((0, n_sums), (middle, n_sums + 7 + 4 * n_z))
    ]
    swap_rows = link(rows_ref.at[1], rgot_ref, across, n_sums + 1)
    swap_part = link(cpart_ref, cswap_ref, across, n_sums + 2)
    core_bound = link(bound_ref.at[0], bgot_ref.at[0], core, n_sums + 3)
    x_bound = link(bound_ref.at[1], bgot_ref.at[1], beside, n_sums + 4)
    z_bounds = [
        link(bound_ref.at[2], bgot_ref.at[2 + s], lines[s], n_sums + 5 + s) for s in range(n_z - 1)
    ]

    first_extra = n_sums + 8 + 4 * n_z
    fc_links = [
        link(fccode_ref.at[s], fcgot_ref.at[s], to, n_sums + 7 + 3 * n_z + s)
        for s, to in enumerate(lines)
    ]
    for one in fc_links:
        one.start()

    def spread(ref, first):
        return (
            [link(ref.at[z, x, c], ref.at[z, x, c], core, first)],
            [link(ref.at[z, x], ref.at[z, x], beside, first + 1)],
            [link(ref.at[z], ref.at[z], to, first + 2 + s) for s, to in enumerate(lines)],
        )

    def start(links):
        for one in links:
            one.start()

    def wait(links):
        for one in links:
            one.wait()

    def largest(ref):
        return jnp.max(jnp.abs(ref[...].astype(f32)))

    def product(t, which, right_own, right_oth):
        made = nn(turned_ref[t, which, :, pl.ds(0, rows)], right_own)
        made += nn(turned_ref[t, which, :, pl.ds(rows, rows)], right_oth)
        return made.reshape(got_ref.shape[1:])

    def columns(k):
        at = pl.ds(pl.multiple_of(k * pad, LANES), pad)
        return down_ref[:, at], doth_ref[:, at]

    def to_core(k, right, t=0):
        part_ref[k] = product(t, 1 - c, *right)
        core_link(k).start()

    def to_beside(k, right, t=0):
        core_link(k).wait_recv()
        got_ref[k] += product(t, c, *right)
        away = got_ref[k, 1 - x].reshape(n_z * block, pad)
        xsend_ref[k] = encode(away, bound_ref[1, 0:1, 0:1])
        x_link(k).start()

    def to_lines(k):
        x_link(k).wait_recv()
        came = decode(xgot_ref[k], bgot_ref[1, 0:1, 0:1])
        got_ref[k, x] += came.reshape(n_z, block, pad)
        for s in range(n_z - 1):
            away = got_ref[k, x, lax.rem(z + s + 1, n_z)]
            zsend_ref[k, s, pl.ds(0, block), :] = encode(away, bound_ref[2, 0:1, 0:1])
            z_link(k, s).start()

    def loop(count, step):
        def body(k, carry):
            step(k)
            return carry

        lax.fori_loop(0, count, body, 0)

    def extra_links(k):
        if k < 3:
            return [link(esend_ref.at[k], egot_ref.at[k], (across, core, beside)[k], first_extra + k)]
        return [
            link(esend_ref.at[3], egot_ref.at[3 + s], to, first_extra + 3 + s)
            for s, to in enumerate(lines)
        ]

    def add_extra(k):
        if k == 0:
            total = extra_ref[...]
        else:
            wait(extra_links(k - 1))
            came = egot_ref[k - 1]
            if k == 1:
                row = lax.broadcasted_iota(jnp.int32, came.shape, 0)
                came = jnp.where(row >= came.shape[0] - n_shared, came, 0.0)
            total = esend_ref[k - 1] + came
        esend_ref[k] = total
        start(extra_links(k))

    add_extra(0)
    norm = 1.01 * depth**0.5
    a_bound = (tops_ref[2:3, 0:1] + 1.0) * norm
    v_bound = a_bound * (0.1875 * norm) + 1.25
    z_top = jnp.max(zsum_ref[4:5, :], axis=1, keepdims=True)
    most = a_bound * jnp.maximum(largest(down_ref), largest(doth_ref)) + 1.01 * v_bound * z_top
    most = most * (1.02 * 2 * rows) + 1e-30
    bound_ref[0] = jnp.broadcast_to(most, bound_ref.shape[1:])
    core_bound.start()
    zsend_ref[...] = jnp.zeros_like(zsend_ref)
    turn_over((lambda: aown_ref[...], lambda: aoth_ref[...]), turned_ref.at[0], n_z, block)
    add_extra(1)
    core_bound.wait()
    bound_ref[1] = bound_ref[0] + bgot_ref[0]
    x_bound.start()
    loop(3, lambda k: to_core(k, columns(k)))
    add_extra(2)
    x_bound.wait()
    bound_ref[2] = bound_ref[1] + bgot_ref[1]
    start(z_bounds)
    to_beside(0, columns(0))
    add_extra(3)
    to_beside(1, columns(1))

    wait(loads[4:7])

    def summed(carry, h, normed):
        return (
            carry[0] + jnp.sum(h, axis=0, keepdims=True),
            carry[1] + jnp.sum(h * normed, axis=0, keepdims=True),
        )

    def h_other(i, carry):
        r = pl.ds(pl.multiple_of(i * tile, tile), tile)
        h = nt(doth_ref[r, :], w_ref[...])
        hsend_ref[r, :] = h.astype(bf16)
        return summed(carry, h, noth_ref[r, :].astype(f32))

    late = lax.fori_loop(0, rows // tile, h_other, (jnp.zeros((1, depth), f32),) * 2)

    def h_own(i, carry):
        r = pl.ds(pl.multiple_of(i * tile, tile), tile)
        h = nt(down_ref[r, :], w_ref[...])
        hown_ref[r, :] = h
        return summed(carry, h, normalize(x_ref[r, :])[0])

    late = lax.fori_loop(0, rows // tile, h_own, late)
    rows_ref[0] = mine_ref[...]
    rows_ref[1] = other_ref[...]
    for j, values in enumerate(late):
        low_half, high_half = values[:, :width], values[:, width:]
        rows_ref[0, pl.ds(j, 1), :] = jnp.where(side == 0, low_half, high_half)
        rows_ref[1, pl.ds(j, 1), :] = jnp.where(side == 0, high_half, low_half)
    swap_rows.start()
    half[0].start()
    ones = jnp.ones((8, rows), bf16)
    d_sums = nn(ones, down_ref[...]) + nn(ones, doth_ref[...])
    for j, at in ((0, 0), (1, 2 * pad)):
        rows_ref[0, pl.ds(n_mods + j, 1), :] = d_sums[:1, at : at + width]
    to_lines(0)

    swap_rows.wait()
    row = lax.broadcasted_iota(jnp.int32, mine_ref.shape, 0)
    all_ref[z, x, c] = rows_ref[0] + jnp.where(row < n_mods, rgot_ref[...], 0.0)
    along = spread(all_ref, n_sums + 4 + n_z)
    start(along[0])
    wait(loads[:4])
    turn_over((lambda: z_ref[0], lambda: z_ref[1]), turned_ref.at[1], n_z, block)
    last = n_parts - 1
    wait(along[0])
    start(along[1])
    to_core(last, (o_ref[0], o_ref[1]), 1)
    to_beside(2, columns(2))
    wait(along[1])
    start(along[2])
    to_beside(last, (o_ref[0], o_ref[1]), 1)
    to_lines(1)
    wait(extra_links(3))
    total = esend_ref[3]
    for s in range(n_z - 1):
        total += egot_ref[3 + s]
    etotal_ref[...] = total
    wait(loads[7:])
    wait(along[2])
    everything = all_ref[...].reshape((n_dp,) + mine_ref.shape)
    total_ref[...] = jnp.sum(everything, axis=0)
    cond = cond_ref[...]
    part = jnp.zeros(cond.shape, f32)
    for j in range(n_mods):
        part += lax.dot_general(
            everything[:, j, :], ada_ref[j].astype(f32), (((1,), (1,)), ((), ())),
            precision=highest_precision_mode, preferred_element_type=f32,
        )
    cpart_ref[...] = part
    swap_part.start()
    half[1].start()
    for j in range(n_mods):
        gada_ref[j] = lax.dot_general(
            cond, everything[:, j, :], (((0,), (0,)), ((), ())),
            precision=highest_precision_mode, preferred_element_type=f32,
        )
    to_lines(2)
    swap_part.wait()
    whole = cpart_ref[...] + cswap_ref[...]
    parts_ref[z, x, c] = whole
    along = spread(parts_ref, n_sums + 6 + 2 * n_z)
    start(along[0])
    half[0].wait_recv()
    wait(along[0])
    start(along[1])

    def last_norm(i):
        r = pl.ds(pl.multiple_of(i * tile, tile), tile)
        h = hown_ref[r, :] + hgot_ref[r, :].astype(f32)
        normed, rscale = normalize(x_ref[r, :])
        tokens_ref[r, :] = mid_ref[r, :] + norm_back(h * (1.0 + scale_ref[...]), normed, rscale)

    wait(along[1])
    start(along[2])
    to_lines(last)
    loop(middle // tile, last_norm)
    half[1].wait_recv()
    loop(middle // tile, lambda i: last_norm(i + middle // tile))
    wait(along[2])
    for p in range(n_dp):
        row_ref[pl.ds(p, 1), :] = parts_ref[p // 4, (p // 2) % 2, p % 2, pl.ds(me, 1), :]

    wait(z_bounds)

    def finish(k):
        total = got_ref[k, x, z]
        for s in range(n_z - 1):
            z_link(k, s).wait_recv()
            total += decode(zgot_ref[k, s, pl.ds(0, block), :], bgot_ref[2 + s, 0:1, 0:1])
        return total

    for k in range(3):
        gqkv_ref[k] = finish(k)[:, :width]
    gproj_ref[...] = finish(last)[:, :width]
    for one in half:
        one.wait_send()
    wait(fc_links)
    fctotal_ref[...] = fcown_ref[...]
    later = fccode_ref.shape[2]
    at = pl.ds(fcown_ref.shape[1] - later, later)
    for s in range(n_z - 1):
        fctotal_ref[:, at] += decode(fcgot_ref[s, pl.ds(0, block), :], fcbound_ref[1:2, 0:1])

    def sent(k):
        core_link(k).wait_send()
        x_link(k).wait_send()
        for s in range(n_z - 1):
            z_link(k, s).wait_send()

    loop(n_parts, sent)


def close(
    a_own, a_oth, d_own, d_oth, mine, other, extra, cond, scale, tops, z_sums, fc_bounds, fc_own, fc_code,
    w_qkv, n_oth, tokens, mid_grad,
    z_own, z_oth, o_own, o_oth, ada, n_shared,
):
    n_dp = lax.axis_size("dp")
    n_z = n_dp // 4
    n_mods, block, width = ada.shape
    rows, depth = tokens.shape
    pad = o_own.shape[1]
    n_rows = mine.shape[0]
    n_parts = 4
    n_links = (n_z + 1) * n_parts + 10 + 5 * n_z
    tall = -(-block // 16) * 16
    vmem = pl.BlockSpec(memory_space=pltpu.VMEM)
    return pl.pallas_call(
        functools.partial(close_kernel, n_dp=n_dp, n_mods=n_mods, n_shared=n_shared, pad=pad),
        out_shape=(
            jax.ShapeDtypeStruct((rows, depth), f32),
            jax.ShapeDtypeStruct((3, block, width), f32),
            jax.ShapeDtypeStruct((block, width), f32),
            jax.ShapeDtypeStruct((n_mods, block, width), f32),
            jax.ShapeDtypeStruct((n_rows, width), f32),
            jax.ShapeDtypeStruct(extra.shape, f32),
            jax.ShapeDtypeStruct((n_dp, block), f32),
            jax.ShapeDtypeStruct(fc_own.shape, f32),
        ),
        in_specs=[vmem] * 14 + [pl.BlockSpec(memory_space=pl.ANY)] * 9,
        out_specs=[vmem] * 8,
        scratch_shapes=[
            pltpu.VMEM(w_qkv.shape, bf16),
            pltpu.VMEM((rows, depth), bf16),
            pltpu.VMEM((rows, depth), f32),
            pltpu.VMEM((rows, depth), f32),
            pltpu.VMEM((2, rows, depth), bf16),
            pltpu.VMEM((2, rows, pad), bf16),
            pltpu.VMEM(ada.shape, bf16),
            pltpu.VMEM((2, 2, depth // 2, 2 * rows), bf16),
            pltpu.VMEM((n_parts, 2, n_z, block, pad), f32),
            pltpu.VMEM((n_parts, 2, n_z, block, pad), f32),
            pltpu.VMEM((n_parts, n_z * block, pad), bf16),
            pltpu.VMEM((n_parts, n_z * block, pad), bf16),
            pltpu.VMEM((n_parts, n_z - 1, tall, pad), bf16),
            pltpu.VMEM((n_parts, n_z - 1, tall, pad), bf16),
            pltpu.VMEM((rows, depth), bf16),
            pltpu.VMEM((rows, depth), bf16),
            pltpu.VMEM((rows, depth), f32),
            pltpu.VMEM(fc_code.shape, bf16),
            pltpu.VMEM((2, n_rows, width), f32),
            pltpu.VMEM((n_rows, width), f32),
            pltpu.VMEM((n_z, 2, 2, n_rows, width), f32),
            pltpu.VMEM((n_dp, block), f32),
            pltpu.VMEM((n_dp, block), f32),
            pltpu.VMEM((n_z, 2, 2, n_dp, block), f32),
            pltpu.VMEM((3, 8, LANES), f32),
            pltpu.VMEM((n_z + 1, 8, LANES), f32),
            pltpu.VMEM((4,) + extra.shape, f32),
            pltpu.VMEM((n_z + 2,) + extra.shape, f32),
            pltpu.SemaphoreType.DMA((9,)),
            pltpu.SemaphoreType.DMA((n_links,)),
            pltpu.SemaphoreType.DMA((n_links,)),
        ],
        cost_estimate=pl.CostEstimate(
            flops=60 * 10**9, bytes_accessed=100 * 10**6, transcendentals=0
        ),
        compiler_params=pltpu.CompilerParams(
            collective_id=0, has_side_effects=True, vmem_limit_bytes=60 * 2**20
        ),
    )(
        a_own, a_oth, d_own, d_oth, mine, other, extra, cond, scale.reshape(1, -1), tops, z_sums,
        fc_bounds, fc_own, fc_code, w_qkv, n_oth, tokens, mid_grad, z_own, z_oth, o_own, o_oth, ada,
    )


def after(value, *others):
    return lax.optimization_barrier((value,) + others)[0]


TOP = 32768.0


def fast_body(
    latent_tokens,
    conditioning,
    out_grad,
    qkv_weight,
    qkv_bias,
    proj_weight,
    proj_bias,
    first_layer_weight,
    fc1_bias,
    fc2_weight,
    second_layer_bias,
    ada_weight,
    ada_bias,
):
    n_dp = lax.axis_size("dp")
    n_z = n_dp // 4
    me = lax.axis_index("dp")
    side = lax.axis_index("tensor")
    core, at_x, at_z = me % 2, (me // 2) % 2, me // 4
    rows, width_full = latent_tokens.shape
    block, _, width = qkv_weight.shape
    heads = width // HEAD_DIM
    pad = -(-width // LANES) * LANES

    def swap(values):
        return lax.ppermute(values, "tensor", [(0, 1), (1, 0)])

    def flip(values, bit):
        return lax.ppermute(values, "dp", [(i, i ^ bit) for i in range(n_dp)])

    def shift(values, step):
        return lax.ppermute(values, "dp", [(i, (i + 4 * step) % n_dp) for i in range(n_dp)])

    def place(pieces, spots):
        out = jnp.zeros((len(pieces),) + pieces[0].shape, pieces[0].dtype)
        for piece, spot in zip(pieces, spots):
            out = lax.dynamic_update_index_in_dim(out, piece, spot, 0)
        return out

    def pair(mine, other, bit):
        return jnp.where(bit == 0, jnp.stack([mine, other]), jnp.stack([other, mine]))

    def along_z(values):
        pieces = [values] + [shift(values, s) for s in range(1, n_z)]
        return place(pieces, [(at_z - s) % n_z for s in range(n_z)])

    def in_order(both, shape):
        both = both.reshape((2, 2, n_z) + shape)
        return jnp.transpose(both, (2, 1, 0) + tuple(range(3, both.ndim))).reshape((n_dp,) + shape)

    def gather(values):
        lines = along_z(values)
        planes = place([lines, flip(lines, 2)], [at_x, 1 - at_x])
        both = place([planes, flip(planes, 1)], [core, 1 - core])
        return in_order(both, values.shape)

    def pick(array, spot, axis):
        return lax.dynamic_index_in_dim(array, spot, axis, keepdims=False)

    def scatter_sum(values):
        parts = values.reshape((n_z, 2, 2) + values.shape[1:])
        parts = pick(parts, core, 2) + flip(pick(parts, 1 - core, 2), 1)
        parts = pick(parts, at_x, 1) + flip(pick(parts, 1 - at_x, 1), 2)
        total = pick(parts, at_z, 0)
        for s in range(1, n_z):
            total = total + shift(pick(parts, (at_z + s) % n_z, 0), s)
        return total

    def narrow(part, bound):
        return (part * (TOP / bound)).astype(jnp.float16)

    def wide(part, bound):
        return part.astype(f32) * (bound * (1.0 / TOP))

    def biggest_over_dp(values):
        values = jnp.maximum(values, flip(values, 1))
        values = jnp.maximum(values, flip(values, 2))
        others = [shift(values, s) for s in range(1, n_z)]
        return functools.reduce(jnp.maximum, others, values)

    def total_over_dp(values):
        values = values + flip(values, 1)
        values = values + flip(values, 2)
        return jnp.sum(along_z(values), axis=0)

    def halves(mine, other, axis):
        first = jnp.where(side == 0, mine, other)
        second = jnp.where(side == 0, other, mine)
        return jnp.concatenate([first, second], axis=axis)

    def pad_lanes(values):
        return jnp.pad(values, [(0, 0)] * (values.ndim - 1) + [(0, pad - width)])

    def biggest(*pieces):
        return functools.reduce(jnp.maximum, [jnp.max(jnp.abs(v.astype(f32))) for v in pieces])

    def full_weight(shard):
        return lax.all_gather(shard, "dp", axis=0, tiled=True)

    first = [
        pad_lanes(qkv_weight.astype(bf16)).reshape(block, 3 * pad),
        pad_lanes(proj_weight.astype(bf16).T),
    ]
    w_first = full_weight(jnp.concatenate(first, axis=1))
    w_qkv, w_proj = w_first[:, : 3 * pad], w_first[:, 3 * pad :]
    second = [first_layer_weight.astype(bf16), fc2_weight.astype(bf16).T]
    w_second = full_weight(jnp.concatenate(second, axis=1))
    hidden = first_layer_weight.shape[1]

    tokens = float(n_dp * SEQ)
    tiny = 1e-30
    silu_cond, silu_pull = jax.vjp(jax.nn.silu, conditioning)
    cond_tiles = lax.reduce_precision(silu_cond, 8, 7).reshape(-1, LANES)
    ada = ada_weight.astype(bf16)
    a_own, g_own, n_oth, mods, tops, cond_mine, g_sums = open_part(
        cond_tiles, pad_lanes(ada).reshape(block, 6 * pad),
        pad_lanes(ada_bias).reshape(-1, LANES), latent_tokens, out_grad, width,
    )
    shift_one, scale_one, gate_one, shift_two, scale_two, gate_two = [mods[j] for j in range(6)]
    a_oth = swap(a_own)
    g_oth = swap(after(g_own, a_own))
    norm = 1.01 * width_full**0.5
    p_bound = ((tops[2, 0] + 1.0) * (norm * 0.1875 * norm) + 1.25) * (1.01 * 0.75 * width)

    bias = pad_lanes(jnp.stack([qkv_bias[0], jnp.zeros_like(qkv_bias[0]), qkv_bias[1]]))
    bias = bias.reshape(3 * pad)
    qkv_own = (nn(a_own, w_qkv) + bias).astype(bf16)
    qkv_oth = (nn(a_oth, w_qkv) + bias).astype(bf16)
    o_oth, lse_oth = attend(qkv_oth, qkv_own, qkv_oth, heads, pad)
    p_send = narrow(nt(o_oth, w_proj), p_bound)
    part_oth = wide(swap(p_send), p_bound)
    o_own, lse_own = attend(after(qkv_own, p_send), qkv_own, qkv_oth, heads, pad)
    branch_one = nt(o_own, w_proj) + part_oth + proj_bias
    middle = latent_tokens + gate_one * branch_one
    normed_two, rscale_two = normalize(middle)

    m_own = low(normed_two * (1.0 + scale_two) + shift_two)
    m_oth = swap(m_own)
    hidden_bias = fc1_bias.reshape(1, -1)
    act_own, gp_own, h_own, b_own = feed(m_own, g_own, w_second, hidden_bias, f32)
    act_oth, gp_oth, h_send, b_send = feed(
        m_oth, after(g_oth, m_own), w_second, hidden_bias, bf16
    )
    (
        mid_grad, z_own, z_oth, go_own, go_oth, turned, fc1_sums,
        fc2_own, fc2_code, fc1_mine, fc1_code, fc_bounds,
    ) = middle_part(
        h_send, scale_two, gate_one, tops, g_own, g_oth, m_own, m_oth, act_own, act_oth,
        gp_own, gp_oth, h_own, middle, out_grad, branch_one, w_proj, block,
    )
    d_own, d_oth, b_oth, grad_fc2, fc1_own, fc1_code = attend_back(
        qkv_own, qkv_oth, go_own, go_oth, lse_own, lse_oth, fc_bounds, fc2_own, b_send,
        fc2_code, fc1_code, fc1_mine, heads, pad,
    )
    branch_two = b_own + b_oth.astype(f32) + second_layer_bias
    layer_out = middle + gate_two * branch_two

    sums = functools.partial(jnp.sum, axis=0)
    empty = jnp.zeros((2, width_full), f32)
    mods_sums = jnp.stack([turned[0], turned[1], turned[2], sums(out_grad * branch_two)])
    mods_sums = jnp.concatenate([empty, mods_sums]).reshape(6, 2, width)
    spare = jnp.zeros((2, width), f32)
    mine = jnp.concatenate([pick(mods_sums, side, 1), spare])
    other = jnp.concatenate([pick(mods_sums, 1 - side, 1), spare])
    shared = jnp.stack([turned[3], g_sums[0]]).reshape(-1, width)
    extra = jnp.concatenate([fc1_sums[0].reshape(-1, width), shared])
    ada = jnp.transpose(ada, (1, 0, 2))
    (
        tokens_grad, grad_qkv, grad_proj, grad_ada, totals, extra, cond_row, grad_fc1,
    ) = close(
        a_own, a_oth, d_own, d_oth, mine, other, extra, cond_mine, scale_one, tops, turned,
        fc_bounds, fc1_own, fc1_code, w_qkv, n_oth, latent_tokens, mid_grad, z_own, z_oth,
        o_own, o_oth, ada, shared.shape[0],
    )
    grad_qkv = jnp.transpose(grad_qkv, (1, 0, 2))
    grad_ada = jnp.transpose(grad_ada, (1, 0, 2))
    grad_proj, grad_fc2 = grad_proj.T, grad_fc2.T
    conditioning_grad = silu_pull(cond_row.reshape(1, width_full))[0]
    fc1_rows = hidden // width
    qkv_bias_grad = totals[6:8]
    grad_ada_bias = totals[:6]
    fc1_bias_grad = extra[:fc1_rows].reshape(hidden)
    proj_bias_grad, fc2_bias_grad = extra[fc1_rows:].reshape(2, width_full)
    return (
        layer_out,
        tokens_grad,
        conditioning_grad,
        grad_qkv,
        qkv_bias_grad,
        grad_proj,
        proj_bias_grad,
        grad_fc1,
        fc1_bias_grad,
        grad_fc2,
        fc2_bias_grad,
        grad_ada,
        grad_ada_bias,
    )


def solution(mesh):
    in_specs = (
        P(("dp", "tensor"), None),
        P("dp", None),
        P(("dp", "tensor"), None),
        P("dp", None, "tensor"),
        P(None, "tensor"),
        P("tensor", "dp"),
        P(),
        P("dp", "tensor"),
        P("tensor"),
        P("tensor", "dp"),
        P(),
        P("dp", None, "tensor"),
        P(None, "tensor"),
    )
    out_specs = (
        P(("dp", "tensor"), None),
        P(("dp", "tensor"), None),
        P("dp", None),
        P("dp", None, "tensor"),
        P(None, "tensor"),
        P("tensor", "dp"),
        P(),
        P("dp", "tensor"),
        P("tensor"),
        P("tensor", "dp"),
        P(),
        P("dp", None, "tensor"),
        P(None, "tensor"),
    )
    body = fast_body if fits(mesh) else general_body
    return jax.shard_map(body, mesh=mesh, in_specs=in_specs, out_specs=out_specs, check_vma=False)
```

```python
import functools

import jax
import jax.numpy as jnp
from jax import lax
from jax.experimental import pallas as pl
from jax.experimental.pallas import tpu as pltpu
from jax.sharding import PartitionSpec as P

HEAD_DIM = 72
SEQ = 1024


highest_precision_mode = lax.Precision.HIGHEST
epsilon = 1e-06


def gelu_tanh(values):
    return jax.nn.gelu(values, approximate=True)


def normalize(values):
    center = values - jnp.mean(values, axis=-1, keepdims=True)
    scaled = lax.rsqrt(jnp.mean(center * center, axis=-1, keepdims=True) + epsilon)
    return (center * scaled, scaled)


def norm_back(grad, normed, scaled):
    first = jnp.mean(grad, axis=-1, keepdims=True)
    second = jnp.mean(grad * normed, axis=-1, keepdims=True)
    return (grad - first - normed * second) * scaled


def general_body(
    latent_tokens,
    conditioning,
    out_grad,
    qkv_weight,
    qkv_bias,
    proj_weight,
    proj_bias,
    first_layer_weight,
    fc1_bias,
    fc2_weight,
    second_layer_bias,
    ada_weight,
    ada_bias,
):

    def fetch():
        return (
            lax.all_gather(qkv_weight.astype(jnp.bfloat16), "dp", axis=0, tiled=True),
            lax.all_gather(proj_weight.astype(jnp.bfloat16), "dp", axis=1, tiled=True),
            lax.all_gather(first_layer_weight.astype(jnp.bfloat16), "dp", axis=0, tiled=True),
            lax.all_gather(fc2_weight.astype(jnp.bfloat16), "dp", axis=1, tiled=True),
            lax.all_gather(ada_weight.astype(jnp.bfloat16), "dp", axis=0, tiled=True),
        )

    w_qkv, w_proj, w_fc1, w_fc2, w_ada = fetch()
    tok_rows, width_full = latent_tokens.shape
    latents = conditioning.shape[0]
    group_rows = tok_rows * lax.axis_size("tensor")
    width = w_qkv.shape[2]
    heads_local = width // HEAD_DIM
    factor = HEAD_DIM ** (-0.5)
    silu_cond, silu_pull = jax.vjp(jax.nn.silu, conditioning)
    cond_low = silu_cond.astype(jnp.bfloat16)
    mod_part = (
        jnp.einsum("ld,dkf->lkf", cond_low, w_ada, preferred_element_type=jnp.float32) + ada_bias
    )
    modulation_values = lax.all_gather(mod_part, "tensor", axis=2, tiled=True)
    span = min(tok_rows, SEQ)
    block_count = tok_rows // span
    first_row = lax.axis_index("tensor") * tok_rows
    block_latent = (first_row + jnp.arange(block_count, dtype=jnp.int32) * span) // SEQ
    select_helper = (block_latent[:, None] == jnp.arange(latents, dtype=jnp.int32)[None, :]).astype(
        jnp.float32
    )
    block_modulation_terms = jnp.einsum(
        "pe,egt->pgt", select_helper, modulation_values, precision=highest_precision_mode
    )

    def spread(values):
        return jnp.broadcast_to(values[:, None, :], (block_count, span, width_full)).reshape(
            tok_rows, width_full
        )

    def per_latent(values):
        sums = jnp.sum(values.reshape(block_count, span, width_full), axis=1)
        return jnp.einsum("bl,bd->ld", select_helper, sums, precision=highest_precision_mode)

    shift_one = spread(block_modulation_terms[:, 0])
    scale_one = spread(block_modulation_terms[:, 1])
    gate_one = spread(block_modulation_terms[:, 2])
    shift_two = spread(block_modulation_terms[:, 3])
    scale_two = spread(block_modulation_terms[:, 4])
    gate_two = spread(block_modulation_terms[:, 5])
    normed_one, rscale_one = normalize(latent_tokens)
    attn_input = (normed_one * (1.0 + scale_one) + shift_one).astype(jnp.bfloat16)
    qkv_shift = jnp.stack([qkv_bias[0], jnp.zeros_like(qkv_bias[0]), qkv_bias[1]])
    piece = lax.all_gather(attn_input, "tensor", axis=0, tiled=True)
    rows_buf = piece
    made = jnp.einsum("rd,dkf->rkf", piece, w_qkv, preferred_element_type=jnp.float32) + qkv_shift
    made_buf = made.astype(jnp.bfloat16)
    attn_rows = rows_buf
    qkv_all = made_buf
    qkv_latent = qkv_all.reshape(group_rows // SEQ, SEQ, 3, heads_local, HEAD_DIM)

    def attend(block):
        query, keys, values = (block[:, 0], block[:, 1], block[:, 2])
        scores = (
            jnp.einsum("qhd,khd->hqk", query, keys, preferred_element_type=jnp.float32) * factor
        )
        peak = jnp.max(scores, axis=-1, keepdims=True)
        expo = jnp.exp(scores - peak)
        total = jnp.sum(expo, axis=-1, keepdims=True)
        probs = (expo / total).astype(jnp.bfloat16)
        result = jnp.einsum("hqk,khd->qhd", probs, values, preferred_element_type=jnp.float32)
        return (result.astype(jnp.bfloat16), peak[..., 0] + jnp.log(total[..., 0]))

    attn_low, logsum = lax.map(attend, qkv_latent)
    attn_low = attn_low.reshape(group_rows, width)
    rows = attn_low
    branch_one = (
        lax.psum_scatter(
            jnp.dot(rows, w_proj, preferred_element_type=jnp.float32),
            "tensor",
            scatter_dimension=0,
            tiled=True,
        )
        + proj_bias
    )
    middle = latent_tokens + gate_one * branch_one
    normed_two, rscale_two = normalize(middle)
    mlp_input = (normed_two * (1.0 + scale_two) + shift_two).astype(jnp.bfloat16)
    piece = lax.all_gather(mlp_input, "tensor", axis=0, tiled=True)
    rows_buf = piece
    made = jnp.dot(piece, w_fc1, preferred_element_type=jnp.float32) + fc1_bias
    made_buf = made
    act, gelu_pull = jax.vjp(gelu_tanh, made_buf)
    act_low = act.astype(jnp.bfloat16)
    rows = act_low
    branch_two = (
        lax.psum_scatter(
            jnp.dot(rows, w_fc2, preferred_element_type=jnp.float32).astype(jnp.bfloat16),
            "tensor",
            scatter_dimension=0,
            tiled=True,
        ).astype(jnp.float32)
        + second_layer_bias
    )
    layer_out = middle + gate_two * branch_two
    w_qkv, w_proj, w_fc1, w_fc2, w_ada = fetch()
    d_gate_two = per_latent(out_grad * branch_two)
    grad_m = (gate_two * out_grad).astype(jnp.bfloat16)
    fc2_bias_part = jnp.sum(grad_m.astype(jnp.float32), axis=0)
    piece = lax.all_gather(grad_m, "tensor", axis=0, tiled=True)
    made = jnp.einsum("rd,fd->rf", piece, w_fc2, preferred_element_type=jnp.float32)
    act_buf = made
    weight_acc = jnp.einsum("rf,rd->fd", act_low, piece, preferred_element_type=jnp.float32)
    grad_fc2 = weight_acc
    grad_pre = gelu_pull(act_buf)[0].astype(jnp.bfloat16)
    fc1_bias_part = jnp.sum(grad_pre.astype(jnp.float32), axis=0)
    grad_fc1 = jnp.einsum("rd,rf->df", rows_buf, grad_pre, preferred_element_type=jnp.float32)
    rows = grad_pre
    grad_h_two = lax.psum_scatter(
        jnp.einsum("rf,df->rd", rows, w_fc1, preferred_element_type=jnp.float32),
        "tensor",
        scatter_dimension=0,
        tiled=True,
    )
    d_shift_two = per_latent(grad_h_two)
    d_scale_two = per_latent(grad_h_two * normed_two)
    grad_mid = out_grad + norm_back(grad_h_two * (1.0 + scale_two), normed_two, rscale_two)
    d_gate_one = per_latent(grad_mid * branch_one)
    grad_z = (gate_one * grad_mid).astype(jnp.bfloat16)
    proj_bias_part = jnp.sum(grad_z.astype(jnp.float32), axis=0)
    piece = lax.all_gather(grad_z, "tensor", axis=0, tiled=True)
    made = jnp.einsum("rd,fd->rf", piece, w_proj, preferred_element_type=jnp.float32)
    weight_acc = jnp.einsum("rf,rd->fd", attn_low, piece, preferred_element_type=jnp.float32)
    grad_attn_low = made.astype(jnp.bfloat16).reshape(group_rows // SEQ, SEQ, heads_local, HEAD_DIM)

    def attend_back(block):
        packed, grad_o, lse = block
        query, keys, values = (packed[:, 0], packed[:, 1], packed[:, 2])
        scores = (
            jnp.einsum("qhd,khd->hqk", query, keys, preferred_element_type=jnp.float32) * factor
        )
        probs = jnp.exp(scores - lse[..., None])
        probs_low = probs.astype(jnp.bfloat16)
        grad_p = jnp.einsum("qhd,khd->hqk", grad_o, values, preferred_element_type=jnp.float32)
        grad_v = jnp.einsum("hqk,qhd->khd", probs_low, grad_o, preferred_element_type=jnp.float32)
        delta = jnp.sum(grad_p * probs, axis=-1, keepdims=True)
        grad_s = (probs * (grad_p - delta)).astype(jnp.bfloat16)
        grad_q = (
            jnp.einsum("hqk,khd->qhd", grad_s, keys, preferred_element_type=jnp.float32) * factor
        )
        grad_k = (
            jnp.einsum("hqk,qhd->khd", grad_s, query, preferred_element_type=jnp.float32) * factor
        )
        return jnp.stack([grad_q, grad_k, grad_v], axis=1).astype(jnp.bfloat16)

    grad_qkv = lax.map(attend_back, (qkv_latent, grad_attn_low, logsum)).reshape(
        group_rows, 3, width
    )
    qkv_bias_part = jnp.sum(grad_qkv.astype(jnp.float32), axis=0)
    grad_qkv_weight = jnp.einsum(
        "rd,rkf->dkf", attn_rows, grad_qkv, preferred_element_type=jnp.float32
    )
    rows = grad_qkv
    grad_h_one = lax.psum_scatter(
        jnp.einsum("rkf,dkf->rd", rows, w_qkv, preferred_element_type=jnp.float32),
        "tensor",
        scatter_dimension=0,
        tiled=True,
    )
    d_shift_one = per_latent(grad_h_one)
    d_scale_one = per_latent(grad_h_one * normed_one)
    tokens_grad = grad_mid + norm_back(grad_h_one * (1.0 + scale_one), normed_one, rscale_one)
    grad_mods = jnp.stack(
        [d_shift_one, d_scale_one, d_gate_one, d_shift_two, d_scale_two, d_gate_two], axis=1
    )
    mods_share = lax.psum_scatter(grad_mods, "tensor", scatter_dimension=2, tiled=True)
    grad_ada = jnp.einsum(
        "ld,lkf->dkf", cond_low.astype(jnp.float32), mods_share, precision=highest_precision_mode
    )
    grad_ada_bias = jnp.sum(mods_share, axis=0)
    cond_part = jnp.einsum(
        "lkf,dkf->ld", mods_share, w_ada.astype(jnp.float32), precision=highest_precision_mode
    )
    tensor_totals = lax.psum((cond_part, proj_bias_part, fc2_bias_part), "tensor")
    conditioning_grad = silu_pull(tensor_totals[0])[0]
    weight_totals = (
        lax.psum_scatter(grad_qkv_weight, "dp", scatter_dimension=0, tiled=True),
        lax.psum_scatter(weight_acc, "dp", scatter_dimension=1, tiled=True),
        lax.psum_scatter(grad_fc1, "dp", scatter_dimension=0, tiled=True),
        lax.psum_scatter(grad_fc2, "dp", scatter_dimension=1, tiled=True),
        lax.psum_scatter(grad_ada, "dp", scatter_dimension=0, tiled=True),
    )
    qkv_bias_pair = jnp.stack([qkv_bias_part[0], qkv_bias_part[2]])
    bias_totals = lax.psum(
        (qkv_bias_pair, tensor_totals[1], fc1_bias_part, tensor_totals[2], grad_ada_bias), "dp"
    )
    return (
        layer_out,
        tokens_grad,
        conditioning_grad,
        weight_totals[0],
        bias_totals[0],
        weight_totals[1],
        bias_totals[1],
        weight_totals[2],
        bias_totals[2],
        weight_totals[3],
        bias_totals[3],
        weight_totals[4],
        bias_totals[4],
    )


LANES = 128
LOG2E = 1.4426950408889634
f32 = jnp.float32
bf16 = jnp.bfloat16


def fits(mesh):
    return mesh.shape["tensor"] == 2 and mesh.shape["dp"] == 16


def low(values):
    return lax.reduce_precision(values, 8, 7).astype(bf16)


def nn(a, b):
    return lax.dot_general(a, b, (((1,), (0,)), ((), ())), preferred_element_type=f32)


def nt(a, b):
    return lax.dot_general(a, b, (((1,), (1,)), ((), ())), preferred_element_type=f32)


def tn(a, b):
    return lax.dot_general(a, b, (((0,), (0,)), ((), ())), preferred_element_type=f32)


def window(head):
    start = pl.multiple_of(((head * HEAD_DIM) // LANES) * LANES, LANES)
    return start, head * HEAD_DIM - start


def lane_mask(shape, first):
    lane = lax.broadcasted_iota(jnp.int32, shape, 1)
    return (lane >= first) & (lane < first + HEAD_DIM)


def attend_kernel(q_ref, own_ref, oth_ref, o_ref, lse_ref, *, heads, block, pad, scale):
    rows = q_ref.shape[0]
    factor = scale * LOG2E
    o_ref[...] = jnp.zeros_like(o_ref)

    def one_head(h, carry):
        at, first = window(h)

        def one_block(i, inner):
            r = pl.ds(pl.multiple_of(i * block, block), block)
            mask = lane_mask((block, 2 * LANES), first)
            q = q_ref[r, pl.ds(at, 2 * LANES)]
            q = jnp.where(mask, q, jnp.zeros_like(q))
            scores = [nt(ref[:, pl.ds(pad + at, 2 * LANES)], q) for ref in (own_ref, oth_ref)]
            peak = functools.reduce(
                jnp.maximum, [jnp.max(s, axis=0, keepdims=True) for s in scores]
            )
            peak = peak * factor
            expo = [jnp.exp2(s * factor - peak) for s in scores]
            total = sum(jnp.sum(e, axis=0, keepdims=True) for e in expo)
            inverse = 1.0 / total
            out = sum(
                tn(ref[:, pl.ds(2 * pad + at, 2 * LANES)], (e * inverse).astype(bf16))
                for ref, e in zip((own_ref, oth_ref), expo)
            ).T
            o_ref[r, pl.ds(at, 2 * LANES)] = jnp.where(
                mask, out.astype(bf16), o_ref[r, pl.ds(at, 2 * LANES)]
            )
            lse_ref[pl.ds(h, 1), r] = peak + jnp.log2(total)
            return inner

        return lax.fori_loop(0, rows // block, one_block, carry)

    lax.fori_loop(0, heads, one_head, 0)


def attend(queries, own, oth, heads, pad):
    rows = queries.shape[0]
    flops = 4 * heads * rows * 2 * rows * 2 * LANES
    return pl.pallas_call(
        functools.partial(
            attend_kernel, heads=heads, block=min(rows, 512), pad=pad, scale=HEAD_DIM**-0.5
        ),
        out_shape=(
            jax.ShapeDtypeStruct((rows, pad), bf16),
            jax.ShapeDtypeStruct((heads, rows), f32),
        ),
        cost_estimate=pl.CostEstimate(
            flops=4 * flops, bytes_accessed=8 * rows * pad * 2, transcendentals=heads * rows * rows * 2
        ),
        compiler_params=pltpu.CompilerParams(vmem_limit_bytes=40 * 2**20),
    )(queries, own, oth)


GELU = 0.7978845608028654


def feed_kernel(
    m_ref, g_ref, w1_ref, w2_ref, b_ref, act_ref, gp_ref, h_ref, out_ref, hacc_ref, oacc_ref, *, steps
):
    i = pl.program_id(0)

    @pl.when(i == 0)
    def _():
        hacc_ref[...] = jnp.zeros_like(hacc_ref)
        oacc_ref[...] = jnp.zeros_like(oacc_ref)

    pre = nn(m_ref[...], w1_ref[...]) + b_ref[...]
    grad_act = nn(g_ref[...], w2_ref[...])
    square = pre * pre
    gate = 1.0 / (1.0 + jnp.exp((-2.0 * GELU) * pre * (1.0 + 0.044715 * square)))
    act = (pre * gate).astype(bf16)
    act_ref[...] = act
    slope = gate + pre * gate * (1.0 - gate) * ((2.0 * GELU) * (1.0 + (3.0 * 0.044715) * square))
    grad_pre = (grad_act * slope).astype(bf16)
    gp_ref[...] = grad_pre
    hacc_ref[...] += nt(grad_pre, w1_ref[...])
    oacc_ref[...] += nt(act, w2_ref[...])

    @pl.when(i == steps - 1)
    def _():
        h_ref[...] = hacc_ref[...].astype(h_ref.dtype)
        out_ref[...] = oacc_ref[...].astype(out_ref.dtype)


def feed(m, g, weights, bias, out_dtype):
    rows, depth = m.shape
    hidden = weights.shape[1] // 2
    steps = 3 if hidden % (3 * LANES) == 0 else 1
    chunk = hidden // steps
    whole = pl.BlockSpec((rows, depth), lambda i: (0, 0))
    first = pl.BlockSpec((depth, chunk), lambda i: (0, i))
    second = pl.BlockSpec((depth, chunk), lambda i: (0, i + steps))
    tall = pl.BlockSpec((rows, chunk), lambda i: (0, i))
    return pl.pallas_call(
        functools.partial(feed_kernel, steps=steps),
        grid=(steps,),
        in_specs=[whole, whole, first, second, pl.BlockSpec((1, chunk), lambda i: (0, i))],
        out_specs=[tall, tall, whole, whole],
        out_shape=(
            jax.ShapeDtypeStruct((rows, hidden), bf16),
            jax.ShapeDtypeStruct((rows, hidden), bf16),
            jax.ShapeDtypeStruct((rows, depth), out_dtype),
            jax.ShapeDtypeStruct((rows, depth), out_dtype),
        ),
        scratch_shapes=[pltpu.VMEM((rows, depth), f32)] * 2,
        cost_estimate=pl.CostEstimate(
            flops=12 * rows * depth * hidden,
            bytes_accessed=4 * depth * hidden + 8 * rows * depth + 4 * rows * hidden,
            transcendentals=rows * hidden,
        ),
        compiler_params=pltpu.CompilerParams(vmem_limit_bytes=56 * 2**20),
    )(m, g, weights, weights, bias)


def peers(n_dp):
    me, side = lax.axis_index("dp"), lax.axis_index("tensor")
    n_z = n_dp // 4
    z, x, c = me // 4, (me // 2) % 2, me % 2
    across = (me, 1 - side)
    core = (z * 4 + x * 2 + 1 - c, side)
    beside = (z * 4 + (1 - x) * 2 + c, side)
    lines = [(lax.rem(z + s, n_z) * 4 + x * 2 + c, side) for s in range(1, n_z)]
    return (me, z, x, c), across, core, beside, lines


def greet(partners):
    barrier = pltpu.get_barrier_semaphore()
    for partner in partners:
        pl.semaphore_signal(barrier, inc=1, device_id=partner, device_id_type=pl.DeviceIdType.MESH)
    pl.semaphore_wait(barrier, len(partners))


SPAN = 2.0**63
QUARTERS = (SPAN, 1.0, 1.0 / SPAN, 1.0 / SPAN / SPAN)
STEP = 1.0 / 512.0


def encode(values, bound):
    scaled = (values * 2.0**40) * (0.98 * 2.0**23 / bound)
    size = jnp.abs(scaled)
    near = size.astype(bf16).astype(f32)
    rest, step = size - near, near * STEP
    below = jnp.where(rest < -step, QUARTERS[0], QUARTERS[1])
    above = jnp.where(rest < step, QUARTERS[2], QUARTERS[3])
    coded = near * jnp.where(rest < 0.0, below, above)
    coded = jnp.where(near <= 1.0, 0.0, coded)
    return jnp.where(scaled < 0.0, -coded, coded).astype(bf16)


def decode(coded, bound):
    coded = coded.astype(f32)
    size = jnp.abs(coded)
    factors = [(1.0 + (k - 1.5) * STEP) / q for k, q in enumerate(QUARTERS)]
    large = jnp.where(size > SPAN, factors[0], factors[1])
    small = jnp.where(size > 1.0 / SPAN, factors[2], factors[3])
    scaled = coded * jnp.where(size > 1.0, large, small)
    return (scaled * 2.0**-40) * (bound * (2.0**-23 / 0.98))


def linker(send_sem, recv_sem):
    def link(source, target, to, k):
        return pltpu.make_async_remote_copy(
            src_ref=source, dst_ref=target, send_sem=send_sem.at[k], recv_sem=recv_sem.at[k],
            device_id=to, device_id_type=pl.DeviceIdType.MESH,
        )

    return link


def turn_over(reads, turned_ref, n_z, block):
    for j, read in enumerate(reads):
        turned = read().astype(f32).T
        rows = turned.shape[1]
        for z in range(n_z):
            for x in range(2):
                for c in range(2):
                    b = (z * 2 + x) * 2 + c
                    at = pl.ds((x * n_z + z) * block, block)
                    turned_ref[c, at, pl.ds(j * rows, rows)] = turned[
                        b * block : (b + 1) * block
                    ].astype(bf16)


def open_kernel(
    cond_ref, ada_ref, bias_ref, x_ref, out_ref,
    aown_ref, gown_ref, noth_ref, mods_ref, top_ref, mine_ref, gsum_ref,
    cond_all, part_ref, cgot_ref, xgot_ref, zgot_ref, half_ref, other_ref, normed_ref, nown_ref,
    send_sem, recv_sem,
    *, n_dp, n_mods, width,
):
    (me, z, x, c), across, core, beside, lines = peers(n_dp)
    n_z = n_dp // 4
    side = lax.axis_index("tensor")
    link = linker(send_sem, recv_sem)
    rows, depth = x_ref.shape
    block = ada_ref.shape[0]
    tile = min(rows, 128)
    per_mod = part_ref.shape[3] // n_mods
    greet([across, core, beside] + lines)

    def step(copies, beside_work=None):
        for copy in copies:
            copy.start()
        if beside_work is not None:
            beside_work()
        for copy in copies:
            copy.wait()

    def loop(body):
        def one(i, carry):
            body(pl.ds(pl.multiple_of(i * tile, tile), tile))
            return carry

        lax.fori_loop(0, rows // tile, one, 0)

    def norm_tile(r):
        normed = normalize(x_ref[r, :])[0]
        normed_ref[r, :] = normed
        nown_ref[r, :] = normed.astype(bf16)

    cond_all[z, x, c] = cond_ref[...]
    mine = cond_all.at[z, x, c]
    step([link(mine, mine, core, 0)], lambda: loop(norm_tile))
    normed_link = link(nown_ref, noth_ref, across, 3 + 2 * n_z)
    normed_link.start()
    mine = cond_all.at[z, x]
    step([link(mine, mine, beside, 1)])
    mine = cond_all.at[z]
    step([link(mine, mine, to, 2 + s) for s, to in enumerate(lines)])
    everyone = cond_all[...].reshape(n_dp, depth // LANES, LANES)
    flat = jnp.concatenate([everyone[:, i, :] for i in range(depth // LANES)], axis=1)
    feature = lax.broadcasted_iota(jnp.int32, (depth, block), 0)
    column = lax.broadcasted_iota(jnp.int32, (depth, block), 1)
    chosen = nn(flat.astype(bf16), (feature == column + me * block).astype(bf16))
    mine_ref[...] = chosen

    made = nn(chosen.astype(bf16), ada_ref[...])
    for g in range(part_ref.shape[3]):
        part_ref[:, :, :, g, :] = made[:, g * LANES : (g + 1) * LANES].reshape(n_z, 2, 2, LANES)
    at = 1 + n_z
    step([link(part_ref.at[:, :, 1 - c], cgot_ref, core, at)])
    cgot_ref[...] += part_ref[:, :, c]
    step([link(cgot_ref.at[:, 1 - x], xgot_ref, beside, at + 1)])
    xgot_ref[...] += cgot_ref[:, x]
    step(
        [
            link(xgot_ref.at[lax.rem(z + s + 1, n_z)], zgot_ref.at[s], to, at + 2 + s)
            for s, to in enumerate(lines)
        ]
    )
    total = xgot_ref[z] + bias_ref[...]
    for s in range(n_z - 1):
        total += zgot_ref[s]
    half_ref[...] = total
    at += n_z + 1
    step([link(half_ref, other_ref, across, at)])
    halves = []
    for ref in (half_ref, other_ref):
        values = ref[...]
        halves.append(
            [
                jnp.concatenate(
                    [values[j * per_mod + i : j * per_mod + i + 1, :] for i in range(per_mod)],
                    axis=1,
                )[:, :width]
                for j in range(n_mods)
            ]
        )
    mods_ref[...] = jnp.zeros_like(mods_ref)
    for j, (own, oth) in enumerate(zip(*halves)):
        first = jnp.where(side == 0, own, oth)
        second = jnp.where(side == 0, oth, own)
        mods_ref[pl.ds(j, 1), :] = jnp.concatenate([first, second], axis=1)

    def input_tile(r):
        made = normed_ref[r, :] * (1.0 + mods_ref[1:2, :]) + mods_ref[0:1, :]
        aown_ref[r, :] = made.astype(bf16)

    loop(input_tile)

    def grad_tile(i, carry):
        r = pl.ds(pl.multiple_of(i * tile, tile), tile)
        made = (mods_ref[5:6, :] * out_ref[r, :]).astype(bf16)
        gown_ref[r, :] = made
        made = made.astype(f32)
        most = jnp.max(jnp.abs(made), axis=0, keepdims=True)
        return carry[0] + jnp.sum(made, axis=0, keepdims=True), jnp.maximum(carry[1], most)

    none = (jnp.zeros((1, depth), f32),) * 2
    g_sum, g_top = lax.fori_loop(0, rows // tile, grad_tile, none)
    gsum_ref[...] = g_sum

    def largest(j):
        return jnp.max(jnp.abs(mods_ref[j : j + 1, :]), axis=1, keepdims=True)

    tops = (
        jnp.max(g_top, axis=1, keepdims=True),
        largest(4) + largest(3),
        largest(1) + largest(0),
    )
    row = lax.broadcasted_iota(jnp.int32, top_ref.shape, 0)
    best = jnp.zeros(top_ref.shape, f32)
    for j, top in enumerate(tops):
        best = jnp.where(row == j, top, best)
    top_ref[...] = best
    normed_link.wait()


def open_part(cond, ada, bias, tokens, out_grad, width):
    n_dp = lax.axis_size("dp")
    n_z = n_dp // 4
    rows, depth = tokens.shape
    block = ada.shape[0]
    groups = bias.shape[0]
    n_links = 4 + 2 * n_z
    vmem = pl.BlockSpec(memory_space=pltpu.VMEM)
    return pl.pallas_call(
        functools.partial(open_kernel, n_dp=n_dp, n_mods=6, width=width),
        out_shape=(
            jax.ShapeDtypeStruct((rows, depth), bf16),
            jax.ShapeDtypeStruct((rows, depth), bf16),
            jax.ShapeDtypeStruct((rows, depth), bf16),
            jax.ShapeDtypeStruct((8, depth), f32),
            jax.ShapeDtypeStruct((8, LANES), f32),
            jax.ShapeDtypeStruct((n_dp, block), f32),
            jax.ShapeDtypeStruct((1, depth), f32),
        ),
        in_specs=[vmem] * 5,
        out_specs=[vmem] * 7,
        scratch_shapes=[
            pltpu.VMEM((n_z, 2, 2, depth // LANES, LANES), f32),
            pltpu.VMEM((n_z, 2, 2, groups, LANES), f32),
            pltpu.VMEM((n_z, 2, groups, LANES), f32),
            pltpu.VMEM((n_z, groups, LANES), f32),
            pltpu.VMEM((n_z - 1, groups, LANES), f32),
            pltpu.VMEM((groups, LANES), f32),
            pltpu.VMEM((groups, LANES), f32),
            pltpu.VMEM((rows, depth), f32),
            pltpu.VMEM((rows, depth), bf16),
            pltpu.SemaphoreType.DMA((n_links,)),
            pltpu.SemaphoreType.DMA((n_links,)),
        ],
        cost_estimate=pl.CostEstimate(
            flops=40 * 10**9, bytes_accessed=20 * 10**6, transcendentals=0
        ),
        compiler_params=pltpu.CompilerParams(
            collective_id=3, has_side_effects=True, vmem_limit_bytes=32 * 2**20
        ),
    )(cond, ada, bias, tokens, out_grad)


def middle_kernel(
    hsend_ref, came_ref, scale_ref, gate_ref, top_ref,
    gown_any, goth_any, mown_any, moth_any, aown_any, aoth_any, pown_any, poth_any,
    hown_any, mid_any, out_any, branch_any, proj_any,
    grad_ref, zown_ref, zoth_ref, goown_ref, gooth_ref, sum_ref, colsum_ref,
    own2_ref, code2_ref, mine1_ref, code1_ref, bound_ref,
    left_ref, right_ref, hown_ref, mid_ref, branch_ref, proj_ref, turned_ref,
    csend_ref, cgot_ref, mine2_ref, xsend_ref, xgot_ref, hgot_ref, zgot_ref, zsend_ref,
    tsend_ref, tgot_ref,
    load_sem, left_sem, right_sem, send_sem, recv_sem,
    *, n_dp, steps, tokens,
):
    (me, z, x, c), across, core, beside, lines = peers(n_dp)
    n_z = n_dp // 4
    rows, depth = hown_ref.shape
    block, hidden = own2_ref.shape
    chunk = hidden // steps
    tile = min(rows, 128)
    link = linker(send_sem, recv_sem)

    def left_loads(pieces):
        return [
            pltpu.make_async_copy(piece, left_ref.at[j], left_sem.at[j])
            for j, piece in enumerate(pieces)
        ]

    def right_loads(pieces, k):
        at = pl.ds(k * chunk, chunk)
        return [
            pltpu.make_async_copy(piece.at[:, at], right_ref.at[k % 2, j], right_sem.at[k % 2, j])
            for j, piece in enumerate(pieces)
        ]

    loads = [
        pltpu.make_async_copy(source, target, load_sem.at[k])
        for k, (source, target) in enumerate(
            (
                (hown_any, hown_ref),
                (mid_any, mid_ref),
                (out_any, grad_ref),
                (branch_any, branch_ref),
                (proj_any, proj_ref),
            )
        )
    ]

    def start(copies):
        for copy in copies:
            copy.start()

    def wait(copies):
        for copy in copies:
            copy.wait()

    start(left_loads((gown_any, goth_any)))
    for k in range(min(2, steps)):
        start(right_loads((aown_any, aoth_any), k))
    start(loads)
    greet([across, core, beside] + lines)

    first_top = 2 + 3 * steps

    def top_links(k):
        if k < 3:
            return [link(tsend_ref.at[k], tgot_ref.at[k], (across, core, beside)[k], first_top + k)]
        return [
            link(tsend_ref.at[3], tgot_ref.at[3 + s], to, first_top + 3 + s)
            for s, to in enumerate(lines)
        ]

    def raise_top(k):
        if k == 0:
            best = top_ref[...]
        else:
            wait(top_links(k - 1))
            best = jnp.maximum(tsend_ref[k - 1], tgot_ref[k - 1])
        tsend_ref[k] = best
        start(top_links(k))

    def settle_bounds():
        wait(top_links(3))
        best = tsend_ref[3]
        for s in range(n_z - 1):
            best = jnp.maximum(best, tgot_ref[3 + s])
        norm = 1.01 * depth**0.5
        g_bound, m_norm = best[0:1, :] * 1.01, (best[1:2, :] + 1.0) * norm
        act_bound = m_norm * (0.1875 * norm) + 3.0
        gp_bound = g_bound * (1.2 * 0.09375 * depth)
        bound_ref[...] = jnp.zeros_like(bound_ref)
        bound_ref[0:1, :] = g_bound * act_bound * (1.01 * tokens) + 1e-30
        bound_ref[1:2, :] = m_norm * gp_bound * (1.01 * tokens) + 1e-30

    code2_ref[...] = jnp.zeros_like(code2_ref)
    zsend_ref[...] = jnp.zeros_like(zsend_ref)
    raise_top(0)
    early = came_ref.shape[0]
    half = link(hsend_ref, hgot_ref, across, 0)
    half.start()

    def product(which, slot):
        made = nn(turned_ref[which, :, pl.ds(0, rows)], right_ref[slot, 0])
        made += nn(turned_ref[which, :, pl.ds(rows, rows)], right_ref[slot, 1])
        return made.reshape(csend_ref.shape[1:])

    def core_link(w, k):
        return link(csend_ref.at[k % 2], cgot_ref.at[w, k], core, 2 + w * steps + k)

    def x_link(k):
        return link(xsend_ref.at[k], xgot_ref.at[k], beside, 2 + 2 * steps + k)

    def rounds(w, pieces, use, meanwhile=lambda: None):
        for k in range(steps + 1):
            if k < steps:
                wait(right_loads(pieces, k))
                if k >= 2:
                    core_link(w, k - 2).wait_send()
                csend_ref[k % 2] = product(1 - c, k % 2)
                core_link(w, k).start()
            if k == 0:
                made = meanwhile()
            if w == 0 and k < 2:
                raise_top(k + 2)
            if w == 0 and k == 1:
                settle_bounds()
            if k > 0:
                j = k - 1
                core_link(w, j).wait_recv()
                cgot_ref[w, j] += product(c, j % 2)
                use(j)
                if j + 2 < steps:
                    start(right_loads(pieces, j + 2))
        for k in range(max(steps - 2, 0), steps):
            core_link(w, k).wait_send()
        return made

    def use_two(j):
        at = pl.ds(j * chunk, chunk)
        mine2_ref[:, :, at] = cgot_ref[0, j, x]
        away = cgot_ref[0, j, 1 - x].reshape(n_z * block, chunk)
        xsend_ref[j] = encode(away, bound_ref[0:1, 0:1])
        x_link(j).start()

    z_links = [
        link(zsend_ref.at[s], zgot_ref.at[s], to, first_top + n_z + 2 + s)
        for s, to in enumerate(lines)
    ]

    def pass_two(k):
        x_link(k).wait()
        at = pl.ds(k * chunk, chunk)
        came = decode(xgot_ref[k], bound_ref[0:1, 0:1]).reshape(n_z, block, chunk)
        mine2_ref[:, :, at] += came
        own2_ref[:, at] = mine2_ref[z, :, at]
        for s in range(n_z - 1):
            away = encode(mine2_ref[lax.rem(z + s + 1, n_z), :, at], bound_ref[0:1, 0:1])
            if k == 0:
                zsend_ref[s, pl.ds(0, block), :] = away
            else:
                code2_ref[s, pl.ds(0, block), pl.ds((k - 1) * chunk, chunk)] = away
        if k == 0:
            start(z_links)

    def use_one(j):
        if j == min(1, steps - 1):
            pass_two(0)
        at = pl.ds(j * chunk, chunk)
        mine1_ref[:, :, at] = cgot_ref[1, j, x]
        away = cgot_ref[1, j, 1 - x].reshape(n_z * block, chunk)
        code1_ref[:, at] = encode(away, bound_ref[1:2, 0:1])
        ones = jnp.ones((8, rows), bf16)
        colsum_ref[:, at] = nn(ones, right_ref[j % 2, 0]) + nn(ones, right_ref[j % 2, 1])

    def turn_link(at, count, k):
        r = pl.ds(at, count)
        return link(zown_ref.at[r], zoth_ref.at[r], across, k)

    turn_links = [
        turn_link(0, early, 1),
        turn_link(early, rows - early, first_top + 2 * n_z + 1),
    ]

    def norm_rows(i, carry, got_ref, skipped):
        r = pl.ds(pl.multiple_of(i * tile, tile), tile)
        rest = pl.ds(pl.multiple_of(i * tile - skipped, tile), tile)
        h = hown_ref[r, :] + got_ref[rest, :].astype(f32)
        normed, rscale = normalize(mid_ref[r, :])
        grad = grad_ref[r, :] + norm_back(h * (1.0 + scale_ref[...]), normed, rscale)
        grad_ref[r, :] = grad
        turned = (gate_ref[...] * grad).astype(bf16)
        zown_ref[r, :] = turned
        parts = (grad * branch_ref[r, :], h, h * normed, turned.astype(f32))
        added = tuple(
            total + jnp.sum(part, axis=0, keepdims=True) for total, part in zip(carry, parts)
        )
        most = jnp.max(jnp.abs(turned.astype(f32)), axis=0, keepdims=True)
        return added + (jnp.maximum(carry[4], most),)

    def norm_tile(i, carry):
        return norm_rows(i, carry, hgot_ref, early)

    def early_norm():
        wait(loads)
        totals = lax.fori_loop(
            0,
            early // tile,
            lambda i, carry: norm_rows(i, carry, came_ref, 0),
            (jnp.zeros((1, depth), f32),) * 5,
        )
        turn_links[0].start()
        return totals

    wait(left_loads((gown_any, goth_any)))
    turn_over([lambda j=j: left_ref[j] for j in range(2)], turned_ref, n_z, block)
    start(left_loads((mown_any, moth_any)))
    raise_top(1)
    totals = rounds(0, (aown_any, aoth_any), use_two, early_norm)
    for k in range(min(2, steps)):
        start(right_loads((pown_any, poth_any), k))

    half.wait()
    totals = lax.fori_loop(early // tile, rows // tile, norm_tile, totals)
    turn_links[1].start()
    sum_ref[...] = jnp.zeros_like(sum_ref)
    for j, total in enumerate(totals):
        sum_ref[pl.ds(j, 1), :] = total

    wait(left_loads((mown_any, moth_any)))
    turn_over([lambda j=j: left_ref[j] for j in range(2)], turned_ref, n_z, block)
    rounds(1, (pown_any, poth_any), use_one)
    goown_ref[...] = nn(zown_ref[...], proj_ref[...]).astype(bf16)

    for k in range(1, steps):
        pass_two(k)
    for s in range(n_z - 1):
        z_links[s].wait()
        came = decode(zgot_ref[s, pl.ds(0, block), :], bound_ref[0:1, 0:1])
        own2_ref[:, pl.ds(0, chunk)] += came
    wait(turn_links)
    gooth_ref[...] = nn(zoth_ref[...], proj_ref[...]).astype(bf16)
    most = jnp.max(jnp.abs(zoth_ref[...].astype(f32)), axis=0, keepdims=True)
    sum_ref[4:5, :] = jnp.maximum(sum_ref[4:5, :], most)


def middle_part(
    h_send, h_came, scale, gate, tops, g_own, g_oth, m_own, m_oth, act_own, act_oth, gp_own, gp_oth,
    h_own, middle, out_grad, branch, w_proj, block,
):
    n_dp = lax.axis_size("dp")
    n_z = n_dp // 4
    rows, depth = middle.shape
    hidden = act_own.shape[1]
    pad = w_proj.shape[1]
    steps = 3 if hidden % (3 * LANES) == 0 else 1
    chunk = hidden // steps
    tall = -(-block // 16) * 16
    vmem = pl.BlockSpec(memory_space=pltpu.VMEM)
    n_links = 2 + 3 * steps + 2 * n_z + 2
    later = max(steps - 1, 1) * chunk
    return pl.pallas_call(
        functools.partial(middle_kernel, n_dp=n_dp, steps=steps, tokens=float(n_dp * SEQ)),
        out_shape=(
            jax.ShapeDtypeStruct((rows, depth), f32),
            jax.ShapeDtypeStruct((rows, depth), bf16),
            jax.ShapeDtypeStruct((rows, depth), bf16),
            jax.ShapeDtypeStruct((rows, pad), bf16),
            jax.ShapeDtypeStruct((rows, pad), bf16),
            jax.ShapeDtypeStruct((8, depth), f32),
            jax.ShapeDtypeStruct((8, hidden), f32),
            jax.ShapeDtypeStruct((block, hidden), f32),
            jax.ShapeDtypeStruct((n_z - 1, tall, later), bf16),
            jax.ShapeDtypeStruct((n_z, block, hidden), f32),
            jax.ShapeDtypeStruct((n_z * block, hidden), bf16),
            jax.ShapeDtypeStruct((8, LANES), f32),
        ),
        in_specs=[vmem] * 5 + [pl.BlockSpec(memory_space=pl.ANY)] * 13,
        out_specs=[vmem] * 12,
        scratch_shapes=[
            pltpu.VMEM((2, rows, depth), bf16),
            pltpu.VMEM((2, 2, rows, chunk), bf16),
            pltpu.VMEM((rows, depth), f32),
            pltpu.VMEM((rows, depth), f32),
            pltpu.VMEM((rows, depth), f32),
            pltpu.VMEM(w_proj.shape, bf16),
            pltpu.VMEM((2, depth // 2, 2 * rows), bf16),
            pltpu.VMEM((2, 2, n_z, block, chunk), f32),
            pltpu.VMEM((2, steps, 2, n_z, block, chunk), f32),
            pltpu.VMEM((n_z, block, hidden), f32),
            pltpu.VMEM((steps, n_z * block, chunk), bf16),
            pltpu.VMEM((steps, n_z * block, chunk), bf16),
            pltpu.VMEM(h_send.shape, bf16),
            pltpu.VMEM((n_z - 1, tall, chunk), bf16),
            pltpu.VMEM((n_z - 1, tall, chunk), bf16),
            pltpu.VMEM((4, 8, LANES), f32),
            pltpu.VMEM((n_z + 2, 8, LANES), f32),
            pltpu.SemaphoreType.DMA((5,)),
            pltpu.SemaphoreType.DMA((2,)),
            pltpu.SemaphoreType.DMA((2, 2)),
            pltpu.SemaphoreType.DMA((n_links,)),
            pltpu.SemaphoreType.DMA((n_links,)),
        ],
        cost_estimate=pl.CostEstimate(
            flops=60 * 10**9, bytes_accessed=100 * 10**6, transcendentals=0
        ),
        compiler_params=pltpu.CompilerParams(
            collective_id=1, has_side_effects=True, vmem_limit_bytes=62 * 2**20
        ),
    )(
        h_send, h_came, scale.reshape(1, -1), gate.reshape(1, -1), tops, g_own, g_oth, m_own, m_oth,
        act_own, act_oth, gp_own, gp_oth, h_own, middle, out_grad, branch, w_proj,
    )


def attend_back_kernel(
    own_ref, oth_ref, gown_ref, goth_ref, lown_ref, loth_ref, bound_ref, own2_ref,
    out_any, code2_any, code1_any, mine1_any,
    down_ref, doth_ref, branch_ref, total2_ref, own1_ref, next1_ref,
    dk_ref, dv_ref, out_ref, code2_ref, got2_ref, code1_ref, got1_ref, mine1_ref, zsend_ref, zgot_ref,
    load_sem, send_sem, recv_sem,
    *, n_dp, chunk, heads, block, pad, scale,
):
    (me, z, x, c), across, core, beside, lines = peers(n_dp)
    n_z = n_dp // 4
    link = linker(send_sem, recv_sem)
    loads = [
        pltpu.make_async_copy(source, target, load_sem.at[k])
        for k, (source, target) in enumerate(
            (
                (out_any, out_ref),
                (code2_any, code2_ref),
                (code1_any, code1_ref),
                (mine1_any, mine1_ref),
            )
        )
    ]
    for load in loads:
        load.start()
    greet([across, beside] + lines)
    for load in loads:
        load.wait()
    depth, hidden = own1_ref.shape
    first, later = pl.ds(0, chunk), pl.ds(chunk, hidden - chunk)
    branch = link(out_ref, branch_ref, across, 0)
    z_links = [link(code2_ref.at[s], got2_ref.at[s], to, 1 + s) for s, to in enumerate(lines)]
    x_links = [
        link(code1_ref.at[:, at], got1_ref.at[:, at], beside, n_z + k)
        for k, at in enumerate((first, later))
    ]
    next_links = [
        link(zsend_ref.at[s], zgot_ref.at[s], to, n_z + 2 + s) for s, to in enumerate(lines)
    ]
    for one in [branch] + x_links + z_links:
        one.start()
    zsend_ref[...] = jnp.zeros_like(zsend_ref)
    next1_ref[...] = jnp.zeros_like(next1_ref)

    def pass_one(k, at, target):
        x_links[k].wait()
        came = decode(got1_ref[:, at], bound_ref[1:2, 0:1])
        mine1_ref[:, :, at] += came.reshape(n_z, depth, came.shape[1])
        own1_ref[:, at] = mine1_ref[z, :, at]
        for s in range(n_z - 1):
            away = mine1_ref[lax.rem(z + s + 1, n_z), :, at]
            target[s, pl.ds(0, depth), :] = encode(away, bound_ref[1:2, 0:1])

    rows = own_ref.shape[0]
    factor = scale * LOG2E
    down_ref[...] = jnp.zeros_like(down_ref)
    doth_ref[...] = jnp.zeros_like(doth_ref)

    def one_head(h, carry):
        at, first = window(h)
        dk_ref[...] = jnp.zeros_like(dk_ref)
        dv_ref[...] = jnp.zeros_like(dv_ref)
        keys = [ref[:, pl.ds(pad + at, 2 * LANES)] for ref in (own_ref, oth_ref)]
        values = [ref[:, pl.ds(2 * pad + at, 2 * LANES)] for ref in (own_ref, oth_ref)]
        parts = ((own_ref, gown_ref, lown_ref, down_ref), (oth_ref, goth_ref, loth_ref, doth_ref))
        for q_ref, g_ref, l_ref, d_ref in parts:

            def one_block(i, inner):
                r = pl.ds(pl.multiple_of(i * block, block), block)
                mask = lane_mask((block, 2 * LANES), first)
                q = q_ref[r, pl.ds(at, 2 * LANES)]
                q = jnp.where(mask, q, jnp.zeros_like(q))
                g = g_ref[r, pl.ds(at, 2 * LANES)]
                g = jnp.where(mask, g, jnp.zeros_like(g))
                lse = l_ref[pl.ds(h, 1), r]
                probs = [jnp.exp2(nt(k, q) * factor - lse) for k in keys]
                grad_p = [nt(v, g) for v in values]
                delta = sum(jnp.sum(p * d, axis=0, keepdims=True) for p, d in zip(probs, grad_p))
                grad_s = [(p * (d - delta)).astype(bf16) for p, d in zip(probs, grad_p)]
                dq = sum(tn(k, s) for k, s in zip(keys, grad_s)).T * scale
                d_ref[r, pl.ds(at, 2 * LANES)] = jnp.where(
                    mask, dq.astype(bf16), d_ref[r, pl.ds(at, 2 * LANES)]
                )
                for j in range(2):
                    dk_ref[j] += nn(grad_s[j], q)
                    dv_ref[j] += nn(probs[j].astype(bf16), g)
                return inner

            lax.fori_loop(0, rows // block, one_block, 0)
        mask = lane_mask((rows, 2 * LANES), first)
        for j, d_ref in enumerate((down_ref, doth_ref)):
            for lane, new in ((pad, dk_ref[j] * scale), (2 * pad, dv_ref[j])):
                d_ref[:, pl.ds(lane + at, 2 * LANES)] = jnp.where(
                    mask, new.astype(bf16), d_ref[:, pl.ds(lane + at, 2 * LANES)]
                )
        return carry

    lax.fori_loop(0, heads // 2, one_head, 0)
    pass_one(0, first, zsend_ref)
    for one in next_links:
        one.start()
    lax.fori_loop(heads // 2, heads, one_head, 0)
    pass_one(1, later, next1_ref)
    branch.wait()
    total2_ref[...] = own2_ref[...]
    for s in range(n_z - 1):
        z_links[s].wait()
        total2_ref[:, later] += decode(got2_ref[s, pl.ds(0, depth), :], bound_ref[0:1, 0:1])
        next_links[s].wait()
        own1_ref[:, first] += decode(zgot_ref[s, pl.ds(0, depth), :], bound_ref[1:2, 0:1])


def attend_back(
    own, oth, gown, goth, lown, loth, bounds, own2, b_send, code2, code1, mine1, heads, pad
):
    n_dp = lax.axis_size("dp")
    n_z, depth, hidden = mine1.shape
    chunk = hidden - code2.shape[2]
    n_links = 2 * n_z + 1
    rows = own.shape[0]
    vmem = pl.BlockSpec(memory_space=pltpu.VMEM)
    flops = 10 * heads * 4 * rows * rows * 2 * LANES
    return pl.pallas_call(
        functools.partial(
            attend_back_kernel, n_dp=n_dp, chunk=chunk, heads=heads, block=min(rows, 512), pad=pad, scale=HEAD_DIM**-0.5
        ),
        out_shape=(jax.ShapeDtypeStruct((rows, 3 * pad), bf16),) * 2
        + (
            jax.ShapeDtypeStruct(b_send.shape, b_send.dtype),
            jax.ShapeDtypeStruct((depth, hidden), f32),
            jax.ShapeDtypeStruct((depth, hidden), f32),
            jax.ShapeDtypeStruct(code2.shape, code2.dtype),
        ),
        in_specs=[vmem] * 8 + [pl.BlockSpec(memory_space=pl.ANY)] * 4,
        out_specs=[vmem] * 6,
        scratch_shapes=[pltpu.VMEM((2, rows, 2 * LANES), f32)] * 2
        + [
            pltpu.VMEM(b_send.shape, b_send.dtype),
            pltpu.VMEM(code2.shape, bf16),
            pltpu.VMEM(code2.shape, bf16),
            pltpu.VMEM(code1.shape, bf16),
            pltpu.VMEM(code1.shape, bf16),
            pltpu.VMEM(mine1.shape, f32),
            pltpu.VMEM(code2.shape[:2] + (chunk,), bf16),
            pltpu.VMEM(code2.shape[:2] + (chunk,), bf16),
            pltpu.SemaphoreType.DMA((4,)),
            pltpu.SemaphoreType.DMA((n_links,)),
            pltpu.SemaphoreType.DMA((n_links,)),
        ],
        cost_estimate=pl.CostEstimate(
            flops=flops, bytes_accessed=16 * rows * pad * 2, transcendentals=heads * rows * rows * 4
        ),
        compiler_params=pltpu.CompilerParams(
            collective_id=2, has_side_effects=True, vmem_limit_bytes=60 * 2**20
        ),
    )(own, oth, gown, goth, lown, loth, bounds, own2, b_send, code2, code1, mine1)


def close_kernel(
    aown_ref, aoth_ref, down_ref, doth_ref, mine_ref, other_ref, extra_ref, cond_ref, scale_ref,
    tops_ref, zsum_ref, fcbound_ref, fcown_ref, fccode_ref,
    w_any, noth_any, x_any, mid_any, zown_any, zoth_any, oown_any, ooth_any, ada_any,
    tokens_ref, gqkv_ref, gproj_ref, gada_ref, total_ref, etotal_ref, row_ref, fctotal_ref,
    w_ref, noth_ref, x_ref, mid_ref, z_ref, o_ref, ada_ref,
    turned_ref, part_ref, got_ref, xsend_ref, xgot_ref, zsend_ref, zgot_ref,
    hsend_ref, hgot_ref, hown_ref, fcgot_ref,
    rows_ref, rgot_ref, all_ref, cpart_ref, cswap_ref, parts_ref, bound_ref, bgot_ref, esend_ref, egot_ref,
    load_sem, send_sem, recv_sem,
    *, n_dp, n_mods, n_shared, pad,
):
    (me, z, x, c), across, core, beside, lines = peers(n_dp)
    n_z = n_dp // 4
    side = lax.axis_index("tensor")
    loads = [
        pltpu.make_async_copy(source, target, load_sem.at[k])
        for k, (source, target) in enumerate(
            (
                (zown_any, z_ref.at[0]),
                (zoth_any, z_ref.at[1]),
                (oown_any, o_ref.at[0]),
                (ooth_any, o_ref.at[1]),
                (w_any, w_ref),
                (noth_any, noth_ref),
                (x_any, x_ref),
                (mid_any, mid_ref),
                (ada_any, ada_ref),
            )
        )
    ]
    for load in loads:
        load.start()
    greet([across, core, beside] + lines)

    rows, depth = aown_ref.shape
    width = mine_ref.shape[1]
    block = got_ref.shape[3]
    n_parts = part_ref.shape[0]
    tile = min(rows, 128)

    link = linker(send_sem, recv_sem)

    def core_link(k):
        return link(part_ref.at[k], got_ref.at[k], core, k)

    def x_link(k):
        return link(xsend_ref.at[k], xgot_ref.at[k], beside, n_parts + k)

    def z_link(k, s):
        at = 2 * n_parts + k * (n_z - 1) + s
        return link(zsend_ref.at[k, s], zgot_ref.at[k, s], lines[s], at)

    n_sums = (n_z + 1) * n_parts
    middle = rows // 2
    half = [
        link(hsend_ref.at[pl.ds(at, middle)], hgot_ref.at[pl.ds(at, middle)], across, k)
        for at, k in ((0, n_sums), (middle, n_sums + 7 + 4 * n_z))
    ]
    swap_rows = link(rows_ref.at[1], rgot_ref, across, n_sums + 1)
    swap_part = link(cpart_ref, cswap_ref, across, n_sums + 2)
    core_bound = link(bound_ref.at[0], bgot_ref.at[0], core, n_sums + 3)
    x_bound = link(bound_ref.at[1], bgot_ref.at[1], beside, n_sums + 4)
    z_bounds = [
        link(bound_ref.at[2], bgot_ref.at[2 + s], lines[s], n_sums + 5 + s) for s in range(n_z - 1)
    ]

    first_extra = n_sums + 8 + 4 * n_z
    fc_links = [
        link(fccode_ref.at[s], fcgot_ref.at[s], to, n_sums + 7 + 3 * n_z + s)
        for s, to in enumerate(lines)
    ]
    for one in fc_links:
        one.start()

    def spread(ref, first):
        return (
            [link(ref.at[z, x, c], ref.at[z, x, c], core, first)],
            [link(ref.at[z, x], ref.at[z, x], beside, first + 1)],
            [link(ref.at[z], ref.at[z], to, first + 2 + s) for s, to in enumerate(lines)],
        )

    def start(links):
        for one in links:
            one.start()

    def wait(links):
        for one in links:
            one.wait()

    def largest(ref):
        return jnp.max(jnp.abs(ref[...].astype(f32)))

    def product(t, which, right_own, right_oth):
        made = nn(turned_ref[t, which, :, pl.ds(0, rows)], right_own)
        made += nn(turned_ref[t, which, :, pl.ds(rows, rows)], right_oth)
        return made.reshape(got_ref.shape[1:])

    def columns(k):
        at = pl.ds(pl.multiple_of(k * pad, LANES), pad)
        return down_ref[:, at], doth_ref[:, at]

    def to_core(k, right, t=0):
        part_ref[k] = product(t, 1 - c, *right)
        core_link(k).start()

    def to_beside(k, right, t=0):
        core_link(k).wait_recv()
        got_ref[k] += product(t, c, *right)
        away = got_ref[k, 1 - x].reshape(n_z * block, pad)
        xsend_ref[k] = encode(away, bound_ref[1, 0:1, 0:1])
        x_link(k).start()

    def to_lines(k):
        x_link(k).wait_recv()
        came = decode(xgot_ref[k], bgot_ref[1, 0:1, 0:1])
        got_ref[k, x] += came.reshape(n_z, block, pad)
        for s in range(n_z - 1):
            away = got_ref[k, x, lax.rem(z + s + 1, n_z)]
            zsend_ref[k, s, pl.ds(0, block), :] = encode(away, bound_ref[2, 0:1, 0:1])
            z_link(k, s).start()

    def loop(count, step):
        def body(k, carry):
            step(k)
            return carry

        lax.fori_loop(0, count, body, 0)

    def extra_links(k):
        if k < 3:
            return [link(esend_ref.at[k], egot_ref.at[k], (across, core, beside)[k], first_extra + k)]
        return [
            link(esend_ref.at[3], egot_ref.at[3 + s], to, first_extra + 3 + s)
            for s, to in enumerate(lines)
        ]

    def add_extra(k):
        if k == 0:
            total = extra_ref[...]
        else:
            wait(extra_links(k - 1))
            came = egot_ref[k - 1]
            if k == 1:
                row = lax.broadcasted_iota(jnp.int32, came.shape, 0)
                came = jnp.where(row >= came.shape[0] - n_shared, came, 0.0)
            total = esend_ref[k - 1] + came
        esend_ref[k] = total
        start(extra_links(k))

    add_extra(0)
    norm = 1.01 * depth**0.5
    a_bound = (tops_ref[2:3, 0:1] + 1.0) * norm
    v_bound = a_bound * (0.1875 * norm) + 1.25
    z_top = jnp.max(zsum_ref[4:5, :], axis=1, keepdims=True)
    most = a_bound * jnp.maximum(largest(down_ref), largest(doth_ref)) + 1.01 * v_bound * z_top
    most = most * (1.02 * 2 * rows) + 1e-30
    bound_ref[0] = jnp.broadcast_to(most, bound_ref.shape[1:])
    core_bound.start()
    zsend_ref[...] = jnp.zeros_like(zsend_ref)
    turn_over((lambda: aown_ref[...], lambda: aoth_ref[...]), turned_ref.at[0], n_z, block)
    add_extra(1)
    core_bound.wait()
    bound_ref[1] = bound_ref[0] + bgot_ref[0]
    x_bound.start()
    loop(3, lambda k: to_core(k, columns(k)))
    add_extra(2)
    x_bound.wait()
    bound_ref[2] = bound_ref[1] + bgot_ref[1]
    start(z_bounds)
    to_beside(0, columns(0))
    add_extra(3)
    to_beside(1, columns(1))

    wait(loads[4:7])

    def summed(carry, h, normed):
        return (
            carry[0] + jnp.sum(h, axis=0, keepdims=True),
            carry[1] + jnp.sum(h * normed, axis=0, keepdims=True),
        )

    def h_other(i, carry):
        r = pl.ds(pl.multiple_of(i * tile, tile), tile)
        h = nt(doth_ref[r, :], w_ref[...])
        hsend_ref[r, :] = h.astype(bf16)
        return summed(carry, h, noth_ref[r, :].astype(f32))

    late = lax.fori_loop(0, rows // tile, h_other, (jnp.zeros((1, depth), f32),) * 2)

    def h_own(i, carry):
        r = pl.ds(pl.multiple_of(i * tile, tile), tile)
        h = nt(down_ref[r, :], w_ref[...])
        hown_ref[r, :] = h
        return summed(carry, h, normalize(x_ref[r, :])[0])

    late = lax.fori_loop(0, rows // tile, h_own, late)
    rows_ref[0] = mine_ref[...]
    rows_ref[1] = other_ref[...]
    for j, values in enumerate(late):
        low_half, high_half = values[:, :width], values[:, width:]
        rows_ref[0, pl.ds(j, 1), :] = jnp.where(side == 0, low_half, high_half)
        rows_ref[1, pl.ds(j, 1), :] = jnp.where(side == 0, high_half, low_half)
    swap_rows.start()
    half[0].start()
    ones = jnp.ones((8, rows), bf16)
    d_sums = nn(ones, down_ref[...]) + nn(ones, doth_ref[...])
    for j, at in ((0, 0), (1, 2 * pad)):
        rows_ref[0, pl.ds(n_mods + j, 1), :] = d_sums[:1, at : at + width]
    to_lines(0)

    swap_rows.wait()
    row = lax.broadcasted_iota(jnp.int32, mine_ref.shape, 0)
    all_ref[z, x, c] = rows_ref[0] + jnp.where(row < n_mods, rgot_ref[...], 0.0)
    along = spread(all_ref, n_sums + 4 + n_z)
    start(along[0])
    wait(loads[:4])
    turn_over((lambda: z_ref[0], lambda: z_ref[1]), turned_ref.at[1], n_z, block)
    last = n_parts - 1
    wait(along[0])
    start(along[1])
    to_core(last, (o_ref[0], o_ref[1]), 1)
    to_beside(2, columns(2))
    wait(along[1])
    start(along[2])
    to_beside(last, (o_ref[0], o_ref[1]), 1)
    to_lines(1)
    wait(extra_links(3))
    total = esend_ref[3]
    for s in range(n_z - 1):
        total += egot_ref[3 + s]
    etotal_ref[...] = total
    wait(loads[7:])
    wait(along[2])
    everything = all_ref[...].reshape((n_dp,) + mine_ref.shape)
    total_ref[...] = jnp.sum(everything, axis=0)
    cond = cond_ref[...]
    part = jnp.zeros(cond.shape, f32)
    for j in range(n_mods):
        part += lax.dot_general(
            everything[:, j, :], ada_ref[j].astype(f32), (((1,), (1,)), ((), ())),
            precision=highest_precision_mode, preferred_element_type=f32,
        )
    cpart_ref[...] = part
    swap_part.start()
    half[1].start()
    for j in range(n_mods):
        gada_ref[j] = lax.dot_general(
            cond, everything[:, j, :], (((0,), (0,)), ((), ())),
            precision=highest_precision_mode, preferred_element_type=f32,
        )
    to_lines(2)
    swap_part.wait()
    whole = cpart_ref[...] + cswap_ref[...]
    parts_ref[z, x, c] = whole
    along = spread(parts_ref, n_sums + 6 + 2 * n_z)
    start(along[0])
    half[0].wait_recv()
    wait(along[0])
    start(along[1])

    def last_norm(i):
        r = pl.ds(pl.multiple_of(i * tile, tile), tile)
        h = hown_ref[r, :] + hgot_ref[r, :].astype(f32)
        normed, rscale = normalize(x_ref[r, :])
        tokens_ref[r, :] = mid_ref[r, :] + norm_back(h * (1.0 + scale_ref[...]), normed, rscale)

    wait(along[1])
    start(along[2])
    to_lines(last)
    loop(middle // tile, last_norm)
    half[1].wait_recv()
    loop(middle // tile, lambda i: last_norm(i + middle // tile))
    wait(along[2])
    for p in range(n_dp):
        row_ref[pl.ds(p, 1), :] = parts_ref[p // 4, (p // 2) % 2, p % 2, pl.ds(me, 1), :]

    wait(z_bounds)

    def finish(k):
        total = got_ref[k, x, z]
        for s in range(n_z - 1):
            z_link(k, s).wait_recv()
            total += decode(zgot_ref[k, s, pl.ds(0, block), :], bgot_ref[2 + s, 0:1, 0:1])
        return total

    for k in range(3):
        gqkv_ref[k] = finish(k)[:, :width]
    gproj_ref[...] = finish(last)[:, :width]
    for one in half:
        one.wait_send()
    wait(fc_links)
    fctotal_ref[...] = fcown_ref[...]
    later = fccode_ref.shape[2]
    at = pl.ds(fcown_ref.shape[1] - later, later)
    for s in range(n_z - 1):
        fctotal_ref[:, at] += decode(fcgot_ref[s, pl.ds(0, block), :], fcbound_ref[1:2, 0:1])

    def sent(k):
        core_link(k).wait_send()
        x_link(k).wait_send()
        for s in range(n_z - 1):
            z_link(k, s).wait_send()

    loop(n_parts, sent)


def close(
    a_own, a_oth, d_own, d_oth, mine, other, extra, cond, scale, tops, z_sums, fc_bounds, fc_own, fc_code,
    w_qkv, n_oth, tokens, mid_grad,
    z_own, z_oth, o_own, o_oth, ada, n_shared,
):
    n_dp = lax.axis_size("dp")
    n_z = n_dp // 4
    n_mods, block, width = ada.shape
    rows, depth = tokens.shape
    pad = o_own.shape[1]
    n_rows = mine.shape[0]
    n_parts = 4
    n_links = (n_z + 1) * n_parts + 10 + 5 * n_z
    tall = -(-block // 16) * 16
    vmem = pl.BlockSpec(memory_space=pltpu.VMEM)
    return pl.pallas_call(
        functools.partial(close_kernel, n_dp=n_dp, n_mods=n_mods, n_shared=n_shared, pad=pad),
        out_shape=(
            jax.ShapeDtypeStruct((rows, depth), f32),
            jax.ShapeDtypeStruct((3, block, width), f32),
            jax.ShapeDtypeStruct((block, width), f32),
            jax.ShapeDtypeStruct((n_mods, block, width), f32),
            jax.ShapeDtypeStruct((n_rows, width), f32),
            jax.ShapeDtypeStruct(extra.shape, f32),
            jax.ShapeDtypeStruct((n_dp, block), f32),
            jax.ShapeDtypeStruct(fc_own.shape, f32),
        ),
        in_specs=[vmem] * 14 + [pl.BlockSpec(memory_space=pl.ANY)] * 9,
        out_specs=[vmem] * 8,
        scratch_shapes=[
            pltpu.VMEM(w_qkv.shape, bf16),
            pltpu.VMEM((rows, depth), bf16),
            pltpu.VMEM((rows, depth), f32),
            pltpu.VMEM((rows, depth), f32),
            pltpu.VMEM((2, rows, depth), bf16),
            pltpu.VMEM((2, rows, pad), bf16),
            pltpu.VMEM(ada.shape, bf16),
            pltpu.VMEM((2, 2, depth // 2, 2 * rows), bf16),
            pltpu.VMEM((n_parts, 2, n_z, block, pad), f32),
            pltpu.VMEM((n_parts, 2, n_z, block, pad), f32),
            pltpu.VMEM((n_parts, n_z * block, pad), bf16),
            pltpu.VMEM((n_parts, n_z * block, pad), bf16),
            pltpu.VMEM((n_parts, n_z - 1, tall, pad), bf16),
            pltpu.VMEM((n_parts, n_z - 1, tall, pad), bf16),
            pltpu.VMEM((rows, depth), bf16),
            pltpu.VMEM((rows, depth), bf16),
            pltpu.VMEM((rows, depth), f32),
            pltpu.VMEM(fc_code.shape, bf16),
            pltpu.VMEM((2, n_rows, width), f32),
            pltpu.VMEM((n_rows, width), f32),
            pltpu.VMEM((n_z, 2, 2, n_rows, width), f32),
            pltpu.VMEM((n_dp, block), f32),
            pltpu.VMEM((n_dp, block), f32),
            pltpu.VMEM((n_z, 2, 2, n_dp, block), f32),
            pltpu.VMEM((3, 8, LANES), f32),
            pltpu.VMEM((n_z + 1, 8, LANES), f32),
            pltpu.VMEM((4,) + extra.shape, f32),
            pltpu.VMEM((n_z + 2,) + extra.shape, f32),
            pltpu.SemaphoreType.DMA((9,)),
            pltpu.SemaphoreType.DMA((n_links,)),
            pltpu.SemaphoreType.DMA((n_links,)),
        ],
        cost_estimate=pl.CostEstimate(
            flops=60 * 10**9, bytes_accessed=100 * 10**6, transcendentals=0
        ),
        compiler_params=pltpu.CompilerParams(
            collective_id=0, has_side_effects=True, vmem_limit_bytes=60 * 2**20
        ),
    )(
        a_own, a_oth, d_own, d_oth, mine, other, extra, cond, scale.reshape(1, -1), tops, z_sums,
        fc_bounds, fc_own, fc_code, w_qkv, n_oth, tokens, mid_grad, z_own, z_oth, o_own, o_oth, ada,
    )


def after(value, *others):
    return lax.optimization_barrier((value,) + others)[0]


TOP = 32768.0


def fast_body(
    latent_tokens,
    conditioning,
    out_grad,
    qkv_weight,
    qkv_bias,
    proj_weight,
    proj_bias,
    first_layer_weight,
    fc1_bias,
    fc2_weight,
    second_layer_bias,
    ada_weight,
    ada_bias,
):
    n_dp = lax.axis_size("dp")
    n_z = n_dp // 4
    me = lax.axis_index("dp")
    side = lax.axis_index("tensor")
    core, at_x, at_z = me % 2, (me // 2) % 2, me // 4
    rows, width_full = latent_tokens.shape
    block, _, width = qkv_weight.shape
    heads = width // HEAD_DIM
    pad = -(-width // LANES) * LANES

    def swap(values):
        return lax.ppermute(values, "tensor", [(0, 1), (1, 0)])

    def flip(values, bit):
        return lax.ppermute(values, "dp", [(i, i ^ bit) for i in range(n_dp)])

    def shift(values, step):
        return lax.ppermute(values, "dp", [(i, (i + 4 * step) % n_dp) for i in range(n_dp)])

    def place(pieces, spots):
        out = jnp.zeros((len(pieces),) + pieces[0].shape, pieces[0].dtype)
        for piece, spot in zip(pieces, spots):
            out = lax.dynamic_update_index_in_dim(out, piece, spot, 0)
        return out

    def pair(mine, other, bit):
        return jnp.where(bit == 0, jnp.stack([mine, other]), jnp.stack([other, mine]))

    def along_z(values):
        pieces = [values] + [shift(values, s) for s in range(1, n_z)]
        return place(pieces, [(at_z - s) % n_z for s in range(n_z)])

    def in_order(both, shape):
        both = both.reshape((2, 2, n_z) + shape)
        return jnp.transpose(both, (2, 1, 0) + tuple(range(3, both.ndim))).reshape((n_dp,) + shape)

    def gather(values):
        lines = along_z(values)
        planes = place([lines, flip(lines, 2)], [at_x, 1 - at_x])
        both = place([planes, flip(planes, 1)], [core, 1 - core])
        return in_order(both, values.shape)

    def pick(array, spot, axis):
        return lax.dynamic_index_in_dim(array, spot, axis, keepdims=False)

    def scatter_sum(values):
        parts = values.reshape((n_z, 2, 2) + values.shape[1:])
        parts = pick(parts, core, 2) + flip(pick(parts, 1 - core, 2), 1)
        parts = pick(parts, at_x, 1) + flip(pick(parts, 1 - at_x, 1), 2)
        total = pick(parts, at_z, 0)
        for s in range(1, n_z):
            total = total + shift(pick(parts, (at_z + s) % n_z, 0), s)
        return total

    def narrow(part, bound):
        return (part * (TOP / bound)).astype(jnp.float16)

    def wide(part, bound):
        return part.astype(f32) * (bound * (1.0 / TOP))

    def biggest_over_dp(values):
        values = jnp.maximum(values, flip(values, 1))
        values = jnp.maximum(values, flip(values, 2))
        others = [shift(values, s) for s in range(1, n_z)]
        return functools.reduce(jnp.maximum, others, values)

    def total_over_dp(values):
        values = values + flip(values, 1)
        values = values + flip(values, 2)
        return jnp.sum(along_z(values), axis=0)

    def halves(mine, other, axis):
        first = jnp.where(side == 0, mine, other)
        second = jnp.where(side == 0, other, mine)
        return jnp.concatenate([first, second], axis=axis)

    def pad_lanes(values):
        return jnp.pad(values, [(0, 0)] * (values.ndim - 1) + [(0, pad - width)])

    def biggest(*pieces):
        return functools.reduce(jnp.maximum, [jnp.max(jnp.abs(v.astype(f32))) for v in pieces])

    def full_weight(shard):
        return lax.all_gather(shard, "dp", axis=0, tiled=True)

    first = [
        pad_lanes(qkv_weight.astype(bf16)).reshape(block, 3 * pad),
        pad_lanes(proj_weight.astype(bf16).T),
    ]
    w_first = full_weight(jnp.concatenate(first, axis=1))
    w_qkv, w_proj = w_first[:, : 3 * pad], w_first[:, 3 * pad :]
    second = [first_layer_weight.astype(bf16), fc2_weight.astype(bf16).T]
    w_second = full_weight(jnp.concatenate(second, axis=1))
    hidden = first_layer_weight.shape[1]

    tokens = float(n_dp * SEQ)
    tiny = 1e-30
    silu_cond, silu_pull = jax.vjp(jax.nn.silu, conditioning)
    cond_tiles = lax.reduce_precision(silu_cond, 8, 7).reshape(-1, LANES)
    ada = ada_weight.astype(bf16)
    a_own, g_own, n_oth, mods, tops, cond_mine, g_sums = open_part(
        cond_tiles, pad_lanes(ada).reshape(block, 6 * pad),
        pad_lanes(ada_bias).reshape(-1, LANES), latent_tokens, out_grad, width,
    )
    shift_one, scale_one, gate_one, shift_two, scale_two, gate_two = [mods[j] for j in range(6)]
    a_oth = swap(a_own)
    g_oth = swap(after(g_own, a_own))
    norm = 1.01 * width_full**0.5
    p_bound = ((tops[2, 0] + 1.0) * (norm * 0.1875 * norm) + 1.25) * (1.01 * 0.75 * width)

    bias = pad_lanes(jnp.stack([qkv_bias[0], jnp.zeros_like(qkv_bias[0]), qkv_bias[1]]))
    bias = bias.reshape(3 * pad)
    qkv_own = (nn(a_own, w_qkv) + bias).astype(bf16)
    qkv_oth = (nn(a_oth, w_qkv) + bias).astype(bf16)
    o_oth, lse_oth = attend(qkv_oth, qkv_own, qkv_oth, heads, pad)
    p_send = narrow(nt(o_oth, w_proj), p_bound)
    part_oth = wide(swap(p_send), p_bound)
    o_own, lse_own = attend(after(qkv_own, p_send), qkv_own, qkv_oth, heads, pad)
    branch_one = nt(o_own, w_proj) + part_oth + proj_bias
    middle = latent_tokens + gate_one * branch_one
    normed_two, rscale_two = normalize(middle)

    m_own = low(normed_two * (1.0 + scale_two) + shift_two)
    m_oth = swap(m_own)
    hidden_bias = fc1_bias.reshape(1, -1)
    act_oth, gp_oth, h_send, b_send = feed(m_oth, g_oth, w_second, hidden_bias, bf16)
    early = rows // 2
    h_came = swap(h_send[:early])
    act_own, gp_own, h_own, b_own = feed(
        after(m_own, h_send), g_own, w_second, hidden_bias, f32
    )
    (
        mid_grad, z_own, z_oth, go_own, go_oth, turned, fc1_sums,
        fc2_own, fc2_code, fc1_mine, fc1_code, fc_bounds,
    ) = middle_part(
        h_send[early:], h_came, scale_two, gate_one, tops, g_own, g_oth, m_own, m_oth, act_own, act_oth,
        gp_own, gp_oth, h_own, middle, out_grad, branch_one, w_proj, block,
    )
    d_own, d_oth, b_oth, grad_fc2, fc1_own, fc1_code = attend_back(
        qkv_own, qkv_oth, go_own, go_oth, lse_own, lse_oth, fc_bounds, fc2_own, b_send,
        fc2_code, fc1_code, fc1_mine, heads, pad,
    )
    branch_two = b_own + b_oth.astype(f32) + second_layer_bias
    layer_out = middle + gate_two * branch_two

    sums = functools.partial(jnp.sum, axis=0)
    empty = jnp.zeros((2, width_full), f32)
    mods_sums = jnp.stack([turned[0], turned[1], turned[2], sums(out_grad * branch_two)])
    mods_sums = jnp.concatenate([empty, mods_sums]).reshape(6, 2, width)
    spare = jnp.zeros((2, width), f32)
    mine = jnp.concatenate([pick(mods_sums, side, 1), spare])
    other = jnp.concatenate([pick(mods_sums, 1 - side, 1), spare])
    shared = jnp.stack([turned[3], g_sums[0]]).reshape(-1, width)
    extra = jnp.concatenate([fc1_sums[0].reshape(-1, width), shared])
    ada = jnp.transpose(ada, (1, 0, 2))
    (
        tokens_grad, grad_qkv, grad_proj, grad_ada, totals, extra, cond_row, grad_fc1,
    ) = close(
        a_own, a_oth, d_own, d_oth, mine, other, extra, cond_mine, scale_one, tops, turned,
        fc_bounds, fc1_own, fc1_code, w_qkv, n_oth, latent_tokens, mid_grad, z_own, z_oth,
        o_own, o_oth, ada, shared.shape[0],
    )
    grad_qkv = jnp.transpose(grad_qkv, (1, 0, 2))
    grad_ada = jnp.transpose(grad_ada, (1, 0, 2))
    grad_proj, grad_fc2 = grad_proj.T, grad_fc2.T
    conditioning_grad = silu_pull(cond_row.reshape(1, width_full))[0]
    fc1_rows = hidden // width
    qkv_bias_grad = totals[6:8]
    grad_ada_bias = totals[:6]
    fc1_bias_grad = extra[:fc1_rows].reshape(hidden)
    proj_bias_grad, fc2_bias_grad = extra[fc1_rows:].reshape(2, width_full)
    return (
        layer_out,
        tokens_grad,
        conditioning_grad,
        grad_qkv,
        qkv_bias_grad,
        grad_proj,
        proj_bias_grad,
        grad_fc1,
        fc1_bias_grad,
        grad_fc2,
        fc2_bias_grad,
        grad_ada,
        grad_ada_bias,
    )


def solution(mesh):
    in_specs = (
        P(("dp", "tensor"), None),
        P("dp", None),
        P(("dp", "tensor"), None),
        P("dp", None, "tensor"),
        P(None, "tensor"),
        P("tensor", "dp"),
        P(),
        P("dp", "tensor"),
        P("tensor"),
        P("tensor", "dp"),
        P(),
        P("dp", None, "tensor"),
        P(None, "tensor"),
    )
    out_specs = (
        P(("dp", "tensor"), None),
        P(("dp", "tensor"), None),
        P("dp", None),
        P("dp", None, "tensor"),
        P(None, "tensor"),
        P("tensor", "dp"),
        P(),
        P("dp", "tensor"),
        P("tensor"),
        P("tensor", "dp"),
        P(),
        P("dp", None, "tensor"),
        P(None, "tensor"),
    )
    body = fast_body if fits(mesh) else general_body
    return jax.shard_map(body, mesh=mesh, in_specs=in_specs, out_specs=out_specs, check_vma=False)
```
